128 devices in a mesh: section: 2 (over x_lo), dp: 16 (over y, x_hi, core), tensor: 4 (over z).
Axes of the slice: x: 4 (x_hi: 2, x_lo: 2; x = x_hi * 2 + x_lo), y: 4, z: 4, core: 2. Of those that a mesh axis runs over, the one named last changes fastest.
Arguments:
- inputs: bfloat16 [2, 2048, 1024], P(None, ('dp', 'tensor')), may hold values from -6 to 6
- doc_ids: int32 [2, 2048], P(None, 'dp'), may hold values from -1 to 7, as said below
- cotangent: bfloat16 [2, 2048, 1024], P(None, ('dp', 'tensor')), may hold values from -6 to 6
- w_qkv: bfloat16 [2, 1024, 3, 1024], P('section', None, None, 'tensor'), may hold values from -0.1875 to 0.1875
- b_qv: float32 [2, 2, 1024], P('section', None, 'tensor'), may hold values from -3 to 3
- w_out: bfloat16 [2, 1024, 1024], P('section', 'tensor'), may hold values from -0.75 to 0.75
- b_out: float32 [2, 1024], P('section'), may hold values from -3 to 3
- gain1: float32 [2, 1024], P('section'), may hold values from 0.5 to 1.5
- shift1: float32 [2, 1024], P('section'), may hold values from -1.75 to 1.75
- w_up: bfloat16 [2, 1024, 4096], P('section', None, 'tensor'), may hold values from -0.1875 to 0.1875
- b_up: float32 [2, 4096], P('section', 'tensor'), may hold values from -3 to 3
- w_down: bfloat16 [2, 4096, 1024], P('section', 'tensor'), may hold values from -0.09375 to 0.09375
- b_down: float32 [2, 1024], P('section'), may hold values from -3 to 3
- gain2: float32 [2, 1024], P('section'), may hold values from 0.5 to 1.5
- shift2: float32 [2, 1024], P('section'), may hold values from -1.75 to 1.75
Outputs:
- outputs: bfloat16 [2, 2, 2048, 1024], P('section', None, ('dp', 'tensor'))
- input_grads: float32 [2, 2, 2048, 1024], P('section', None, ('dp', 'tensor'))
- grad_w_qkv: float32 [2, 1024, 3, 1024], P('section', None, None, 'tensor')
- grad_b_qv: float32 [2, 2, 1024], P('section', None, 'tensor')
- grad_w_out: float32 [2, 1024, 1024], P('section', 'tensor')
- grad_b_out: float32 [2, 1024], P('section')
- grad_gain1: float32 [2, 1024], P('section')
- grad_shift1: float32 [2, 1024], P('section')
- grad_w_up: float32 [2, 1024, 4096], P('section', None, 'tensor')
- grad_b_up: float32 [2, 4096], P('section', 'tensor')
- grad_w_down: float32 [2, 4096, 1024], P('section', 'tensor')
- grad_b_down: float32 [2, 1024], P('section')
- grad_gain2: float32 [2, 1024], P('section')
- grad_shift2: float32 [2, 1024], P('section')
The draws below stay inside these ranges and needn't reach their ends.
Inputs may be any that keep to these rules, and one draw needn't show every extreme that they name: `doc_ids`: within each slot of 128 rows the valid rows come first and their ids rise from 0 in steps of 0 or 1, never above 7; padding rows at the end are -1; at least half of a slot's rows are valid; one slot in every draw is a single sequence of all 128 rows, another holds sequences numbered up to 7, and every slot but the first of these has padding.
All inputs are finite; a program needn't handle non-finite values.
Results may differ from the reference program's by a relative error of at most 0.025.
Values may be sent and summed in bfloat16 or wider, within the bound.
A program may use at most 128 MiB of HBM per device.

```python
import jax
import jax.numpy as jnp
from jax import lax

D = 1024
HEADS = 16
HEAD_DIM = 64
FF = 4096
ROWS = 128
MB = 2
LAYERS = 2
GROUPS = 16
ROWS_ALL = 2048


def draw_doc_ids(key, part):
    key = jax.random.fold_in(key, 7)
    key_fill, key_cut, key_full = jax.random.split(key, 3)
    slot_count = MB * GROUPS
    valid_len = jax.random.randint(key_fill, (slot_count, 1), ROWS // 2, ROWS)
    cut_draw = jax.random.randint(key_cut, (slot_count, ROWS), 0, 96)
    chosen = jax.random.randint(key_full, (), 0, slot_count)
    dense_pick = (chosen + 1) % slot_count
    slot_index = jnp.arange(slot_count)[:, None]
    positions = jnp.arange(ROWS)[None, :]
    full_slot = slot_index == chosen
    dense_slot = slot_index == dense_pick
    random_cut = (cut_draw == 0) & (positions > 0) & jnp.logical_not(full_slot)
    dense_cut = dense_slot & (positions > 0) & (positions % (ROWS // 16) == 0)
    boundary = random_cut | dense_cut
    doc_number = jnp.minimum(jnp.cumsum(boundary.astype(jnp.int32), axis=1), 7)
    valid_limit = jnp.where(full_slot, ROWS, valid_len)
    doc_all = jnp.where(positions < valid_limit, doc_number, -1)
    return doc_all.reshape(MB, GROUPS * ROWS).astype(jnp.int32)


def block_levels(stream_key, shape, cuts, least, top_value):
    level, own = 1.0, jax.random.fold_in(stream_key, 6)
    for position, shards_of in cuts:
        draws = jnp.exp(jax.random.uniform(jax.random.fold_in(own, position), (shards_of,), jnp.float32, least / len(cuts), top_value / len(cuts)))
        level = level * jnp.repeat(draws, shape[position] // shards_of).reshape([-1 if axis == position else 1 for axis in range(len(shape))])
    return level


def noise(key, extent, scale, bound, pieces=(), kind=jnp.bfloat16):
    values = scale * jax.random.normal(key, extent, jnp.float32)
    if pieces:
        values = values * block_levels(key, extent, pieces, -0.22, 0.18)
    return jnp.clip(values, -bound, bound).astype(kind)


def setup_inputs(seed: int = 0) -> dict:
    key_list = jax.random.split(jax.random.key(seed), 16)
    return {
        "inputs": noise(key_list[0], (MB, ROWS_ALL, D), 1.0, 6.0, ((1, 64),)),
        "doc_ids": draw_doc_ids(jax.random.fold_in(key_list[15], 71), 0),
        "cotangent": noise(key_list[2], (MB, ROWS_ALL, D), 1.0, 6.0, ((1, 64),)),
        "w_qkv": noise(key_list[3], (LAYERS, D, 3, D), D ** -0.5, 0.1875, ((0, 2), (3, 4))),
        "b_qv": noise(key_list[4], (LAYERS, 2, D), 0.5, 3.0, ((0, 2), (2, 4)), jnp.float32),
        "w_out": noise(key_list[5], (LAYERS, D, D), (D // 16) ** -0.5, 0.75, ((0, 2), (1, 4))),
        "b_out": noise(key_list[6], (LAYERS, D), 0.5, 3.0, ((0, 2),), jnp.float32),
        "gain1": jnp.clip(1.0 + 0.1 * jax.random.normal(key_list[7], (LAYERS, D), jnp.float32), 0.5, 1.5),
        "shift1": noise(key_list[8], (LAYERS, D), 0.3, 1.75, ((0, 2),), jnp.float32),
        "w_up": noise(key_list[9], (LAYERS, D, FF), D ** -0.5, 0.1875, ((0, 2), (2, 4))),
        "b_up": noise(key_list[10], (LAYERS, FF), 0.5, 3.0, ((0, 2), (1, 4)), jnp.float32),
        "w_down": noise(key_list[11], (LAYERS, FF, D), FF ** -0.5, 0.09375, ((0, 2), (1, 4))),
        "b_down": noise(key_list[12], (LAYERS, D), 0.5, 3.0, ((0, 2),), jnp.float32),
        "gain2": jnp.clip(1.0 + 0.1 * jax.random.normal(key_list[13], (LAYERS, D), jnp.float32), 0.5, 1.5),
        "shift2": noise(key_list[14], (LAYERS, D), 0.3, 1.75, ((0, 2),), jnp.float32),
    }


@jax.custom_vjp
def low(v):
    return lax.optimization_barrier(v.astype(jnp.bfloat16)).astype(jnp.float32)

@jax.custom_vjp
def low_back(v):
    return v

def low_keep(v):
    return (low(v), None)

def low_pass(kept, grad):
    return (grad,)

def back_keep(v):
    return (v, None)

def back_low(kept, grad):
    return (low(grad),)
low.defvjp(low_keep, low_pass)
low_back.defvjp(back_keep, back_low)

def matmul(left, right):
    return jnp.dot(left, right, precision=lax.Precision.HIGHEST, preferred_element_type=jnp.float32)

def normalize(hidden, gain, shift):
    mean_row = lax.optimization_barrier(jnp.mean(hidden, axis=-1, keepdims=True))
    centred = hidden - mean_row
    variance = lax.optimization_barrier(jnp.mean(centred * centred, axis=-1, keepdims=True))
    return centred * lax.rsqrt(variance + 1e-05) * gain + shift

def encoder_layer(hidden, slot_docs, w_qkv, b_qv, w_out, b_out, gain1, shift1, w_up, b_up, w_down, b_down, gain2, shift2):
    rounded = low(hidden)
    joined = matmul(rounded, w_qkv.reshape(D, 3 * D))
    queries = low(low_back(joined[:, :D] + b_qv[0])).reshape(ROWS, HEADS, HEAD_DIM)
    key_heads = low(low_back(joined[:, D:2 * D])).reshape(ROWS, HEADS, HEAD_DIM)
    values = low(low_back(joined[:, 2 * D:] + b_qv[1])).reshape(ROWS, HEADS, HEAD_DIM)
    scale_factor = HEAD_DIM ** (-0.5)
    scores = low_back(jnp.einsum('qhd,khd->hqk', queries, key_heads, precision=lax.Precision.HIGHEST) * scale_factor)
    same_doc = (slot_docs[:, None] == slot_docs[None, :]) & (slot_docs[None, :] >= 0)
    allowed = same_doc | jnp.eye(ROWS, dtype=bool)
    scores = jnp.where(allowed[None], scores, -1e+30)
    row_max = lax.optimization_barrier(jnp.max(scores, axis=-1, keepdims=True))
    exp_scores = jnp.exp(scores - row_max)
    attn_probs = low(exp_scores / lax.optimization_barrier(jnp.sum(exp_scores, axis=-1, keepdims=True)))
    context = jnp.einsum('hqk,khd->qhd', attn_probs, values, precision=lax.Precision.HIGHEST).reshape(ROWS, D)
    context = low(low_back(context))
    first_out = normalize(hidden + low_back(matmul(context, w_out)) + b_out, gain1, shift1)
    upper_pre = low_back(matmul(low(first_out), w_up) + b_up)
    activation = low(jax.nn.gelu(upper_pre, approximate=False))
    return normalize(first_out + low_back(matmul(activation, w_down)) + b_down, gain2, shift2)

def reference(inputs, doc_ids, cotangent, w_qkv, b_qv, w_out, b_out, gain1, shift1, w_up, b_up, w_down, b_down, gain2, shift2):
    stacked = (w_qkv, b_qv, w_out, b_out, gain1, shift1, w_up, b_up, w_down, b_down, gain2, shift2)
    slot_count = MB * GROUPS
    first_in = inputs.astype(jnp.float32).reshape(slot_count, ROWS, D)
    slot_docs = doc_ids.reshape(slot_count, ROWS)
    slot_cot = cotangent.astype(jnp.float32).reshape(slot_count, ROWS, D)
    lower = tuple((weight[0].astype(jnp.float32) for weight in stacked))
    higher = tuple((weight[1].astype(jnp.float32) for weight in stacked))

    def forward_slot(state_none, slot_item):
        return (state_none, low(encoder_layer(slot_item[0], slot_item[1], *lower)))
    state_end, second_in = lax.scan(forward_slot, jnp.float32(0.0), (first_in, slot_docs))

    def backward_pass(params, layer_in, layer_cot):

        def slot_step(totals, slot_item):

            def apply_layer(hidden, *weights):
                return encoder_layer(hidden, slot_item[1], *weights)
            result, pullback = jax.vjp(apply_layer, slot_item[0], *params)
            slot_grads = pullback(slot_item[2])
            return (jax.tree.map(jnp.add, totals, tuple(slot_grads[1:])), (result, slot_grads[0]))
        zero_totals = tuple((jnp.zeros_like(weight) for weight in params))
        return lax.scan(slot_step, zero_totals, (layer_in, slot_docs, layer_cot))
    high_grads, (second_out, second_grad) = backward_pass(higher, second_in, slot_cot)
    low_grads, (first_out, first_grad) = backward_pass(lower, first_in, low(second_grad))
    shape_out = (MB, GROUPS * ROWS, D)
    outputs = jnp.stack([second_in.reshape(shape_out), second_out.reshape(shape_out)]).astype(jnp.bfloat16)
    input_grads = jnp.stack([first_grad.reshape(shape_out), second_grad.reshape(shape_out)])
    merged = tuple((jnp.stack([low_part, high_part]) for low_part, high_part in zip(low_grads, high_grads)))
    return (outputs, input_grads, merged[0], merged[1], merged[2], merged[3], merged[4], merged[5], merged[6], merged[7], merged[8], merged[9], merged[10], merged[11])
```

```python
import functools
import math

import jax
import jax.numpy as jnp
from jax import lax
from jax.experimental import pallas as pl
from jax.experimental.pallas import tpu as pltpu
from jax.sharding import PartitionSpec as P

HEAD_DIM = 64
MESH = pl.DeviceIdType.MESH
F32 = jnp.float32
BF16 = jnp.bfloat16
STEP = 256
VMEM_BYTES = 60 * 1024 * 1024


def dot(left, right):
    return lax.dot_general(left, right, (((1,), (0,)), ((), ())), preferred_element_type=F32)


def dot_last(left, right):
    return lax.dot_general(left, right, (((1,), (1,)), ((), ())), preferred_element_type=F32)


def dot_rows(left, right):
    return lax.dot_general(left, right, (((0,), (0,)), ((), ())), preferred_element_type=F32)


def norm(hidden, gain, shift):
    centred = hidden - jnp.mean(hidden, axis=-1, keepdims=True)
    inv_std = lax.rsqrt(jnp.mean(centred * centred, axis=-1, keepdims=True) + 1e-05)
    normed = centred * inv_std
    return normed * gain + shift, normed, inv_std


def norm_back(grad_out, normed, inv_std, gain):
    scaled = grad_out * gain
    return inv_std * (
        scaled
        - jnp.mean(scaled, axis=-1, keepdims=True)
        - normed * jnp.mean(scaled * normed, axis=-1, keepdims=True)
    )


def column_sum(block):
    return jnp.sum(block, axis=0, keepdims=True)


def layer_kernel(
    tensor_size,
    x_ref, doc_ref, cot_ref,
    wqkv_ref, bqv_ref, wout_ref, bout_ref, gain1_ref, shift1_ref,
    wup_ref, bup_ref, wdown_ref, bdown_ref, gain2_ref, shift2_ref,
    out_ref, dx_ref, gqkv_ref, gout_ref, gup_ref, gdown_ref, small_ref,
    gath, rs_send, rs_recv, rs_own,
    qkv, probs, ctx, entry, y1, n1, r1, slope, act, n2, r2, dh2, dh, du, dqkv,
    sent_up, back_in, sent_back, small_acc, small_all,
    ag_ssem, ag_rsem, rs_ssem, rs_rsem, up_ssem, up_rsem, back_ssem, back_rsem,
    small_ssem, small_rsem,
):
    batches, rows, width = x_ref.shape
    slot = rows * tensor_size
    local = wout_ref.shape[0]
    units = wup_ref.shape[1]
    pairs = local // (2 * HEAD_DIM)
    sec = lax.axis_index("section")
    me = lax.axis_index("tensor")
    other = 1 - sec
    scale = HEAD_DIM ** (-0.5)

    barrier = pltpu.get_barrier_semaphore()
    for k in range(1, tensor_size):
        pl.semaphore_signal(
            barrier, inc=1, device_id={"tensor": lax.rem(me + k, tensor_size)}, device_id_type=MESH
        )
    pl.semaphore_signal(barrier, inc=1, device_id={"section": other}, device_id_type=MESH)
    pl.semaphore_wait(barrier, tensor_size)

    def band(index):
        return pl.ds(pl.multiple_of(index * rows, rows), rows)

    mine = band(me)

    def gather_copy(e, m, k):
        return pltpu.make_async_remote_copy(
            src_ref=gath.at[e, m, mine],
            dst_ref=gath.at[e, m, mine],
            send_sem=ag_ssem.at[e, m, k - 1],
            recv_sem=ag_rsem.at[e, m, k - 1],
            device_id={"tensor": lax.rem(me + k, tensor_size)},
            device_id_type=MESH,
        )

    def gather_start(e, m):
        for k in range(1, tensor_size):
            gather_copy(e, m, k).start()

    def gather_wait(e, m):
        for k in range(1, tensor_size):
            source = band(lax.rem(me + tensor_size - k, tensor_size))
            pltpu.make_async_remote_copy(
                src_ref=gath.at[e, m, source],
                dst_ref=gath.at[e, m, source],
                send_sem=ag_ssem.at[e, m, k - 1],
                recv_sem=ag_rsem.at[e, m, k - 1],
                device_id={"tensor": lax.rem(me + k, tensor_size)},
                device_id_type=MESH,
            ).wait_recv()

    def scatter_copy(e, m, k):
        target = lax.rem(me + k, tensor_size)
        return pltpu.make_async_remote_copy(
            src_ref=rs_send.at[e, m, band(target)],
            dst_ref=rs_recv.at[e, m, k - 1],
            send_sem=rs_ssem.at[e, m, k - 1],
            recv_sem=rs_rsem.at[e, m, k - 1],
            device_id={"tensor": target},
            device_id_type=MESH,
        )

    def scatter_start(e, m):
        for k in range(1, tensor_size):
            scatter_copy(e, m, k).start()

    def scatter_wait(e, m):
        total = rs_own[m, mine, :]
        for k in range(1, tensor_size):
            scatter_copy(e, m, k).wait_recv()
        for k in range(1, tensor_size):
            total = total + rs_recv[e, m, k - 1].astype(F32)
        return total

    def put_part(e, m, columns, part):
        rs_own[m, :, columns] = part
        rs_send[e, m, :, columns] = part.astype(BF16)

    def up_copy(m):
        return pltpu.make_async_remote_copy(
            src_ref=sent_up.at[m],
            dst_ref=gath.at[0, m, mine],
            send_sem=up_ssem.at[m],
            recv_sem=up_rsem.at[m],
            device_id={"section": other},
            device_id_type=MESH,
        )

    def back_copy(m):
        return pltpu.make_async_remote_copy(
            src_ref=sent_back.at[m],
            dst_ref=back_in.at[m],
            send_sem=back_ssem.at[m],
            recv_sem=back_rsem.at[m],
            device_id={"section": other},
            device_id_type=MESH,
        )

    def each_batch(body):
        def step(m, carry):
            body(m)
            return carry

        lax.fori_loop(0, batches, step, 0)

    def chunks(total):
        return [pl.ds(c, min(STEP, total - c)) for c in range(0, total, STEP)]

    def head_mask():
        return lax.broadcasted_iota(jnp.int32, (slot, 2 * HEAD_DIM), 1) < HEAD_DIM

    def pick(first, block):
        low_half = head_mask()
        keep = low_half if first else jnp.logical_not(low_half)
        return jnp.where(keep, block, jnp.zeros_like(block))

    small_acc[...] = jnp.zeros_like(small_acc)

    @pl.when(sec == 0)
    def _():
        for m in range(batches):
            gath[0, m, mine, :] = x_ref[m]

    def send_entry(m):
        @pl.when(sec == 1)
        def _():
            up_copy(m).wait_recv()

        gather_start(0, m)

    each_batch(send_entry)

    def attention(m):
        entry[m] = gath[0, m, mine, :].astype(F32)
        gather_wait(0, m)
        for cols in chunks(3 * local):
            part = dot(gath[0, m], wqkv_ref[:, cols])
            if cols.start < local:
                part = part + bqv_ref[0:1, cols]
            elif cols.start >= 2 * local:
                part = part + bqv_ref[1:2, pl.ds(cols.start - 2 * local, cols.size)]
            qkv[m, :, cols] = part.astype(BF16)
        across = jnp.broadcast_to(doc_ref[pl.ds(m, 1), :].astype(F32), (slot, slot))
        down = jnp.transpose(across)
        row_id = lax.broadcasted_iota(jnp.int32, (slot, slot), 0)
        col_id = lax.broadcasted_iota(jnp.int32, (slot, slot), 1)
        allowed = ((across == down) & (across >= 0)) | (row_id == col_id)
        low_half = head_mask()
        for pair in range(pairs):
            at = pair * 2 * HEAD_DIM
            queries = qkv[m, :, pl.ds(at, 2 * HEAD_DIM)]
            key_heads = qkv[m, :, pl.ds(local + at, 2 * HEAD_DIM)]
            values = qkv[m, :, pl.ds(2 * local + at, 2 * HEAD_DIM)]
            halves = []
            for half in range(2):
                raw = dot_last(pick(half == 0, queries), key_heads) * scale
                scores = jnp.where(allowed, raw, -1e30)
                peak = jnp.max(scores, axis=-1, keepdims=True)
                exps = jnp.exp(scores - peak)
                soft = exps / jnp.sum(exps, axis=-1, keepdims=True)
                probs[m, pair * 2 + half] = soft
                halves.append(dot(soft.astype(BF16), values))
            ctx[m, :, pl.ds(at, 2 * HEAD_DIM)] = jnp.where(low_half, halves[0], halves[1]).astype(BF16)
        for cols in chunks(width):
            put_part(0, m, cols, dot(ctx[m], wout_ref[:, cols]))
        scatter_start(0, m)

    each_batch(attention)

    def first_norm(m):
        hidden = entry[m] + scatter_wait(0, m) + bout_ref[...]
        out, normed, inv_std = norm(hidden, gain1_ref[...], shift1_ref[...])
        y1[m], n1[m], r1[m] = out, normed, inv_std
        gath[1, m, mine, :] = out.astype(BF16)
        gather_start(1, m)

    each_batch(first_norm)

    def feed_forward(m):
        gather_wait(1, m)
        for cols in chunks(units):
            pre = dot(gath[1, m], wup_ref[:, cols]) + bup_ref[:, cols]
            cdf = 0.5 * (1.0 + lax.erf(pre * (1.0 / math.sqrt(2.0))))
            slope[m, :, cols] = cdf + pre * jnp.exp(-0.5 * pre * pre) * (
                1.0 / math.sqrt(2.0 * math.pi)
            )
            act[m, :, cols] = (pre * cdf).astype(BF16)
        for cols in chunks(width):
            put_part(1, m, cols, dot(act[m], wdown_ref[:, cols]))
        scatter_start(1, m)

    each_batch(feed_forward)

    def second_norm(m):
        hidden = y1[m] + scatter_wait(1, m) + bdown_ref[...]
        out, normed, inv_std = norm(hidden, gain2_ref[...], shift2_ref[...])
        n2[m], r2[m] = normed, inv_std
        rounded = out.astype(BF16)
        out_ref[m] = rounded

        @pl.when(sec == 0)
        def _():
            sent_up[m] = rounded
            up_copy(m).start()

    each_batch(second_norm)

    def back_entry(m):
        @pl.when(sec == 1)
        def _():
            back_in[m] = cot_ref[m]

        @pl.when(sec == 0)
        def _():
            back_copy(m).wait_recv()

        grad_out = back_in[m].astype(F32)
        grad = norm_back(grad_out, n2[m], r2[m], gain2_ref[...])
        small_acc[0:1, :] += column_sum(grad)
        small_acc[1:2, :] += column_sum(grad_out * n2[m])
        small_acc[2:3, :] += column_sum(grad_out)
        dh2[m] = grad
        gath[2, m, mine, :] = grad.astype(BF16)
        gather_start(2, m)

    each_batch(back_entry)

    def feed_back(m):
        gather_wait(2, m)
        for cols in chunks(units):
            grad = (dot_last(gath[2, m], wdown_ref[cols, :]) * slope[m, :, cols]).astype(BF16)
            du[m, :, cols] = grad
            small_acc[6:7, cols] += column_sum(grad.astype(F32))
        for cols in chunks(width):
            put_part(2, m, cols, dot_last(du[m], wup_ref[cols, :]))
        scatter_start(2, m)

    each_batch(feed_back)

    def weight_grad(left, right, target):
        total = batches * slot
        for rows_at in chunks(left.shape[-1]):
            lhs = left[:, :, rows_at].reshape(total, rows_at.size)
            target[rows_at, :] = dot_rows(lhs, right[...].reshape(total, right.shape[-1])).astype(BF16)

    weight_grad(act, gath.at[2], gdown_ref)
    weight_grad(gath.at[1], du, gup_ref)

    def first_back(m):
        grad_out = dh2[m] + scatter_wait(2, m)
        grad = norm_back(grad_out, n1[m], r1[m], gain1_ref[...])
        small_acc[3:4, :] += column_sum(grad)
        small_acc[4:5, :] += column_sum(grad_out * n1[m])
        small_acc[5:6, :] += column_sum(grad_out)
        dh[m] = grad
        gath[3, m, mine, :] = grad.astype(BF16)
        gather_start(3, m)

    each_batch(first_back)

    def attention_back(m):
        gather_wait(3, m)
        low_half = head_mask()
        for pair in range(pairs):
            at = pair * 2 * HEAD_DIM
            dctx = dot_last(gath[3, m], wout_ref[pl.ds(at, 2 * HEAD_DIM), :]).astype(BF16)
            queries = qkv[m, :, pl.ds(at, 2 * HEAD_DIM)]
            key_heads = qkv[m, :, pl.ds(local + at, 2 * HEAD_DIM)]
            values = qkv[m, :, pl.ds(2 * local + at, 2 * HEAD_DIM)]
            dq, dk, dv = [], [], []
            for half in range(2):
                soft = probs[m, pair * 2 + half]
                dv.append(dot_rows(soft.astype(BF16), dctx))
                dprob = dot_last(pick(half == 0, dctx), values)
                dscore = soft * (dprob - jnp.sum(soft * dprob, axis=-1, keepdims=True))
                dscore = dscore.astype(BF16)
                dq.append(dot(dscore, key_heads) * scale)
                dk.append(dot_rows(dscore, queries) * scale)
            for place, (first, second) in enumerate((dq, dk, dv)):
                cols = pl.ds(place * local + at, 2 * HEAD_DIM)
                grad = jnp.where(low_half, first, second).astype(BF16)
                dqkv[m, :, cols] = grad
                if place != 1:
                    to = at if place == 0 else local + at
                    small_acc[7:8, pl.ds(to, 2 * HEAD_DIM)] += column_sum(grad.astype(F32))
        for cols in chunks(width):
            put_part(3, m, cols, dot_last(dqkv[m], wqkv_ref[cols, :]))
        scatter_start(3, m)

    each_batch(attention_back)

    def small_copy(k, source):
        return pltpu.make_async_remote_copy(
            src_ref=small_all.at[source],
            dst_ref=small_all.at[source],
            send_sem=small_ssem.at[k - 1],
            recv_sem=small_rsem.at[k - 1],
            device_id={"tensor": lax.rem(me + k, tensor_size)},
            device_id_type=MESH,
        )

    small_all[me] = small_acc[...]
    for k in range(1, tensor_size):
        small_copy(k, me).start()

    weight_grad(ctx, gath.at[3], gout_ref)

    def last_back(m):
        grad = dh[m] + scatter_wait(3, m)
        dx_ref[m] = grad

        @pl.when(sec == 1)
        def _():
            sent_back[m] = grad.astype(BF16)
            back_copy(m).start()

    each_batch(last_back)
    weight_grad(gath.at[0], dqkv, gqkv_ref)

    for k in range(1, tensor_size):
        small_copy(k, lax.rem(me + tensor_size - k, tensor_size)).wait_recv()
    total = small_all[0]
    for index in range(1, tensor_size):
        total = total + small_all[index]
    small_row = lax.broadcasted_iota(jnp.int32, total.shape, 0)
    small_ref[...] = jnp.where(small_row < 6, total, small_acc[...])

    for k in range(1, tensor_size):
        small_copy(k, me).wait_send()

    def drain(m):
        for e in range(4):
            for k in range(1, tensor_size):
                gather_copy(e, m, k).wait_send()
                scatter_copy(e, m, k).wait_send()

        @pl.when(sec == 0)
        def _():
            up_copy(m).wait_send()

        @pl.when(sec == 1)
        def _():
            back_copy(m).wait_send()

    each_batch(drain)


def run_layer(x, docs, cot, weights, tensor_size):
    batches, rows, width = x.shape
    slot = rows * tensor_size
    wqkv, bqv, wout, bout, gain1, shift1, wup, bup, wdown, bdown, gain2, shift2 = weights
    local = wout.shape[0]
    units = wup.shape[1]
    heads = local // HEAD_DIM
    vmem = pl.BlockSpec(memory_space=pltpu.VMEM)
    others = tensor_size - 1
    dma = pltpu.SemaphoreType.DMA
    operands = (x, docs, cot) + weights
    small_shape = (8, width)
    shard = (batches, rows, width)
    shapes = (
        jax.ShapeDtypeStruct(shard, BF16),
        jax.ShapeDtypeStruct(shard, F32),
        jax.ShapeDtypeStruct(wqkv.shape, BF16),
        jax.ShapeDtypeStruct(wout.shape, BF16),
        jax.ShapeDtypeStruct(wup.shape, BF16),
        jax.ShapeDtypeStruct(wdown.shape, BF16),
        jax.ShapeDtypeStruct(small_shape, F32),
    )
    scratch = [
        pltpu.VMEM((4, batches, slot, width), BF16),
        pltpu.VMEM((4, batches, slot, width), BF16),
        pltpu.VMEM((4, batches, others, rows, width), BF16),
        pltpu.VMEM((batches, slot, width), F32),
        pltpu.VMEM((batches, slot, 3 * local), BF16),
        pltpu.VMEM((batches, heads, slot, slot), F32),
        pltpu.VMEM((batches, slot, local), BF16),
        pltpu.VMEM(shard, F32),
        pltpu.VMEM(shard, F32),
        pltpu.VMEM(shard, F32),
        pltpu.VMEM((batches, rows, 1), F32),
        pltpu.VMEM((batches, slot, units), F32),
        pltpu.VMEM((batches, slot, units), BF16),
        pltpu.VMEM(shard, F32),
        pltpu.VMEM((batches, rows, 1), F32),
        pltpu.VMEM(shard, F32),
        pltpu.VMEM(shard, F32),
        pltpu.VMEM((batches, slot, units), BF16),
        pltpu.VMEM((batches, slot, 3 * local), BF16),
        pltpu.VMEM(shard, BF16),
        pltpu.VMEM(shard, BF16),
        pltpu.VMEM(shard, BF16),
        pltpu.VMEM(small_shape, F32),
        pltpu.VMEM((tensor_size,) + small_shape, F32),
        dma((4, batches, others)),
        dma((4, batches, others)),
        dma((4, batches, others)),
        dma((4, batches, others)),
        dma((batches,)),
        dma((batches,)),
        dma((batches,)),
        dma((batches,)),
        dma((others,)),
        dma((others,)),
    ]
    return pl.pallas_call(
        functools.partial(layer_kernel, tensor_size),
        out_shape=shapes,
        in_specs=[vmem] * len(operands),
        out_specs=[vmem] * len(shapes),
        scratch_shapes=scratch,
        compiler_params=pltpu.CompilerParams(
            collective_id=0, has_side_effects=True, vmem_limit_bytes=VMEM_BYTES
        ),
        name="layer",
    )(*operands)


AXES = {"core": (1, 2), "x": (2, 2), "y": (4, 4)}
ORDERS = (("core", "x", "y"), ("core", "y", "x"), ("core", "y", "x"), ("core", "x", "y"))


def sum_kernel(count, *refs):
    grads, refs = refs[:count], refs[count:]
    small_in, refs = refs[0], refs[1:]
    outs, refs = refs[:count], refs[count:]
    small_out, refs = refs[0], refs[1:]
    recvs = [refs[c * 3 : c * 3 + 3] for c in range(count)]
    refs = refs[3 * count :]
    sums = [refs[c * 2 : c * 2 + 2] for c in range(count)]
    refs = refs[2 * count :]
    smalls, refs = refs[:3], refs[3:]
    rs_ssem, rs_rsem, ag_ssem, ag_rsem, sm_ssem, sm_rsem = refs
    dp = lax.axis_index("dp")

    def place(axis):
        stride, size = AXES[axis]
        return lax.rem(dp // stride, size)

    def peer(axis, k):
        stride, size = AXES[axis]
        index = lax.rem(place(axis) + k, size)
        return index, {"dp": dp + (index - place(axis)) * stride}

    barrier = pltpu.get_barrier_semaphore()
    greeted = 0
    for axis, (_, size) in AXES.items():
        for k in range(1, size):
            pl.semaphore_signal(barrier, inc=1, device_id=peer(axis, k)[1], device_id_type=MESH)
            greeted += 1
    pl.semaphore_wait(barrier, greeted)

    waits = []

    def small_copy(step, axis, k, source):
        return pltpu.make_async_remote_copy(
            src_ref=smalls[step].at[source],
            dst_ref=smalls[step].at[source],
            send_sem=sm_ssem.at[step, k - 1],
            recv_sem=sm_rsem.at[step, k - 1],
            device_id=peer(axis, k)[1],
            device_id_type=MESH,
        )

    def small_start(step, axis, value):
        smalls[step][place(axis)] = value
        for k in range(1, AXES[axis][1]):
            copy = small_copy(step, axis, k, place(axis))
            copy.start()
            waits.append(copy)

    def small_finish(step, axis):
        size = AXES[axis][1]
        for k in range(1, size):
            small_copy(step, axis, k, lax.rem(place(axis) + size - k, size)).wait_recv()
        total = smalls[step][0]
        for index in range(1, size):
            total = total + smalls[step][index]
        return total

    def rs_copy(c, step, axis, k):
        source = grads[c] if step == 0 else sums[c][step - 1]
        size = AXES[axis][1]
        block = source.shape[0] // size
        index, device = peer(axis, k)
        return pltpu.make_async_remote_copy(
            src_ref=source.at[pl.ds(pl.multiple_of(index * block, block), block)],
            dst_ref=recvs[c][step].at[k - 1],
            send_sem=rs_ssem.at[c, step, k - 1],
            recv_sem=rs_rsem.at[c, step, k - 1],
            device_id=device,
            device_id_type=MESH,
        )

    def rs_start(c, step):
        axis = ORDERS[c][step]
        for k in range(1, AXES[axis][1]):
            copy = rs_copy(c, step, axis, k)
            copy.start()
            waits.append(copy)

    offsets = [[] for _ in range(count)]

    def rs_finish(c, step):
        axis = ORDERS[c][step]
        size = AXES[axis][1]
        source = grads[c] if step == 0 else sums[c][step - 1]
        block = source.shape[0] // size
        for k in range(1, size):
            rs_copy(c, step, axis, k).wait_recv()
        at = pl.multiple_of(place(axis) * block, block)
        total = source[pl.ds(at, block), :].astype(F32)
        for k in range(1, size):
            total = total + recvs[c][step][k - 1].astype(F32)
        base = offsets[c][-1] if step else 0
        offsets[c].append(base + at)
        if step < 2:
            sums[c][step][...] = total.astype(BF16)
        else:
            outs[c][pl.ds(pl.multiple_of(base + at, block), block), :] = total.astype(BF16)

    def block_of(c, step):
        total = outs[c].shape[0]
        for axis in ORDERS[c][: step + 1]:
            total //= AXES[axis][1]
        return total

    def ag_copy(c, step, k, start):
        axis = ORDERS[c][step]
        block = block_of(c, step)
        region = outs[c].at[pl.ds(pl.multiple_of(start, block), block)]
        return pltpu.make_async_remote_copy(
            src_ref=region,
            dst_ref=region,
            send_sem=ag_ssem.at[c, step, k - 1],
            recv_sem=ag_rsem.at[c, step, k - 1],
            device_id=peer(axis, k)[1],
            device_id_type=MESH,
        )

    def ag_start(c, step):
        for k in range(1, AXES[ORDERS[c][step]][1]):
            copy = ag_copy(c, step, k, offsets[c][step])
            copy.start()
            waits.append(copy)

    def ag_finish(c, step):
        axis = ORDERS[c][step]
        size = AXES[axis][1]
        block = block_of(c, step)
        base = offsets[c][step - 1] if step else 0
        for k in range(1, size):
            source = lax.rem(place(axis) + size - k, size)
            ag_copy(c, step, k, base + source * block).wait_recv()

    small_axes = ("core", "y", "x")
    for c in range(count):
        rs_start(c, 0)
    small_start(0, small_axes[0], small_in[...])
    for step in range(3):
        for c in range(count):
            rs_finish(c, step)
            if step < 2:
                rs_start(c, step + 1)
            else:
                ag_start(c, 2)
        total = small_finish(step, small_axes[step])
        if step < 2:
            small_start(step + 1, small_axes[step + 1], total)
        else:
            small_out[...] = total
    for step in (2, 1, 0):
        for c in range(count):
            ag_finish(c, step)
            if step:
                ag_start(c, step - 1)
    for copy in waits:
        copy.wait_send()


def run_sum(grads, small):
    count = len(grads)
    vmem = pl.BlockSpec(memory_space=pltpu.VMEM)
    dma = pltpu.SemaphoreType.DMA
    recvs, sums = [], []
    for grad, order in zip(grads, ORDERS):
        rows = grad.shape[0]
        for step, axis in enumerate(order):
            size = AXES[axis][1]
            rows //= size
            recvs.append(pltpu.VMEM((size - 1, rows, grad.shape[1]), BF16))
            if step < 2:
                sums.append(pltpu.VMEM((rows, grad.shape[1]), BF16))
    smalls = [pltpu.VMEM((AXES[axis][1],) + small.shape, F32) for axis in ("core", "y", "x")]
    shapes = [jax.ShapeDtypeStruct(grad.shape, BF16) for grad in grads]
    shapes.append(jax.ShapeDtypeStruct(small.shape, F32))
    return pl.pallas_call(
        functools.partial(sum_kernel, count),
        out_shape=shapes,
        in_specs=[vmem] * (count + 1),
        out_specs=[vmem] * (count + 1),
        scratch_shapes=recvs + sums + smalls
        + [dma((count, 3, 3)), dma((count, 3, 3)), dma((count, 3, 3)), dma((count, 3, 3))]
        + [dma((3, 3)), dma((3, 3))],
        compiler_params=pltpu.CompilerParams(
            collective_id=1, has_side_effects=True, vmem_limit_bytes=VMEM_BYTES
        ),
        name="sum",
    )(*grads, small)


def shards(
    inputs, doc_ids, cotangent, w_qkv, b_qv, w_out, b_out, gain1, shift1,
    w_up, b_up, w_down, b_down, gain2, shift2,
):
    tensor_size = lax.axis_size("tensor")
    width = inputs.shape[2]
    local = w_out.shape[1]
    weights = (
        w_qkv[0].reshape(width, 3 * local), b_qv[0], w_out[0], b_out, gain1, shift1,
        w_up[0], b_up, w_down[0], b_down, gain2, shift2,
    )
    outputs, input_grads, *grads, small = run_layer(
        inputs, doc_ids, cotangent, weights, tensor_size
    )
    gqkv, gout, gup, gdown, small = run_sum(grads, small)
    return (
        outputs[None],
        input_grads[None],
        gqkv.astype(F32).reshape(1, width, 3, local),
        small[7:8, : 2 * local].reshape(1, 2, local),
        gout.astype(F32)[None],
        small[3:4],
        small[4:5],
        small[5:6],
        gup.astype(F32)[None],
        small[6:7],
        gdown.astype(F32)[None],
        small[0:1],
        small[1:2],
        small[2:3],
    )


def solution(mesh):
    rows = P(None, ("dp", "tensor"), None)
    banked = P("section", None, ("dp", "tensor"), None)
    vector = P("section", None)
    return jax.shard_map(
        shards,
        mesh=mesh,
        in_specs=(
            rows,
            P(None, "dp"),
            rows,
            P("section", None, None, "tensor"),
            P("section", None, "tensor"),
            P("section", "tensor", None),
            vector,
            vector,
            vector,
            P("section", None, "tensor"),
            P("section", "tensor"),
            P("section", "tensor", None),
            vector,
            vector,
            vector,
        ),
        out_specs=(
            banked,
            banked,
            P("section", None, None, "tensor"),
            P("section", None, "tensor"),
            P("section", "tensor", None),
            vector,
            vector,
            vector,
            P("section", None, "tensor"),
            P("section", "tensor"),
            P("section", "tensor", None),
            vector,
            vector,
            vector,
        ),
        check_vma=False,
    )
```

```python
import functools
import math

import jax
import jax.numpy as jnp
from jax import lax
from jax.experimental import pallas as pl
from jax.experimental.pallas import tpu as pltpu
from jax.sharding import PartitionSpec as P

HEAD_DIM = 64
MESH = pl.DeviceIdType.MESH
F32 = jnp.float32
BF16 = jnp.bfloat16
STEP = 256
SPREAD = ("tensor", "core", "y", "x")
VMEM_BYTES = 60 * 1024 * 1024
AXES = {"core": (1, 2), "x": (2, 2), "y": (4, 4)}
RS_SEM = {"core": 0, "x": 1, "y": 2}
AG_SEM = {"core": 8, "x": 9, "y": 10}
X_FIRST = ("core", "x", "y")
Y_FIRST = ("core", "y", "x")


def sum_plan(width, local, units):
    joined = 3 * width
    return (
        ("down", 0, units, width, X_FIRST),
        ("up", 0, width, units, Y_FIRST),
        ("out", 0, local, width, Y_FIRST),
        ("qkv", 0, joined // 2, local, X_FIRST),
        ("qkv", joined // 2, joined // 2, local, Y_FIRST),
    )


def sum_buffers(rows, columns, order):
    shapes = []
    for axis in order:
        rows //= AXES[axis][1]
        if axis == "y":
            shapes.append((8, rows, columns // 2))
        else:
            shapes.append((rows, columns))
        shapes.append((rows, columns))
    return shapes


def dot(left, right):
    return lax.dot_general(left, right, (((1,), (0,)), ((), ())), preferred_element_type=F32)


def dot_last(left, right):
    return lax.dot_general(left, right, (((1,), (1,)), ((), ())), preferred_element_type=F32)


def dot_rows(left, right):
    return lax.dot_general(left, right, (((0,), (0,)), ((), ())), preferred_element_type=F32)


def norm(hidden, gain, shift):
    centred = hidden - jnp.mean(hidden, axis=-1, keepdims=True)
    inv_std = lax.rsqrt(jnp.mean(centred * centred, axis=-1, keepdims=True) + 1e-05)
    normed = centred * inv_std
    return normed * gain + shift, normed, inv_std


def norm_back(grad_out, normed, inv_std, gain):
    scaled = grad_out * gain
    return inv_std * (
        scaled
        - jnp.mean(scaled, axis=-1, keepdims=True)
        - normed * jnp.mean(scaled * normed, axis=-1, keepdims=True)
    )


def column_sum(block):
    return jnp.sum(block, axis=0, keepdims=True)


def layer_kernel(tensor_size, plan, *refs):
    (
        x_ref, doc_ref, cot_ref,
        wqkv_hbm, bqv_ref, wout_hbm, bout_ref, gain1_ref, shift1_ref,
        wup_hbm, bup_ref, wdown_hbm, bdown_ref, gain2_ref, shift2_ref,
        out_ref, dx_ref, gqkv_ref, gout_ref, gup_ref, gdown_ref, small_ref,
        wqkv_ref, wout_ref, wup_ref, wdown_ref,
        gath, rs_send, rs_recv, rs_own,
        qkv, probs, ctx, entry, y1, n1, r1, slope, act, n2, r2, dh2, dh, du, dqkv,
        sent_up, back_in, sent_back, small_acc,
        pqkv, pout, pup, pdown,
        ag_ssem, ag_rsem, rs_ssem, rs_rsem, up_ssem, up_rsem, back_ssem, back_rsem,
        sum_ssem, sum_rsem, small_ssem, small_rsem, load_sem,
        *more,
    ) = refs
    spread_refs, sum_refs = more[: len(SPREAD)], more[len(SPREAD) :]
    grads = {"qkv": pqkv, "out": pout, "up": pup, "down": pdown}
    totals = {"qkv": gqkv_ref, "out": gout_ref, "up": gup_ref, "down": gdown_ref}
    loads = [
        pltpu.make_async_copy(source, target, load_sem.at[index])
        for index, (source, target) in enumerate(
            (
                (wqkv_hbm, wqkv_ref), (wout_hbm, wout_ref),
                (wup_hbm, wup_ref), (wdown_hbm, wdown_ref),
            )
        )
    ]
    for load in loads:
        load.start()
    batches, rows, width = x_ref.shape
    slot = rows * tensor_size
    local = wout_ref.shape[0]
    units = wup_ref.shape[1]
    pairs = local // (2 * HEAD_DIM)
    sec = lax.axis_index("section")
    me = lax.axis_index("tensor")
    dp = lax.axis_index("dp")
    other = 1 - sec
    scale = HEAD_DIM ** (-0.5)

    barrier = pltpu.get_barrier_semaphore()
    for k in range(1, tensor_size):
        pl.semaphore_signal(
            barrier, inc=1, device_id={"tensor": lax.rem(me + k, tensor_size)}, device_id_type=MESH
        )
    pl.semaphore_signal(barrier, inc=1, device_id={"section": other}, device_id_type=MESH)
    greeted = tensor_size
    for axis, (stride, size) in AXES.items():
        for k in range(1, size):
            index = lax.rem(dp // stride, size)
            near = dp + (lax.rem(index + k, size) - index) * stride
            pl.semaphore_signal(barrier, inc=1, device_id={"dp": near}, device_id_type=MESH)
            greeted += 1
    pl.semaphore_wait(barrier, greeted)

    def band(index):
        return pl.ds(pl.multiple_of(index * rows, rows), rows)

    mine = band(me)

    def gather_copy(e, m, k):
        return pltpu.make_async_remote_copy(
            src_ref=gath.at[e, m, mine],
            dst_ref=gath.at[e, m, mine],
            send_sem=ag_ssem.at[e, m, k - 1],
            recv_sem=ag_rsem.at[e, m, k - 1],
            device_id={"tensor": lax.rem(me + k, tensor_size)},
            device_id_type=MESH,
        )

    def gather_start(e, m):
        for k in range(1, tensor_size):
            gather_copy(e, m, k).start()

    def gather_wait(e, m):
        for k in range(1, tensor_size):
            source = band(lax.rem(me + tensor_size - k, tensor_size))
            pltpu.make_async_remote_copy(
                src_ref=gath.at[e, m, source],
                dst_ref=gath.at[e, m, source],
                send_sem=ag_ssem.at[e, m, k - 1],
                recv_sem=ag_rsem.at[e, m, k - 1],
                device_id={"tensor": lax.rem(me + k, tensor_size)},
                device_id_type=MESH,
            ).wait_recv()

    def scatter_copy(e, m, k):
        target = lax.rem(me + k, tensor_size)
        return pltpu.make_async_remote_copy(
            src_ref=rs_send.at[e, m, band(target)],
            dst_ref=rs_recv.at[e, m, k - 1],
            send_sem=rs_ssem.at[e, m, k - 1],
            recv_sem=rs_rsem.at[e, m, k - 1],
            device_id={"tensor": target},
            device_id_type=MESH,
        )

    def scatter_start(e, m):
        for k in range(1, tensor_size):
            scatter_copy(e, m, k).start()

    def scatter_wait(e, m):
        total = rs_own[m, mine, :]
        for k in range(1, tensor_size):
            scatter_copy(e, m, k).wait_recv()
        for k in range(1, tensor_size):
            total = total + rs_recv[e, m, k - 1].astype(F32)
        return total

    def put_part(e, m, columns, part):
        rs_own[m, :, columns] = part
        rs_send[e, m, :, columns] = part.astype(BF16)

    def up_copy(m):
        return pltpu.make_async_remote_copy(
            src_ref=sent_up.at[m],
            dst_ref=gath.at[0, m, mine],
            send_sem=up_ssem.at[m],
            recv_sem=up_rsem.at[m],
            device_id={"section": other},
            device_id_type=MESH,
        )

    def back_copy(m):
        return pltpu.make_async_remote_copy(
            src_ref=sent_back.at[m],
            dst_ref=back_in.at[m],
            send_sem=back_ssem.at[m],
            recv_sem=back_rsem.at[m],
            device_id={"section": other},
            device_id_type=MESH,
        )

    def each_batch(body):
        def step(m, carry):
            body(m)
            return carry

        lax.fori_loop(0, batches, step, 0)

    def chunks(total):
        return [pl.ds(c, min(STEP, total - c)) for c in range(0, total, STEP)]

    def head_mask():
        return lax.broadcasted_iota(jnp.int32, (slot, 2 * HEAD_DIM), 1) < HEAD_DIM

    def pick(first, block):
        low_half = head_mask()
        keep = low_half if first else jnp.logical_not(low_half)
        return jnp.where(keep, block, jnp.zeros_like(block))


    place = {axis: lax.rem(dp // stride, size) for axis, (stride, size) in AXES.items()}

    def dp_peer(axis, k):
        stride, size = AXES[axis]
        return {"dp": dp + (lax.rem(place[axis] + k, size) - place[axis]) * stride}

    sends = []

    def send(copy):
        copy.start()
        sends.append(copy)

    def sum_events(c):
        name, first, rows_all, columns, order = plan[c]
        grad, total = grads[name], totals[name]
        buffers = sum_refs[6 * c : 6 * c + 6]
        half = columns // 2
        low, high = pl.ds(0, half), pl.ds(half, half)
        sources, starts, blocks = [(grad, first)], [first], [rows_all]
        for axis in order:
            blocks.append(blocks[-1] // AXES[axis][1])

        def lines(start, count):
            return pl.ds(pl.multiple_of(start, count), count)

        def remote(source, target, sem, axis, k):
            return pltpu.make_async_remote_copy(
                src_ref=source,
                dst_ref=target,
                send_sem=sum_ssem.at[c, sem],
                recv_sem=sum_rsem.at[c, sem],
                device_id=dp_peer(axis, k),
                device_id_type=MESH,
            )

        def block_at(step, index):
            ref, base = sources[step]
            return ref, lines(base + index * blocks[step + 1], blocks[step + 1])

        def add(step, columns_at, parts):
            ref, at = block_at(step, place[order[step]])
            value = ref[at, columns_at].astype(F32)
            for part in parts:
                value = value + part.astype(F32)
            return value.astype(BF16)

        def finish(step, pieces):
            base = starts[step] + place[order[step]] * blocks[step + 1]
            starts.append(base)
            for columns_at, value in pieces:
                if step == 2:
                    total[lines(base, blocks[3]), columns_at] = value
                else:
                    buffers[2 * step + 1][:, columns_at] = value
            sources.append((buffers[2 * step + 1], 0))

        def pair_scatter(step):
            axis = order[step]
            landing = buffers[2 * step]

            def copy():
                ref, at = block_at(step, 1 - place[axis])
                return remote(ref.at[at], landing, RS_SEM[axis], axis, 1)

            def begin():
                send(copy())

            def end():
                copy().wait_recv()
                for columns_at in (low, high):
                    finish_piece = add(step, columns_at, [landing[:, columns_at]])
                    pieces.append((columns_at, finish_piece))
                finish(step, pieces)

            pieces = []
            return [begin, end]

        def ring_scatter(step):
            landing = buffers[2 * step]
            here = place["y"]

            def at(k, columns_at):
                ref, lines_at = block_at(step, lax.rem(here + k, 4))
                return ref.at[lines_at, columns_at]

            def copy(number):
                source, k = (
                    (lambda: at(2, high), 1),
                    (lambda: at(1, low), 1),
                    (lambda: at(2, low), 3),
                    (lambda: at(3, high), 3),
                    (lambda: landing.at[6], 1),
                    (lambda: landing.at[7], 3),
                )[number]
                return remote(source(), landing.at[number], RS_SEM["y"] + number, "y", k)

            def begin():
                for number in range(4):
                    send(copy(number))

            def relay():
                for number, k, columns_at, out in ((0, 1, high, 4), (2, 3, low, 5)):
                    copy(number).wait_recv()
                    value = at(k, columns_at)[...].astype(F32) + landing[number].astype(F32)
                    landing[out + 2] = value.astype(BF16)
                    send(copy(out))

            def end():
                for number in (1, 3, 4, 5):
                    copy(number).wait_recv()
                finish(
                    step,
                    [
                        (low, add(step, low, [landing[1], landing[5]])),
                        (high, add(step, high, [landing[3], landing[4]])),
                    ],
                )

            return [begin, relay, end]

        def region(step, index, columns_at=None):
            at = lines(starts[step] + index * blocks[step + 1], blocks[step + 1])
            return total.at[at] if columns_at is None else total.at[at, columns_at]

        def pair_gather(step):
            axis = order[step]

            def copy(index):
                return remote(region(step, index), region(step, index), AG_SEM[axis], axis, 1)

            return [
                lambda: send(copy(place[axis])),
                lambda: copy(1 - place[axis]).wait_recv(),
            ]

        def ring_gather(step):
            def copy(number, back):
                index = lax.rem(place["y"] + 4 - back, 4)
                columns_at = (None, None, low, high)[number]
                part = region(step, index, columns_at)
                return remote(part, part, AG_SEM["y"] + number, "y", (1, 3, 1, 3)[number])

            def begin():
                send(copy(0, 0))
                send(copy(1, 0))

            def relay():
                copy(0, 1).wait_recv()
                send(copy(2, 1))
                copy(1, 3).wait_recv()
                send(copy(3, 3))

            def end():
                copy(2, 2).wait_recv()
                copy(3, 2).wait_recv()

            return [begin, relay, end]

        def join(stages):
            events = [stages[0][0]]
            for stage, later in zip(stages, stages[1:] + [None]):
                events.extend(stage[1:-1])
                if later is None:
                    events.append(stage[-1])
                else:
                    events.append(lambda end=stage[-1], begin=later[0]: (end(), begin()))
            return events

        scatters = [ring_scatter(i) if a == "y" else pair_scatter(i) for i, a in enumerate(order)]
        gathers = [ring_gather(i) if a == "y" else pair_gather(i) for i, a in enumerate(order)]
        return join(scatters + gathers[::-1])

    events = [sum_events(c) for c in range(len(plan))]

    def advance(*which):
        for c in which:
            if events[c]:
                events[c].pop(0)()

    def spread_copy(step, k, source):
        axis = SPREAD[step]
        size = tensor_size if axis == "tensor" else AXES[axis][1]
        at = spread_refs[step].at[source]
        return pltpu.make_async_remote_copy(
            src_ref=at,
            dst_ref=at,
            send_sem=small_ssem.at[step, k - 1],
            recv_sem=small_rsem.at[step, k - 1],
            device_id={"tensor": lax.rem(me + k, size)} if axis == "tensor" else dp_peer(axis, k),
            device_id_type=MESH,
        )

    def spread_place(step):
        axis = SPREAD[step]
        return (me, tensor_size) if axis == "tensor" else (place[axis], AXES[axis][1])

    def spread_start(step, value):
        index, size = spread_place(step)
        spread_refs[step][index] = value
        for k in range(1, size):
            send(spread_copy(step, k, index))

    def spread_finish(step):
        index, size = spread_place(step)
        for k in range(1, size):
            spread_copy(step, k, lax.rem(index + size - k, size)).wait_recv()
        value = spread_refs[step][0]
        for other_index in range(1, size):
            value = value + spread_refs[step][other_index]
        return value

    small_acc[...] = jnp.zeros_like(small_acc)

    @pl.when(sec == 0)
    def _():
        for m in range(batches):
            gath[0, m, mine, :] = x_ref[m]

    for m in range(batches):
        @pl.when(sec == 1)
        def _():
            up_copy(m).wait_recv()

        gather_start(0, m)
        if m < batches - 1:
            for k in range(1, tensor_size):
                gather_copy(0, m, k).wait_send()

    for load in loads[:2]:
        load.wait()

    def attention(m):
        entry[m] = gath[0, m, mine, :].astype(F32)
        gather_wait(0, m)
        for third in range(3):
            part = dot(gath[0, m], wqkv_ref[third])
            if third != 1:
                part = part + bqv_ref[0, third // 2 : third // 2 + 1, :]
            qkv[m, :, pl.ds(third * local, local)] = part.astype(BF16)
        across = jnp.broadcast_to(doc_ref[pl.ds(m, 1), :].astype(F32), (slot, slot))
        down = jnp.transpose(across)
        row_id = lax.broadcasted_iota(jnp.int32, (slot, slot), 0)
        col_id = lax.broadcasted_iota(jnp.int32, (slot, slot), 1)
        allowed = ((across == down) & (across >= 0)) | (row_id == col_id)
        low_half = head_mask()
        for pair in range(pairs):
            at = pair * 2 * HEAD_DIM
            queries = qkv[m, :, pl.ds(at, 2 * HEAD_DIM)]
            key_heads = qkv[m, :, pl.ds(local + at, 2 * HEAD_DIM)]
            values = qkv[m, :, pl.ds(2 * local + at, 2 * HEAD_DIM)]
            halves = []
            for half in range(2):
                raw = dot_last(pick(half == 0, queries), key_heads) * scale
                scores = jnp.where(allowed, raw, -1e30)
                peak = jnp.max(scores, axis=-1, keepdims=True)
                exps = jnp.exp(scores - peak)
                soft = exps / jnp.sum(exps, axis=-1, keepdims=True)
                probs[m, pair * 2 + half] = soft
                halves.append(dot(soft.astype(BF16), values))
            ctx[m, :, pl.ds(at, 2 * HEAD_DIM)] = jnp.where(low_half, halves[0], halves[1]).astype(BF16)
        for cols in chunks(width):
            put_part(0, m, cols, dot(ctx[m], wout_ref[:, cols]))
        scatter_start(0, m)

    each_batch(attention)

    def first_norm(m):
        hidden = entry[m] + scatter_wait(0, m) + bout_ref[...]
        out, normed, inv_std = norm(hidden, gain1_ref[...], shift1_ref[...])
        y1[m], n1[m], r1[m] = out, normed, inv_std
        gath[1, m, mine, :] = out.astype(BF16)
        gather_start(1, m)

    each_batch(first_norm)

    for load in loads[2:]:
        load.wait()

    def feed_forward(m):
        gather_wait(1, m)
        for cols in chunks(units):
            pre = dot(gath[1, m], wup_ref[:, cols]) + bup_ref[:, cols]
            cdf = 0.5 * (1.0 + lax.erf(pre * (1.0 / math.sqrt(2.0))))
            slope[m, :, cols] = cdf + pre * jnp.exp(-0.5 * pre * pre) * (
                1.0 / math.sqrt(2.0 * math.pi)
            )
            act[m, :, cols] = (pre * cdf).astype(BF16)
        for cols in chunks(width):
            put_part(1, m, cols, dot(act[m], wdown_ref[:, cols]))
        scatter_start(1, m)

    each_batch(feed_forward)

    def second_norm(m):
        hidden = y1[m] + scatter_wait(1, m) + bdown_ref[...]
        out, normed, inv_std = norm(hidden, gain2_ref[...], shift2_ref[...])
        n2[m], r2[m] = normed, inv_std
        rounded = out.astype(BF16)
        out_ref[m] = rounded

        @pl.when(sec == 0)
        def _():
            sent_up[m] = rounded
            up_copy(m).start()

    each_batch(second_norm)

    def back_entry(m):
        @pl.when(sec == 1)
        def _():
            back_in[m] = cot_ref[m]

        @pl.when(sec == 0)
        def _():
            back_copy(m).wait_recv()

        grad_out = back_in[m].astype(F32)
        grad = norm_back(grad_out, n2[m], r2[m], gain2_ref[...])
        small_acc[0:1, :] += column_sum(grad)
        small_acc[1:2, :] += column_sum(grad_out * n2[m])
        small_acc[2:3, :] += column_sum(grad_out)
        dh2[m] = grad
        gath[2, m, mine, :] = grad.astype(BF16)
        gather_start(2, m)

    each_batch(back_entry)

    def feed_back(m):
        gather_wait(2, m)
        for cols in chunks(units):
            grad = (dot_last(gath[2, m], wdown_ref[cols, :]) * slope[m, :, cols]).astype(BF16)
            du[m, :, cols] = grad
            small_acc[6:7, cols] += column_sum(grad.astype(F32))
        for cols in chunks(width):
            put_part(2, m, cols, dot_last(du[m], wup_ref[cols, :]))
        scatter_start(2, m)

    each_batch(feed_back)

    def weight_grad(left, right, target, base=0):
        total = batches * slot
        rhs = right[...].reshape(total, right.shape[-1])
        for rows_at in chunks(left.shape[-1]):
            lhs = left[:, :, rows_at].reshape(total, rows_at.size)
            target[pl.ds(base + rows_at.start, rows_at.size), :] = dot_rows(lhs, rhs).astype(BF16)

    weight_grad(act, gath.at[2], pdown)
    advance(0)
    weight_grad(gath.at[1], du, pup)
    advance(1)

    def first_back(m):
        grad_out = dh2[m] + scatter_wait(2, m)
        grad = norm_back(grad_out, n1[m], r1[m], gain1_ref[...])
        small_acc[3:4, :] += column_sum(grad)
        small_acc[4:5, :] += column_sum(grad_out * n1[m])
        small_acc[5:6, :] += column_sum(grad_out)
        dh[m] = grad
        gath[3, m, mine, :] = grad.astype(BF16)
        gather_start(3, m)

    each_batch(first_back)

    advance(0, 1)

    def attention_back(m):
        gather_wait(3, m)
        low_half = head_mask()
        for pair in range(pairs):
            at = pair * 2 * HEAD_DIM
            dctx = dot_last(gath[3, m], wout_ref[pl.ds(at, 2 * HEAD_DIM), :]).astype(BF16)
            queries = qkv[m, :, pl.ds(at, 2 * HEAD_DIM)]
            key_heads = qkv[m, :, pl.ds(local + at, 2 * HEAD_DIM)]
            values = qkv[m, :, pl.ds(2 * local + at, 2 * HEAD_DIM)]
            dq, dk, dv = [], [], []
            for half in range(2):
                soft = probs[m, pair * 2 + half]
                dv.append(dot_rows(soft.astype(BF16), dctx))
                dprob = dot_last(pick(half == 0, dctx), values)
                dscore = soft * (dprob - jnp.sum(soft * dprob, axis=-1, keepdims=True))
                dscore = dscore.astype(BF16)
                dq.append(dot(dscore, key_heads) * scale)
                dk.append(dot_rows(dscore, queries) * scale)
            for place, (first, second) in enumerate((dq, dk, dv)):
                cols = pl.ds(place * local + at, 2 * HEAD_DIM)
                grad = jnp.where(low_half, first, second).astype(BF16)
                dqkv[m, :, cols] = grad
                if place != 1:
                    to = at if place == 0 else local + at
                    small_acc[7:8, pl.ds(to, 2 * HEAD_DIM)] += column_sum(grad.astype(F32))
        for cols in chunks(width):
            part = dot_last(dqkv[m, :, pl.ds(0, local)], wqkv_ref[0, cols, :])
            for third in range(1, 3):
                part = part + dot_last(
                    dqkv[m, :, pl.ds(third * local, local)], wqkv_ref[third, cols, :]
                )
            put_part(3, m, cols, part)
        scatter_start(3, m)

    each_batch(attention_back)

    spread_start(0, small_acc[...])
    advance(0, 1)
    weight_grad(ctx, gath.at[3], pout)
    advance(2)

    def last_back(m):
        grad = dh[m] + scatter_wait(3, m)
        dx_ref[m] = grad

        @pl.when(sec == 1)
        def _():
            sent_back[m] = grad.astype(BF16)
            back_copy(m).start()

    each_batch(last_back)
    for third in range(3):
        weight_grad(
            gath.at[0], dqkv.at[:, :, pl.ds(third * local, local)], pqkv, base=third * width
        )
    advance(3, 4)
    advance(0, 1)
    small_row = lax.broadcasted_iota(jnp.int32, small_acc.shape, 0)
    spread_start(1, jnp.where(small_row < 6, spread_finish(0), small_acc[...]))
    small_step = 1
    while any(events):
        for c in (2, 3, 4, 0, 1):
            advance(c)
        if small_step < len(SPREAD):
            value = spread_finish(small_step)
            small_step += 1
            if small_step < len(SPREAD):
                spread_start(small_step, value)
            else:
                small_ref[...] = value

    for copy in sends:
        copy.wait_send()

    def drain(m):
        for e in range(4):
            for k in range(1, tensor_size):
                scatter_copy(e, m, k).wait_send()
                if e:
                    gather_copy(e, m, k).wait_send()

        @pl.when(sec == 0)
        def _():
            up_copy(m).wait_send()

        @pl.when(sec == 1)
        def _():
            back_copy(m).wait_send()

    for k in range(1, tensor_size):
        gather_copy(0, batches - 1, k).wait_send()
    each_batch(drain)


def run_layer(x, docs, cot, weights, tensor_size):
    batches, rows, width = x.shape
    slot = rows * tensor_size
    wqkv, bqv, wout, bout, gain1, shift1, wup, bup, wdown, bdown, gain2, shift2 = weights
    local = wout.shape[0]
    units = wup.shape[1]
    heads = local // HEAD_DIM
    vmem = pl.BlockSpec(memory_space=pltpu.VMEM)
    others = tensor_size - 1
    dma = pltpu.SemaphoreType.DMA
    operands = (x, docs, cot) + weights
    small_shape = (8, width)
    shard = (batches, rows, width)
    shapes = (
        jax.ShapeDtypeStruct(shard, BF16),
        jax.ShapeDtypeStruct(shard, F32),
        jax.ShapeDtypeStruct((3 * width, local), BF16),
        jax.ShapeDtypeStruct(wout.shape, BF16),
        jax.ShapeDtypeStruct(wup.shape, BF16),
        jax.ShapeDtypeStruct(wdown.shape, BF16),
        jax.ShapeDtypeStruct(small_shape, F32),
    )
    plan = sum_plan(width, local, units)
    scratch = [
        pltpu.VMEM(wqkv.shape, BF16),
        pltpu.VMEM(wout.shape, BF16),
        pltpu.VMEM(wup.shape, BF16),
        pltpu.VMEM(wdown.shape, BF16),
        pltpu.VMEM((4, batches, slot, width), BF16),
        pltpu.VMEM((4, batches, slot, width), BF16),
        pltpu.VMEM((4, batches, others, rows, width), BF16),
        pltpu.VMEM((batches, slot, width), F32),
        pltpu.VMEM((batches, slot, 3 * local), BF16),
        pltpu.VMEM((batches, heads, slot, slot), F32),
        pltpu.VMEM((batches, slot, local), BF16),
        pltpu.VMEM(shard, F32),
        pltpu.VMEM(shard, F32),
        pltpu.VMEM(shard, F32),
        pltpu.VMEM((batches, rows, 1), F32),
        pltpu.VMEM((batches, slot, units), F32),
        pltpu.VMEM((batches, slot, units), BF16),
        pltpu.VMEM(shard, F32),
        pltpu.VMEM((batches, rows, 1), F32),
        pltpu.VMEM(shard, F32),
        pltpu.VMEM(shard, F32),
        pltpu.VMEM((batches, slot, units), BF16),
        pltpu.VMEM((batches, slot, 3 * local), BF16),
        pltpu.VMEM(shard, BF16),
        pltpu.VMEM(shard, BF16),
        pltpu.VMEM(shard, BF16),
        pltpu.VMEM(small_shape, F32),
        pltpu.VMEM((3 * width, local), BF16),
        pltpu.VMEM(wout.shape, BF16),
        pltpu.VMEM(wup.shape, BF16),
        pltpu.VMEM(wdown.shape, BF16),
        dma((4, batches, others)),
        dma((4, batches, others)),
        dma((4, batches, others)),
        dma((4, batches, others)),
        dma((batches,)),
        dma((batches,)),
        dma((batches,)),
        dma((batches,)),
        dma((len(plan), 14)),
        dma((len(plan), 14)),
        dma((len(SPREAD), 3)),
        dma((len(SPREAD), 3)),
        dma((4,)),
    ]
    for axis in SPREAD:
        size = tensor_size if axis == "tensor" else AXES[axis][1]
        scratch.append(pltpu.VMEM((size,) + small_shape, F32))
    for _, _, rows_all, columns, order in plan:
        scratch.extend(pltpu.VMEM(shape, BF16) for shape in sum_buffers(rows_all, columns, order))
    in_specs = [vmem] * len(operands)
    for index in (3, 5, 9, 11):
        in_specs[index] = pl.BlockSpec(memory_space=pl.ANY)
    return pl.pallas_call(
        functools.partial(layer_kernel, tensor_size, plan),
        out_shape=shapes,
        in_specs=in_specs,
        out_specs=[vmem] * len(shapes),
        scratch_shapes=scratch,
        compiler_params=pltpu.CompilerParams(
            collective_id=0, has_side_effects=True, vmem_limit_bytes=VMEM_BYTES
        ),
        name="layer",
    )(*operands)


def shards(
    inputs, doc_ids, cotangent, w_qkv, b_qv, w_out, b_out, gain1, shift1,
    w_up, b_up, w_down, b_down, gain2, shift2,
):
    tensor_size = lax.axis_size("tensor")
    width = inputs.shape[2]
    local = w_out.shape[1]
    weights = (
        jnp.transpose(w_qkv[0], (1, 0, 2)), b_qv, w_out[0], b_out, gain1, shift1,
        w_up[0], b_up, w_down[0], b_down, gain2, shift2,
    )
    outputs, input_grads, gqkv, gout, gup, gdown, small = run_layer(
        inputs, doc_ids, cotangent, weights, tensor_size
    )
    return (
        outputs[None],
        input_grads[None],
        jnp.transpose(gqkv.astype(F32).reshape(3, width, local), (1, 0, 2))[None],
        small[7:8, : 2 * local].reshape(1, 2, local),
        gout.astype(F32)[None],
        small[3:4],
        small[4:5],
        small[5:6],
        gup.astype(F32)[None],
        small[6:7],
        gdown.astype(F32)[None],
        small[0:1],
        small[1:2],
        small[2:3],
    )


def solution(mesh):
    rows = P(None, ("dp", "tensor"), None)
    banked = P("section", None, ("dp", "tensor"), None)
    vector = P("section", None)
    return jax.shard_map(
        shards,
        mesh=mesh,
        in_specs=(
            rows,
            P(None, "dp"),
            rows,
            P("section", None, None, "tensor"),
            P("section", None, "tensor"),
            P("section", "tensor", None),
            vector,
            vector,
            vector,
            P("section", None, "tensor"),
            P("section", "tensor"),
            P("section", "tensor", None),
            vector,
            vector,
            vector,
        ),
        out_specs=(
            banked,
            banked,
            P("section", None, None, "tensor"),
            P("section", None, "tensor"),
            P("section", "tensor", None),
            vector,
            vector,
            vector,
            P("section", None, "tensor"),
            P("section", "tensor"),
            P("section", "tensor", None),
            vector,
            vector,
            vector,
        ),
        check_vma=False,
    )
```

```python
import functools
import math

import jax
import jax.numpy as jnp
from jax import lax
from jax.experimental import pallas as pl
from jax.experimental.pallas import tpu as pltpu
from jax.sharding import PartitionSpec as P

HEAD_DIM = 64
MESH = pl.DeviceIdType.MESH
F32 = jnp.float32
BF16 = jnp.bfloat16
STEP = 256
SPREAD = ("tensor", "core", "y", "x")
VMEM_BYTES = 52 * 1024 * 1024
UNPACK_BYTES = 40 * 1024 * 1024
AXES = {"core": (1, 2), "x": (2, 2), "y": (4, 4)}
SIZES = {"core": 2, "x": 2, "y": 4, "ring": 4}
RS_SEM = {"core": 0, "x": 1, "y": 2, "ring": 2}
AG_SEM = {"core": 8, "x": 9, "y": 10, "ring": 10}
X_FIRST = ("core", "x", "ring")
Y_FIRST = ("core", "ring", "x")
X_FIRST_DIRECT = ("core", "x", "y")
Y_FIRST_DIRECT = ("core", "y", "x")


def sum_plan(width, local, units):
    joined = 3 * width
    return (
        ("down", 0, units // 2, width, X_FIRST),
        ("down", units // 2, units // 2, width, Y_FIRST),
        ("up", 0, width // 2, units, X_FIRST),
        ("up", width // 2, width // 2, units, Y_FIRST),
        ("out", 0, local, width, Y_FIRST_DIRECT),
        ("qkv", 0, joined // 2, local, X_FIRST_DIRECT),
        ("qkv", joined // 2, joined // 2, local, Y_FIRST_DIRECT),
    )


def sum_buffers(rows, columns, order):
    shapes = []
    for axis in order:
        rows //= SIZES[axis]
        if axis == "ring":
            shapes.append((8, rows, columns // 2))
        elif axis == "y":
            shapes.append((3, rows, columns))
        else:
            shapes.append((rows, columns))
        shapes.append((rows, columns))
    return shapes


def dot(left, right):
    return lax.dot_general(left, right, (((1,), (0,)), ((), ())), preferred_element_type=F32)


def dot_last(left, right):
    return lax.dot_general(left, right, (((1,), (1,)), ((), ())), preferred_element_type=F32)


def dot_rows(left, right):
    return lax.dot_general(left, right, (((0,), (0,)), ((), ())), preferred_element_type=F32)


def norm(hidden, gain, shift):
    centred = hidden - jnp.mean(hidden, axis=-1, keepdims=True)
    inv_std = lax.rsqrt(jnp.mean(centred * centred, axis=-1, keepdims=True) + 1e-05)
    normed = centred * inv_std
    return normed * gain + shift, normed, inv_std


def norm_back(grad_out, normed, inv_std, gain):
    scaled = grad_out * gain
    return inv_std * (
        scaled
        - jnp.mean(scaled, axis=-1, keepdims=True)
        - normed * jnp.mean(scaled * normed, axis=-1, keepdims=True)
    )


def column_sum(block):
    return jnp.sum(block, axis=0, keepdims=True)


def layer_kernel(tensor_size, plan, *refs):
    (
        x_ref, doc_ref, cot_ref,
        wqkv_hbm, bqv_ref, wout_hbm, bout_ref, gain1_ref, shift1_ref,
        wup_hbm, bup_ref, wdown_hbm, bdown_ref, gain2_ref, shift2_ref,
        out_ref, dx_ref, gqkv_ref, gout_ref, gup_ref, gdown_ref, small_ref,
        wqkv_ref, wout_ref, wup_ref, wdown_ref,
        gath, rs_send, rs_recv, rs_own,
        qkv, probs, ctx, entry, y1, n1, r1, slope, act, n2, r2, dh2, dh, du, dqkv,
        sent_up, back_in, sent_back, small_acc,
        pqkv, pout, pup, pdown,
        ag_ssem, ag_rsem, rs_ssem, rs_rsem, up_ssem, up_rsem, back_ssem, back_rsem,
        sum_ssem, sum_rsem, small_ssem, small_rsem, load_sem,
        *more,
    ) = refs
    spread_refs, sum_refs = more[: len(SPREAD)], more[len(SPREAD) :]
    grads = {"qkv": pqkv, "out": pout, "up": pup, "down": pdown}
    totals = {"qkv": gqkv_ref, "out": gout_ref, "up": gup_ref, "down": gdown_ref}
    loads = [
        pltpu.make_async_copy(source, target, load_sem.at[index])
        for index, (source, target) in enumerate(
            (
                (wqkv_hbm, wqkv_ref), (wout_hbm, wout_ref),
                (wup_hbm, wup_ref), (wdown_hbm, wdown_ref),
            )
        )
    ]
    for load in loads:
        load.start()
    batches, rows, width = x_ref.shape
    slot = rows * tensor_size
    local = wout_ref.shape[0]
    units = wup_ref.shape[1]
    pairs = local // (2 * HEAD_DIM)
    sec = lax.axis_index("section")
    me = lax.axis_index("tensor")
    dp = lax.axis_index("dp")
    other = 1 - sec
    scale = HEAD_DIM ** (-0.5)

    barrier = pltpu.get_barrier_semaphore()
    for k in range(1, tensor_size):
        pl.semaphore_signal(
            barrier, inc=1, device_id={"tensor": lax.rem(me + k, tensor_size)}, device_id_type=MESH
        )
    pl.semaphore_signal(barrier, inc=1, device_id={"section": other}, device_id_type=MESH)
    greeted = tensor_size
    for axis, (stride, size) in AXES.items():
        for k in range(1, size):
            index = lax.rem(dp // stride, size)
            near = dp + (lax.rem(index + k, size) - index) * stride
            pl.semaphore_signal(barrier, inc=1, device_id={"dp": near}, device_id_type=MESH)
            greeted += 1
    pl.semaphore_wait(barrier, greeted)

    def band(index):
        return pl.ds(pl.multiple_of(index * rows, rows), rows)

    mine = band(me)

    def gather_copy(e, m, k):
        return pltpu.make_async_remote_copy(
            src_ref=gath.at[e, m, mine],
            dst_ref=gath.at[e, m, mine],
            send_sem=ag_ssem.at[e, m, k - 1],
            recv_sem=ag_rsem.at[e, m, k - 1],
            device_id={"tensor": lax.rem(me + k, tensor_size)},
            device_id_type=MESH,
        )

    def gather_start(e, m):
        for k in range(1, tensor_size):
            gather_copy(e, m, k).start()

    def gather_wait(e, m):
        for k in range(1, tensor_size):
            source = band(lax.rem(me + tensor_size - k, tensor_size))
            pltpu.make_async_remote_copy(
                src_ref=gath.at[e, m, source],
                dst_ref=gath.at[e, m, source],
                send_sem=ag_ssem.at[e, m, k - 1],
                recv_sem=ag_rsem.at[e, m, k - 1],
                device_id={"tensor": lax.rem(me + k, tensor_size)},
                device_id_type=MESH,
            ).wait_recv()

    def scatter_copy(e, m, k):
        target = lax.rem(me + k, tensor_size)
        return pltpu.make_async_remote_copy(
            src_ref=rs_send.at[e, m, band(target)],
            dst_ref=rs_recv.at[e, m, k - 1],
            send_sem=rs_ssem.at[e, m, k - 1],
            recv_sem=rs_rsem.at[e, m, k - 1],
            device_id={"tensor": target},
            device_id_type=MESH,
        )

    def scatter_start(e, m):
        for k in range(1, tensor_size):
            scatter_copy(e, m, k).start()

    def scatter_wait(e, m):
        total = rs_own[m, mine, :]
        for k in range(1, tensor_size):
            scatter_copy(e, m, k).wait_recv()
        for k in range(1, tensor_size):
            total = total + rs_recv[e, m, k - 1].astype(F32)
        return total

    def put_part(e, m, columns, part):
        rs_own[m, :, columns] = part
        rs_send[e, m, :, columns] = part.astype(BF16)

    def up_copy(m):
        return pltpu.make_async_remote_copy(
            src_ref=sent_up.at[m],
            dst_ref=gath.at[0, m, mine],
            send_sem=up_ssem.at[m],
            recv_sem=up_rsem.at[m],
            device_id={"section": other},
            device_id_type=MESH,
        )

    def back_copy(m):
        return pltpu.make_async_remote_copy(
            src_ref=sent_back.at[m],
            dst_ref=back_in.at[m],
            send_sem=back_ssem.at[m],
            recv_sem=back_rsem.at[m],
            device_id={"section": other},
            device_id_type=MESH,
        )

    def each_batch(body, between=None):
        def step(m, carry):
            body(m)
            return carry

        if between is None:
            lax.fori_loop(0, batches, step, 0)
        else:
            for m in range(batches):
                body(m)
                between(m)

    def chunks(total):
        return [pl.ds(c, min(STEP, total - c)) for c in range(0, total, STEP)]

    def head_mask():
        return lax.broadcasted_iota(jnp.int32, (slot, 2 * HEAD_DIM), 1) < HEAD_DIM

    def pick(first, block):
        low_half = head_mask()
        keep = low_half if first else jnp.logical_not(low_half)
        return jnp.where(keep, block, jnp.zeros_like(block))


    place = {axis: lax.rem(dp // stride, size) for axis, (stride, size) in AXES.items()}

    def dp_peer(axis, k):
        stride, size = AXES[axis]
        return {"dp": dp + (lax.rem(place[axis] + k, size) - place[axis]) * stride}

    sends = []

    def send(copy):
        copy.start()
        sends.append(copy)

    def sum_events(c):
        name, first, rows_all, columns, order = plan[c]
        grad, total = grads[name], totals[name]
        buffers = sum_refs[6 * c : 6 * c + 6]
        half = columns // 2
        low, high = pl.ds(0, half), pl.ds(half, half)
        sources, starts, blocks = [(grad, first)], [first], [rows_all]
        for axis in order:
            blocks.append(blocks[-1] // SIZES[axis])

        def lines(start, count):
            return pl.ds(pl.multiple_of(start, count), count)

        def remote(source, target, sem, axis, k):
            return pltpu.make_async_remote_copy(
                src_ref=source,
                dst_ref=target,
                send_sem=sum_ssem.at[c, sem],
                recv_sem=sum_rsem.at[c, sem],
                device_id=dp_peer(axis, k),
                device_id_type=MESH,
            )

        def spot(step):
            return place["y" if order[step] == "ring" else order[step]]

        def block_at(step, index):
            ref, base = sources[step]
            return ref, lines(base + index * blocks[step + 1], blocks[step + 1])

        def add(step, columns_at, parts):
            ref, at = block_at(step, spot(step))
            value = ref[at, columns_at].astype(F32)
            for part in parts:
                value = value + part.astype(F32)
            return value.astype(BF16)

        def finish(step, pieces):
            base = starts[step] + spot(step) * blocks[step + 1]
            starts.append(base)
            for columns_at, value in pieces:
                if step == 2:
                    total[lines(base, blocks[3]), columns_at] = value
                else:
                    buffers[2 * step + 1][:, columns_at] = value
            sources.append((buffers[2 * step + 1], 0))

        def pair_scatter(step):
            axis = order[step]
            landing = buffers[2 * step]

            def copy():
                ref, at = block_at(step, 1 - place[axis])
                return remote(ref.at[at], landing, RS_SEM[axis], axis, 1)

            def begin():
                send(copy())

            def end():
                copy().wait_recv()
                for columns_at in (low, high):
                    finish_piece = add(step, columns_at, [landing[:, columns_at]])
                    pieces.append((columns_at, finish_piece))
                finish(step, pieces)

            pieces = []
            return [begin, end]

        def direct_scatter(step):
            landing = buffers[2 * step]

            def copy(k):
                ref, at = block_at(step, lax.rem(place["y"] + k, 4))
                return remote(ref.at[at], landing.at[k - 1], RS_SEM["y"] + k - 1, "y", k)

            def begin():
                for k in range(1, 4):
                    send(copy(k))

            def end():
                for k in range(1, 4):
                    copy(k).wait_recv()
                pieces = []
                for columns_at in (low, high):
                    parts = [landing[k, :, columns_at] for k in range(3)]
                    pieces.append((columns_at, add(step, columns_at, parts)))
                finish(step, pieces)

            return [begin, end]

        def ring_scatter(step):
            landing = buffers[2 * step]
            here = place["y"]

            def at(k, columns_at):
                ref, lines_at = block_at(step, lax.rem(here + k, 4))
                return ref.at[lines_at, columns_at]

            def copy(number):
                source, k = (
                    (lambda: at(2, high), 1),
                    (lambda: at(1, low), 1),
                    (lambda: at(2, low), 3),
                    (lambda: at(3, high), 3),
                    (lambda: landing.at[6], 1),
                    (lambda: landing.at[7], 3),
                )[number]
                return remote(source(), landing.at[number], RS_SEM["y"] + number, "y", k)

            def begin():
                for number in range(4):
                    send(copy(number))

            def relay():
                for number, k, columns_at, out in ((0, 1, high, 4), (2, 3, low, 5)):
                    copy(number).wait_recv()
                    value = at(k, columns_at)[...].astype(F32) + landing[number].astype(F32)
                    landing[out + 2] = value.astype(BF16)
                    send(copy(out))

            def end():
                for number in (1, 3, 4, 5):
                    copy(number).wait_recv()
                finish(
                    step,
                    [
                        (low, add(step, low, [landing[1], landing[5]])),
                        (high, add(step, high, [landing[3], landing[4]])),
                    ],
                )

            return [begin, relay, end]

        def region(step, index, columns_at=None):
            at = lines(starts[step] + index * blocks[step + 1], blocks[step + 1])
            return total.at[at] if columns_at is None else total.at[at, columns_at]

        def pair_gather(step):
            axis = order[step]

            def copy(index):
                return remote(region(step, index), region(step, index), AG_SEM[axis], axis, 1)

            return [
                lambda: send(copy(place[axis])),
                lambda: copy(1 - place[axis]).wait_recv(),
            ]

        def direct_gather(step):
            def copy(k, back):
                part = region(step, lax.rem(place["y"] + 4 - back, 4))
                return remote(part, part, AG_SEM["y"] + k - 1, "y", k)

            def begin():
                for k in range(1, 4):
                    send(copy(k, 0))

            def end():
                for k in range(1, 4):
                    copy(k, k).wait_recv()

            return [begin, end]

        def ring_gather(step):
            def copy(number, back):
                index = lax.rem(place["y"] + 4 - back, 4)
                columns_at = (None, None, low, high)[number]
                part = region(step, index, columns_at)
                return remote(part, part, AG_SEM["y"] + number, "y", (1, 3, 1, 3)[number])

            def begin():
                send(copy(0, 0))
                send(copy(1, 0))

            def relay():
                copy(0, 1).wait_recv()
                send(copy(2, 1))
                copy(1, 3).wait_recv()
                send(copy(3, 3))

            def end():
                copy(2, 2).wait_recv()
                copy(3, 2).wait_recv()

            return [begin, relay, end]

        def join(stages):
            events = [stages[0][0]]
            for stage, later in zip(stages, stages[1:] + [None]):
                events.extend(stage[1:-1])
                if later is None:
                    events.append(stage[-1])
                else:
                    events.append(lambda end=stage[-1], begin=later[0]: (end(), begin()))
            return events

        forms = {
            "core": (pair_scatter, pair_gather),
            "x": (pair_scatter, pair_gather),
            "y": (direct_scatter, direct_gather),
            "ring": (ring_scatter, ring_gather),
        }
        scatters = [forms[axis][0](step) for step, axis in enumerate(order)]
        gathers = [forms[axis][1](step) for step, axis in enumerate(order)]
        return join(scatters + gathers[::-1])

    events = [sum_events(c) for c in range(len(plan))]

    def advance(*which):
        for c in which:
            if events[c]:
                events[c].pop(0)()

    def spread_copy(step, k, source):
        axis = SPREAD[step]
        size = tensor_size if axis == "tensor" else AXES[axis][1]
        at = spread_refs[step].at[source]
        return pltpu.make_async_remote_copy(
            src_ref=at,
            dst_ref=at,
            send_sem=small_ssem.at[step, k - 1],
            recv_sem=small_rsem.at[step, k - 1],
            device_id={"tensor": lax.rem(me + k, size)} if axis == "tensor" else dp_peer(axis, k),
            device_id_type=MESH,
        )

    def spread_place(step):
        axis = SPREAD[step]
        return (me, tensor_size) if axis == "tensor" else (place[axis], AXES[axis][1])

    def spread_start(step, value):
        index, size = spread_place(step)
        spread_refs[step][index] = value
        for k in range(1, size):
            send(spread_copy(step, k, index))

    def spread_finish(step):
        index, size = spread_place(step)
        for k in range(1, size):
            spread_copy(step, k, lax.rem(index + size - k, size)).wait_recv()
        value = spread_refs[step][0]
        for other_index in range(1, size):
            value = value + spread_refs[step][other_index]
        return value

    small_acc[...] = jnp.zeros_like(small_acc)

    @pl.when(sec == 0)
    def _():
        for m in range(batches):
            gath[0, m, mine, :] = x_ref[m]

    for m in range(batches):
        @pl.when(sec == 1)
        def _():
            up_copy(m).wait_recv()

        gather_start(0, m)
        if m < batches - 1:
            for k in range(1, tensor_size):
                gather_copy(0, m, k).wait_send()

    for load in loads[:2]:
        load.wait()

    def attention(m):
        entry[m] = gath[0, m, mine, :].astype(F32)
        gather_wait(0, m)
        for third in range(3):
            part = dot(gath[0, m], wqkv_ref[third])
            if third != 1:
                part = part + bqv_ref[0, third // 2 : third // 2 + 1, :]
            qkv[m, :, pl.ds(third * local, local)] = part.astype(BF16)
        across = jnp.broadcast_to(doc_ref[pl.ds(m, 1), :].astype(F32), (slot, slot))
        down = jnp.transpose(across)
        row_id = lax.broadcasted_iota(jnp.int32, (slot, slot), 0)
        col_id = lax.broadcasted_iota(jnp.int32, (slot, slot), 1)
        allowed = ((across == down) & (across >= 0)) | (row_id == col_id)
        low_half = head_mask()
        for pair in range(pairs):
            at = pair * 2 * HEAD_DIM
            queries = qkv[m, :, pl.ds(at, 2 * HEAD_DIM)]
            key_heads = qkv[m, :, pl.ds(local + at, 2 * HEAD_DIM)]
            values = qkv[m, :, pl.ds(2 * local + at, 2 * HEAD_DIM)]
            halves = []
            for half in range(2):
                raw = dot_last(pick(half == 0, queries), key_heads) * scale
                scores = jnp.where(allowed, raw, -1e30)
                peak = jnp.max(scores, axis=-1, keepdims=True)
                exps = jnp.exp(scores - peak)
                soft = exps / jnp.sum(exps, axis=-1, keepdims=True)
                probs[m, pair * 2 + half] = soft
                halves.append(dot(soft.astype(BF16), values))
            ctx[m, :, pl.ds(at, 2 * HEAD_DIM)] = jnp.where(low_half, halves[0], halves[1]).astype(BF16)
        for cols in chunks(width):
            put_part(0, m, cols, dot(ctx[m], wout_ref[:, cols]))
        scatter_start(0, m)

    each_batch(attention)

    def first_norm(m):
        hidden = entry[m] + scatter_wait(0, m) + bout_ref[...]
        out, normed, inv_std = norm(hidden, gain1_ref[...], shift1_ref[...])
        y1[m], n1[m], r1[m] = out, normed, inv_std
        gath[1, m, mine, :] = out.astype(BF16)
        gather_start(1, m)

    each_batch(first_norm)

    for load in loads[2:]:
        load.wait()

    def feed_forward(m):
        gather_wait(1, m)
        for cols in chunks(units):
            pre = dot(gath[1, m], wup_ref[:, cols]) + bup_ref[:, cols]
            cdf = 0.5 * (1.0 + lax.erf(pre * (1.0 / math.sqrt(2.0))))
            slope[m, :, cols] = cdf + pre * jnp.exp(-0.5 * pre * pre) * (
                1.0 / math.sqrt(2.0 * math.pi)
            )
            act[m, :, cols] = (pre * cdf).astype(BF16)
        for cols in chunks(width):
            put_part(1, m, cols, dot(act[m], wdown_ref[:, cols]))
        scatter_start(1, m)

    each_batch(feed_forward)

    def second_norm(m):
        hidden = y1[m] + scatter_wait(1, m) + bdown_ref[...]
        out, normed, inv_std = norm(hidden, gain2_ref[...], shift2_ref[...])
        n2[m], r2[m] = normed, inv_std
        rounded = out.astype(BF16)
        out_ref[m] = rounded

        @pl.when(sec == 0)
        def _():
            sent_up[m] = rounded
            up_copy(m).start()

    each_batch(second_norm)

    def back_entry(m):
        @pl.when(sec == 1)
        def _():
            back_in[m] = cot_ref[m]

        @pl.when(sec == 0)
        def _():
            back_copy(m).wait_recv()

        grad_out = back_in[m].astype(F32)
        grad = norm_back(grad_out, n2[m], r2[m], gain2_ref[...])
        small_acc[0:1, :] += column_sum(grad)
        small_acc[1:2, :] += column_sum(grad_out * n2[m])
        small_acc[2:3, :] += column_sum(grad_out)
        dh2[m] = grad
        gath[2, m, mine, :] = grad.astype(BF16)
        gather_start(2, m)

    each_batch(back_entry)

    def feed_back(m):
        gather_wait(2, m)
        for cols in chunks(units):
            grad = (dot_last(gath[2, m], wdown_ref[cols, :]) * slope[m, :, cols]).astype(BF16)
            du[m, :, cols] = grad
            small_acc[6:7, cols] += column_sum(grad.astype(F32))
        for cols in chunks(width):
            put_part(2, m, cols, dot_last(du[m], wup_ref[cols, :]))
        scatter_start(2, m)

    each_batch(feed_back)

    def weight_grad(left, right, target, base=0):
        total = batches * slot
        rhs = right[...].reshape(total, right.shape[-1])
        for rows_at in chunks(left.shape[-1]):
            lhs = left[:, :, rows_at].reshape(total, rows_at.size)
            target[pl.ds(base + rows_at.start, rows_at.size), :] = dot_rows(lhs, rhs).astype(BF16)

    weight_grad(act, gath.at[2], pdown)
    advance(0, 1)
    weight_grad(gath.at[1], du, pup)
    advance(2, 3)

    def first_back(m):
        grad_out = dh2[m] + scatter_wait(2, m)
        grad = norm_back(grad_out, n1[m], r1[m], gain1_ref[...])
        small_acc[3:4, :] += column_sum(grad)
        small_acc[4:5, :] += column_sum(grad_out * n1[m])
        small_acc[5:6, :] += column_sum(grad_out)
        dh[m] = grad
        gath[3, m, mine, :] = grad.astype(BF16)
        gather_start(3, m)

    each_batch(first_back, lambda m: advance(0, 1) if m == 0 else advance(2, 3))

    def attention_back(m):
        gather_wait(3, m)
        low_half = head_mask()
        for pair in range(pairs):
            at = pair * 2 * HEAD_DIM
            dctx = dot_last(gath[3, m], wout_ref[pl.ds(at, 2 * HEAD_DIM), :]).astype(BF16)
            queries = qkv[m, :, pl.ds(at, 2 * HEAD_DIM)]
            key_heads = qkv[m, :, pl.ds(local + at, 2 * HEAD_DIM)]
            values = qkv[m, :, pl.ds(2 * local + at, 2 * HEAD_DIM)]
            dq, dk, dv = [], [], []
            for half in range(2):
                soft = probs[m, pair * 2 + half]
                dv.append(dot_rows(soft.astype(BF16), dctx))
                dprob = dot_last(pick(half == 0, dctx), values)
                dscore = soft * (dprob - jnp.sum(soft * dprob, axis=-1, keepdims=True))
                dscore = dscore.astype(BF16)
                dq.append(dot(dscore, key_heads) * scale)
                dk.append(dot_rows(dscore, queries) * scale)
            for place, (first, second) in enumerate((dq, dk, dv)):
                cols = pl.ds(place * local + at, 2 * HEAD_DIM)
                grad = jnp.where(low_half, first, second).astype(BF16)
                dqkv[m, :, cols] = grad
                if place != 1:
                    to = at if place == 0 else local + at
                    small_acc[7:8, pl.ds(to, 2 * HEAD_DIM)] += column_sum(grad.astype(F32))
        for cols in chunks(width):
            part = dot_last(dqkv[m, :, pl.ds(0, local)], wqkv_ref[0, cols, :])
            for third in range(1, 3):
                part = part + dot_last(
                    dqkv[m, :, pl.ds(third * local, local)], wqkv_ref[third, cols, :]
                )
            put_part(3, m, cols, part)
        scatter_start(3, m)

    each_batch(attention_back, lambda m: advance(1) if m == 0 else None)

    spread_start(0, small_acc[...])
    weight_grad(ctx, gath.at[3], pout)
    advance(4)
    advance(0, 1)

    def last_back(m):
        grad = dh[m] + scatter_wait(3, m)
        dx_ref[m] = grad

        @pl.when(sec == 1)
        def _():
            sent_back[m] = grad.astype(BF16)
            back_copy(m).start()

    each_batch(last_back, lambda m: advance(2, 3, 4) if m == 0 else None)
    for third in range(3):
        weight_grad(
            gath.at[0], dqkv.at[:, :, pl.ds(third * local, local)], pqkv, base=third * width
        )
    advance(5, 6)
    small_row = lax.broadcasted_iota(jnp.int32, small_acc.shape, 0)
    spread_start(1, jnp.where(small_row < 6, spread_finish(0), small_acc[...]))
    small_step = 1
    while any(events):
        advance(0, 1, 2, 3, 4, 5, 6)
        if small_step < len(SPREAD):
            value = spread_finish(small_step)
            small_step += 1
            if small_step < len(SPREAD):
                spread_start(small_step, value)
            else:
                small_ref[...] = value

    for copy in sends:
        copy.wait_send()

    def drain(m):
        for e in range(4):
            for k in range(1, tensor_size):
                scatter_copy(e, m, k).wait_send()
                if e:
                    gather_copy(e, m, k).wait_send()

        @pl.when(sec == 0)
        def _():
            up_copy(m).wait_send()

        @pl.when(sec == 1)
        def _():
            back_copy(m).wait_send()

    for k in range(1, tensor_size):
        gather_copy(0, batches - 1, k).wait_send()
    each_batch(drain)


def run_layer(x, docs, cot, weights, tensor_size):
    batches, rows, width = x.shape
    slot = rows * tensor_size
    wqkv, bqv, wout, bout, gain1, shift1, wup, bup, wdown, bdown, gain2, shift2 = weights
    local = wout.shape[0]
    units = wup.shape[1]
    heads = local // HEAD_DIM
    vmem = pl.BlockSpec(memory_space=pltpu.VMEM)
    others = tensor_size - 1
    dma = pltpu.SemaphoreType.DMA
    operands = (x, docs, cot) + weights
    small_shape = (8, width)
    shard = (batches, rows, width)
    shapes = (
        pltpu.VMEM(shard, BF16),
        pltpu.VMEM(shard, F32),
        pltpu.VMEM((3 * width, local), BF16),
        pltpu.VMEM(wout.shape, BF16),
        pltpu.VMEM(wup.shape, BF16),
        pltpu.VMEM(wdown.shape, BF16),
        pltpu.VMEM(small_shape, F32),
    )
    plan = sum_plan(width, local, units)
    scratch = [
        pltpu.VMEM(wqkv.shape, BF16),
        pltpu.VMEM(wout.shape, BF16),
        pltpu.VMEM(wup.shape, BF16),
        pltpu.VMEM(wdown.shape, BF16),
        pltpu.VMEM((4, batches, slot, width), BF16),
        pltpu.VMEM((4, batches, slot, width), BF16),
        pltpu.VMEM((4, batches, others, rows, width), BF16),
        pltpu.VMEM((batches, slot, width), F32),
        pltpu.VMEM((batches, slot, 3 * local), BF16),
        pltpu.VMEM((batches, heads, slot, slot), F32),
        pltpu.VMEM((batches, slot, local), BF16),
        pltpu.VMEM(shard, F32),
        pltpu.VMEM(shard, F32),
        pltpu.VMEM(shard, F32),
        pltpu.VMEM((batches, rows, 1), F32),
        pltpu.VMEM((batches, slot, units), F32),
        pltpu.VMEM((batches, slot, units), BF16),
        pltpu.VMEM(shard, F32),
        pltpu.VMEM((batches, rows, 1), F32),
        pltpu.VMEM(shard, F32),
        pltpu.VMEM(shard, F32),
        pltpu.VMEM((batches, slot, units), BF16),
        pltpu.VMEM((batches, slot, 3 * local), BF16),
        pltpu.VMEM(shard, BF16),
        pltpu.VMEM(shard, BF16),
        pltpu.VMEM(shard, BF16),
        pltpu.VMEM(small_shape, F32),
        pltpu.VMEM((3 * width, local), BF16),
        pltpu.VMEM(wout.shape, BF16),
        pltpu.VMEM(wup.shape, BF16),
        pltpu.VMEM(wdown.shape, BF16),
        dma((4, batches, others)),
        dma((4, batches, others)),
        dma((4, batches, others)),
        dma((4, batches, others)),
        dma((batches,)),
        dma((batches,)),
        dma((batches,)),
        dma((batches,)),
        dma((len(plan), 14)),
        dma((len(plan), 14)),
        dma((len(SPREAD), 3)),
        dma((len(SPREAD), 3)),
        dma((4,)),
    ]
    for axis in SPREAD:
        size = tensor_size if axis == "tensor" else AXES[axis][1]
        scratch.append(pltpu.VMEM((size,) + small_shape, F32))
    for _, _, rows_all, columns, order in plan:
        scratch.extend(pltpu.VMEM(shape, BF16) for shape in sum_buffers(rows_all, columns, order))
    in_specs = [vmem] * len(operands)
    for index in (3, 5, 9, 11):
        in_specs[index] = pl.BlockSpec(memory_space=pl.ANY)
    return pl.pallas_call(
        functools.partial(layer_kernel, tensor_size, plan),
        out_shape=shapes,
        in_specs=in_specs,
        out_specs=[vmem] * len(shapes),
        scratch_shapes=scratch,
        compiler_params=pltpu.CompilerParams(
            collective_id=0, has_side_effects=True, vmem_limit_bytes=VMEM_BYTES
        ),
        name="layer",
    )(*operands)


def unpack_kernel(count, *refs):
    sums, rows_ref, grad_ref, small_ref = refs[:count], *refs[count : count + 3]
    refs = refs[count + 3 :]
    targets, rows_out, grad_out, bqv_out, vectors = (
        refs[:count], refs[count], refs[count + 1], refs[count + 2], refs[count + 3 : count + 10]
    )
    wides, sem = refs[count + 10 : count + 10 + count], refs[-1]
    copies = []
    for source, target, wide in zip(sums, targets, wides):
        for at in range(0, source.shape[0], 2 * STEP):
            rows_at = pl.ds(at, min(2 * STEP, source.shape[0] - at))
            wide[rows_at, :] = source[rows_at, :].astype(F32)
            copy = pltpu.make_async_copy(wide.at[rows_at], target.at[rows_at], sem.at[len(copies)])
            copy.start()
            copies.append(copy)
    rows_out[...] = rows_ref[...]
    grad_out[...] = grad_ref[...]
    for index, vector in enumerate(vectors):
        vector[...] = small_ref[index : index + 1, :]
    half = bqv_out.shape[-1]
    for index in range(2):
        bqv_out[0, index : index + 1, :] = small_ref[7:8, pl.ds(index * half, half)]
    for copy in copies:
        copy.wait()


def unpack(sums, rows, grad, small, local):
    vmem = pl.BlockSpec(memory_space=pltpu.VMEM)
    count = len(sums)
    vector = jax.ShapeDtypeStruct((1, small.shape[1]), F32)
    wide = [jax.ShapeDtypeStruct(part.shape, F32) for part in sums]
    shapes = wide + [
        jax.ShapeDtypeStruct(rows.shape, rows.dtype),
        jax.ShapeDtypeStruct(grad.shape, grad.dtype),
        jax.ShapeDtypeStruct((1, 2, local), F32),
    ] + [vector] * 7
    pieces = sum(-(-part.shape[0] // (2 * STEP)) for part in sums)
    return pl.pallas_call(
        functools.partial(unpack_kernel, count),
        out_shape=shapes,
        in_specs=[vmem] * (count + 3),
        out_specs=[pl.BlockSpec(memory_space=pl.ANY)] * count + [vmem] * 10,
        scratch_shapes=[pltpu.VMEM(part.shape, F32) for part in sums]
        + [pltpu.SemaphoreType.DMA((pieces,))],
        compiler_params=pltpu.CompilerParams(vmem_limit_bytes=UNPACK_BYTES),
        name="unpack",
    )(*sums, rows, grad, small)


def shards(
    inputs, doc_ids, cotangent, w_qkv, b_qv, w_out, b_out, gain1, shift1,
    w_up, b_up, w_down, b_down, gain2, shift2,
):
    tensor_size = lax.axis_size("tensor")
    width = inputs.shape[2]
    local = w_out.shape[1]
    weights = (
        jnp.transpose(w_qkv[0], (1, 0, 2)), b_qv, w_out[0], b_out, gain1, shift1,
        w_up[0], b_up, w_down[0], b_down, gain2, shift2,
    )
    outputs, input_grads, gqkv, gout, gup, gdown, small = run_layer(
        inputs, doc_ids, cotangent, weights, tensor_size
    )
    sums = (gqkv, gout, gup, gdown)
    gqkv, gout, gup, gdown, outputs, input_grads, gbqv, *vectors = unpack(
        sums, outputs, input_grads, small, local
    )
    return (
        outputs[None],
        input_grads[None],
        jnp.transpose(gqkv.reshape(3, width, local), (1, 0, 2))[None],
        gbqv,
        gout[None],
        vectors[3],
        vectors[4],
        vectors[5],
        gup[None],
        vectors[6],
        gdown[None],
        vectors[0],
        vectors[1],
        vectors[2],
    )


def solution(mesh):
    rows = P(None, ("dp", "tensor"), None)
    banked = P("section", None, ("dp", "tensor"), None)
    vector = P("section", None)
    return jax.shard_map(
        shards,
        mesh=mesh,
        in_specs=(
            rows,
            P(None, "dp"),
            rows,
            P("section", None, None, "tensor"),
            P("section", None, "tensor"),
            P("section", "tensor", None),
            vector,
            vector,
            vector,
            P("section", None, "tensor"),
            P("section", "tensor"),
            P("section", "tensor", None),
            vector,
            vector,
            vector,
        ),
        out_specs=(
            banked,
            banked,
            P("section", None, None, "tensor"),
            P("section", None, "tensor"),
            P("section", "tensor", None),
            vector,
            vector,
            vector,
            P("section", None, "tensor"),
            P("section", "tensor"),
            P("section", "tensor", None),
            vector,
            vector,
            vector,
        ),
        check_vma=False,
    )
```

```python
import functools
import math

import jax
import jax.numpy as jnp
from jax import lax
from jax.experimental import pallas as pl
from jax.experimental.pallas import tpu as pltpu
from jax.sharding import PartitionSpec as P

HEAD_DIM = 64
MESH = pl.DeviceIdType.MESH
F32 = jnp.float32
BF16 = jnp.bfloat16
STEP = 256
SPREAD = ("tensor", "core", "y", "x")
VMEM_BYTES = 52 * 1024 * 1024
UNPACK_BYTES = 40 * 1024 * 1024
AFTER_FIRST = ((0,), (1, 2))
AFTER_ATTENTION = ((3,), ())
AFTER_GRADS = (0, 1, 2)
AFTER_LAST = ((3, 5, 6), ())
TAIL = (4, 0, 1, 2, 3, 5, 6, 0, 4, 5, 1, 6, 2, 0, 4, 3, 5, 1, 0, 6, 4, 5, 2, 3, 1, 4, 5, 2, 0, 6, 3, 0, 1, 4, 2, 5, 1, 6, 2, 3, 5, 4, 6, 3, 4, 6)
TAIL_ONE = (0, 1, 2, 3, 4, 5, 6) * 8
ROUNDS = 4
AXES = {"core": (1, 2), "x": (2, 2), "y": (4, 4)}
SIZES = {"core": 2, "x": 2, "y": 4, "ring": 4}
RS_SEM = {"core": 0, "x": 1, "y": 2, "ring": 2}
AG_SEM = {"core": 8, "x": 9, "y": 10, "ring": 10}
X_FIRST = ("core", "x", "ring")
Y_FIRST = ("core", "ring", "x")
X_FIRST_DIRECT = ("core", "x", "y")
Y_FIRST_DIRECT = ("core", "y", "x")


def sum_plan(width, local, units):
    joined = 3 * width
    return (
        ("down", 0, units // 2, width, X_FIRST),
        ("down", units // 2, units // 2, width, Y_FIRST),
        ("up", 0, width // 2, units, Y_FIRST),
        ("up", width // 2, width // 2, units, Y_FIRST),
        ("out", 0, local, width, X_FIRST),
        ("qkv", 0, joined // 2, local, X_FIRST),
        ("qkv", joined // 2, joined // 2, local, Y_FIRST),
    )


def sum_buffers(rows, columns, order):
    shapes = []
    for axis in order:
        rows //= SIZES[axis]
        if axis == "ring":
            shapes.append((8, rows, columns // 2))
        elif axis == "y":
            shapes.append((3, rows, columns))
        else:
            shapes.append((rows, columns))
        shapes.append((rows, columns))
    return shapes


def dot(left, right):
    return lax.dot_general(left, right, (((1,), (0,)), ((), ())), preferred_element_type=F32)


def dot_last(left, right):
    return lax.dot_general(left, right, (((1,), (1,)), ((), ())), preferred_element_type=F32)


def dot_rows(left, right):
    return lax.dot_general(left, right, (((0,), (0,)), ((), ())), preferred_element_type=F32)


def norm(hidden, gain, shift):
    centred = hidden - jnp.mean(hidden, axis=-1, keepdims=True)
    inv_std = lax.rsqrt(jnp.mean(centred * centred, axis=-1, keepdims=True) + 1e-05)
    normed = centred * inv_std
    return normed * gain + shift, normed, inv_std


def norm_back(grad_out, normed, inv_std, gain):
    scaled = grad_out * gain
    return inv_std * (
        scaled
        - jnp.mean(scaled, axis=-1, keepdims=True)
        - normed * jnp.mean(scaled * normed, axis=-1, keepdims=True)
    )


def column_sum(block):
    return jnp.sum(block, axis=0, keepdims=True)


def layer_kernel(tensor_size, plan, *refs):
    (
        x_ref, doc_ref, cot_ref,
        wqkv_hbm, bqv_ref, wout_hbm, bout_ref, gain1_ref, shift1_ref,
        wup_hbm, bup_ref, wdown_hbm, bdown_ref, gain2_ref, shift2_ref,
        out_ref, dx_ref, gqkv_ref, gout_ref, gup_ref, gdown_ref, small_ref,
        wqkv_ref, wfull, wup_ref, wdown_ref,
        gath, rs_send, rs_recv, rs_own,
        qkv, probs, ctx, entry, y1, n1, r1, slope, act, n2, r2, dh2, dh, du, dqkv,
        sent_up, back_in, sent_back, small_acc,
        ctx_all, dctx_sent, dctx_all,
        pqkv, pout, pup, pdown,
        ag_ssem, ag_rsem, rs_ssem, rs_rsem, up_ssem, up_rsem, back_ssem, back_rsem,
        wide_ssem, wide_rsem, ctx_ssem, ctx_rsem, dctx_ssem, dctx_rsem,
        sum_ssem, sum_rsem, small_ssem, small_rsem, load_sem, calm_sem,
        *more,
    ) = refs
    spread_refs, sum_refs = more[: len(SPREAD)], more[len(SPREAD) :]
    grads = {"qkv": pqkv, "out": pout, "up": pup, "down": pdown}
    totals = {"qkv": gqkv_ref, "out": gout_ref, "up": gup_ref, "down": gdown_ref}
    batches, rows, width = x_ref.shape
    slot = rows * tensor_size
    local = wfull.shape[1]
    units = wup_ref.shape[1]
    pairs = local // (2 * HEAD_DIM)
    sec = lax.axis_index("section")
    me = lax.axis_index("tensor")
    dp = lax.axis_index("dp")
    other = 1 - sec
    scale = HEAD_DIM ** (-0.5)
    loads = [
        pltpu.make_async_copy(source, target, load_sem.at[index])
        for index, (source, target) in enumerate(
            (
                (wqkv_hbm, wqkv_ref), (wout_hbm, wfull.at[me]),
                (wup_hbm, wup_ref), (wdown_hbm, wdown_ref),
            )
        )
    ]
    for load in loads:
        load.start()

    barrier = pltpu.get_barrier_semaphore()
    for k in range(1, tensor_size):
        pl.semaphore_signal(
            barrier, inc=1, device_id={"tensor": lax.rem(me + k, tensor_size)}, device_id_type=MESH
        )
    pl.semaphore_signal(barrier, inc=1, device_id={"section": other}, device_id_type=MESH)
    greeted = tensor_size
    for axis, (stride, size) in AXES.items():
        for k in range(1, size):
            index = lax.rem(dp // stride, size)
            near = dp + (lax.rem(index + k, size) - index) * stride
            pl.semaphore_signal(barrier, inc=1, device_id={"dp": near}, device_id_type=MESH)
            greeted += 1
    pl.semaphore_wait(barrier, greeted)

    def band(index):
        return pl.ds(pl.multiple_of(index * rows, rows), rows)

    mine = band(me)

    def gather_copy(e, m, k):
        return pltpu.make_async_remote_copy(
            src_ref=gath.at[e, m, mine],
            dst_ref=gath.at[e, m, mine],
            send_sem=ag_ssem.at[e, m, k - 1],
            recv_sem=ag_rsem.at[e, m, k - 1],
            device_id={"tensor": lax.rem(me + k, tensor_size)},
            device_id_type=MESH,
        )

    def gather_start(e, m):
        for k in range(1, tensor_size):
            gather_copy(e, m, k).start()

    def gather_wait(e, m):
        for k in range(1, tensor_size):
            source = band(lax.rem(me + tensor_size - k, tensor_size))
            pltpu.make_async_remote_copy(
                src_ref=gath.at[e, m, source],
                dst_ref=gath.at[e, m, source],
                send_sem=ag_ssem.at[e, m, k - 1],
                recv_sem=ag_rsem.at[e, m, k - 1],
                device_id={"tensor": lax.rem(me + k, tensor_size)},
                device_id_type=MESH,
            ).wait_recv()

    def scatter_copy(e, m, k):
        target = lax.rem(me + k, tensor_size)
        return pltpu.make_async_remote_copy(
            src_ref=rs_send.at[e, m, band(target)],
            dst_ref=rs_recv.at[e, m, k - 1],
            send_sem=rs_ssem.at[e, m, k - 1],
            recv_sem=rs_rsem.at[e, m, k - 1],
            device_id={"tensor": target},
            device_id_type=MESH,
        )

    def scatter_start(e, m):
        for k in range(1, tensor_size):
            scatter_copy(e, m, k).start()

    def scatter_wait(e, m):
        total = rs_own[m, mine, :]
        for k in range(1, tensor_size):
            scatter_copy(e, m, k).wait_recv()
        for k in range(1, tensor_size):
            total = total + rs_recv[e, m, k - 1].astype(F32)
        return total

    def share_copy(whole, ssem, rsem, k, source):
        at = whole.at[source]
        return pltpu.make_async_remote_copy(
            src_ref=at,
            dst_ref=at,
            send_sem=ssem.at[k - 1],
            recv_sem=rsem.at[k - 1],
            device_id={"tensor": lax.rem(me + k, tensor_size)},
            device_id_type=MESH,
        )

    def share_start(whole, ssem, rsem):
        for k in range(1, tensor_size):
            share_copy(whole, ssem, rsem, k, me).start()

    def share_wait(whole, ssem, rsem):
        for k in range(1, tensor_size):
            source = lax.rem(me + tensor_size - k, tensor_size)
            share_copy(whole, ssem, rsem, k, source).wait_recv()

    def share_drain(whole, ssem, rsem):
        for k in range(1, tensor_size):
            share_copy(whole, ssem, rsem, k, me).wait_send()

    wide = (wfull, wide_ssem, wide_rsem)

    def contexts(m):
        return ctx_all.at[m], ctx_ssem.at[m], ctx_rsem.at[m]

    def dctx_copy(m, k):
        target = lax.rem(me + k, tensor_size)
        return pltpu.make_async_remote_copy(
            src_ref=dctx_sent.at[m, target],
            dst_ref=dctx_all.at[m, mine],
            send_sem=dctx_ssem.at[m, k - 1],
            recv_sem=dctx_rsem.at[m, k - 1],
            device_id={"tensor": target},
            device_id_type=MESH,
        )

    def dctx_wait(m):
        for k in range(1, tensor_size):
            source = lax.rem(me + tensor_size - k, tensor_size)
            pltpu.make_async_remote_copy(
                src_ref=dctx_sent.at[m, source],
                dst_ref=dctx_all.at[m, band(source)],
                send_sem=dctx_ssem.at[m, k - 1],
                recv_sem=dctx_rsem.at[m, k - 1],
                device_id={"tensor": source},
                device_id_type=MESH,
            ).wait_recv()

    def put_part(e, m, columns, part):
        rs_own[m, :, columns] = part
        rs_send[e, m, :, columns] = part.astype(BF16)

    def up_copy(m):
        return pltpu.make_async_remote_copy(
            src_ref=sent_up.at[m],
            dst_ref=gath.at[0, m, mine],
            send_sem=up_ssem.at[m],
            recv_sem=up_rsem.at[m],
            device_id={"section": other},
            device_id_type=MESH,
        )

    def back_copy(m):
        return pltpu.make_async_remote_copy(
            src_ref=sent_back.at[m],
            dst_ref=back_in.at[m],
            send_sem=back_ssem.at[m],
            recv_sem=back_rsem.at[m],
            device_id={"section": other},
            device_id_type=MESH,
        )

    def each_batch(body, between=None):
        def step(m, carry):
            body(m)
            return carry

        if between is None:
            lax.fori_loop(0, batches, step, 0)
        else:
            for m in range(batches):
                body(m)
                between(m)

    def chunks(total):
        return [pl.ds(c, min(STEP, total - c)) for c in range(0, total, STEP)]

    def head_mask():
        return lax.broadcasted_iota(jnp.int32, (slot, 2 * HEAD_DIM), 1) < HEAD_DIM

    def pick(first, block):
        low_half = head_mask()
        keep = low_half if first else jnp.logical_not(low_half)
        return jnp.where(keep, block, jnp.zeros_like(block))


    place = {axis: lax.rem(dp // stride, size) for axis, (stride, size) in AXES.items()}

    def dp_peer(axis, k):
        stride, size = AXES[axis]
        return {"dp": dp + (lax.rem(place[axis] + k, size) - place[axis]) * stride}

    def sum_events(c, send):
        name, first, rows_all, columns, order = plan[c]
        grad, total = grads[name], totals[name]
        buffers = sum_refs[6 * c : 6 * c + 6]
        half = columns // 2
        low, high = pl.ds(0, half), pl.ds(half, half)
        sources, starts, blocks = [(grad, first)], [first], [rows_all]
        for step, axis in enumerate(order):
            blocks.append(blocks[-1] // SIZES[axis])
            index = place["y" if axis == "ring" else axis]
            starts.append(starts[-1] + index * blocks[-1])
            sources.append((buffers[2 * step + 1], 0))

        def lines(start, count):
            return pl.ds(pl.multiple_of(start, count), count)

        def remote(source, target, sem, axis, k):
            return pltpu.make_async_remote_copy(
                src_ref=source,
                dst_ref=target,
                send_sem=sum_ssem.at[c, sem],
                recv_sem=sum_rsem.at[c, sem],
                device_id=dp_peer(axis, k),
                device_id_type=MESH,
            )

        def spot(step):
            return place["y" if order[step] == "ring" else order[step]]

        def block_at(step, index):
            ref, base = sources[step]
            return ref, lines(base + index * blocks[step + 1], blocks[step + 1])

        def add(step, columns_at, parts):
            ref, at = block_at(step, spot(step))
            value = ref[at, columns_at].astype(F32)
            for part in parts:
                value = value + part.astype(F32)
            return value.astype(BF16)

        def finish(step, pieces):
            for columns_at, value in pieces:
                if step == 2:
                    total[lines(starts[3], blocks[3]), columns_at] = value
                else:
                    buffers[2 * step + 1][:, columns_at] = value

        def pair_scatter(step):
            axis = order[step]
            landing = buffers[2 * step]

            def copy():
                ref, at = block_at(step, 1 - place[axis])
                return remote(ref.at[at], landing, RS_SEM[axis], axis, 1)

            def begin():
                send(copy)

            def end():
                copy().wait_recv()
                pieces = []
                for columns_at in (low, high):
                    pieces.append((columns_at, add(step, columns_at, [landing[:, columns_at]])))
                finish(step, pieces)

            return [begin, end]

        def direct_scatter(step):
            landing = buffers[2 * step]

            def copy(k):
                ref, at = block_at(step, lax.rem(place["y"] + k, 4))
                return remote(ref.at[at], landing.at[k - 1], RS_SEM["y"] + k - 1, "y", k)

            def begin():
                for k in range(1, 4):
                    send(functools.partial(copy, k))

            def end():
                for k in range(1, 4):
                    copy(k).wait_recv()
                pieces = []
                for columns_at in (low, high):
                    parts = [landing[k, :, columns_at] for k in range(3)]
                    pieces.append((columns_at, add(step, columns_at, parts)))
                finish(step, pieces)

            return [begin, end]

        def ring_scatter(step):
            landing = buffers[2 * step]
            here = place["y"]

            def at(k, columns_at):
                ref, lines_at = block_at(step, lax.rem(here + k, 4))
                return ref.at[lines_at, columns_at]

            def copy(number):
                source, k = (
                    (lambda: at(2, high), 1),
                    (lambda: at(1, low), 1),
                    (lambda: at(2, low), 3),
                    (lambda: at(3, high), 3),
                    (lambda: landing.at[6], 1),
                    (lambda: landing.at[7], 3),
                )[number]
                return remote(source(), landing.at[number], RS_SEM["y"] + number, "y", k)

            def begin():
                for number in range(4):
                    send(functools.partial(copy, number))

            def relay():
                for number, k, columns_at, out in ((0, 1, high, 4), (2, 3, low, 5)):
                    copy(number).wait_recv()
                    value = at(k, columns_at)[...].astype(F32) + landing[number].astype(F32)
                    landing[out + 2] = value.astype(BF16)
                    send(functools.partial(copy, out))

            def end():
                for number in (1, 3, 4, 5):
                    copy(number).wait_recv()
                finish(
                    step,
                    [
                        (low, add(step, low, [landing[1], landing[5]])),
                        (high, add(step, high, [landing[3], landing[4]])),
                    ],
                )

            return [begin, relay, end]

        def region(step, index, columns_at=None):
            at = lines(starts[step] + index * blocks[step + 1], blocks[step + 1])
            return total.at[at] if columns_at is None else total.at[at, columns_at]

        def pair_gather(step):
            axis = order[step]

            def copy(index):
                return remote(region(step, index), region(step, index), AG_SEM[axis], axis, 1)

            return [
                lambda: send(lambda: copy(place[axis])),
                lambda: copy(1 - place[axis]).wait_recv(),
            ]

        def direct_gather(step):
            def copy(k, back):
                part = region(step, lax.rem(place["y"] + 4 - back, 4))
                return remote(part, part, AG_SEM["y"] + k - 1, "y", k)

            def begin():
                for k in range(1, 4):
                    send(functools.partial(copy, k, 0))

            def end():
                for k in range(1, 4):
                    copy(k, k).wait_recv()

            return [begin, end]

        def ring_gather(step):
            def copy(number, back):
                index = lax.rem(place["y"] + 4 - back, 4)
                columns_at = (None, None, low, high)[number]
                part = region(step, index, columns_at)
                return remote(part, part, AG_SEM["y"] + number, "y", (1, 3, 1, 3)[number])

            def begin():
                send(functools.partial(copy, 0, 0))
                send(functools.partial(copy, 1, 0))

            def relay():
                copy(0, 1).wait_recv()
                send(functools.partial(copy, 2, 1))
                copy(1, 3).wait_recv()
                send(functools.partial(copy, 3, 3))

            def end():
                copy(2, 2).wait_recv()
                copy(3, 2).wait_recv()

            return [begin, relay, end]

        def join(stages):
            events = [stages[0][0]]
            for stage, later in zip(stages, stages[1:] + [None]):
                events.extend(stage[1:-1])
                if later is None:
                    events.append(stage[-1])
                else:
                    events.append(lambda end=stage[-1], begin=later[0]: (end(), begin()))
            return events

        forms = {
            "core": (pair_scatter, pair_gather),
            "x": (pair_scatter, pair_gather),
            "y": (direct_scatter, direct_gather),
            "ring": (ring_scatter, ring_gather),
        }
        scatters = [forms[axis][0](step) for step, axis in enumerate(order)]
        gathers = [forms[axis][1](step) for step, axis in enumerate(order)]
        return join(scatters + gathers[::-1])

    sends, events = ([], []), ([], [])
    for section in range(2):

        def send(make, section=section):
            make().start()
            sends[section].append(make)

        events[section].extend(sum_events(c, send) for c in range(len(plan)))

    def advance(section, *which):
        @pl.when(sec == section)
        def _():
            for c in which:
                if events[section][c]:
                    events[section][c].pop(0)()

    def spread_copy(step, k, source):
        axis = SPREAD[step]
        size = tensor_size if axis == "tensor" else AXES[axis][1]
        at = spread_refs[step].at[source]
        return pltpu.make_async_remote_copy(
            src_ref=at,
            dst_ref=at,
            send_sem=small_ssem.at[step, k - 1],
            recv_sem=small_rsem.at[step, k - 1],
            device_id={"tensor": lax.rem(me + k, size)} if axis == "tensor" else dp_peer(axis, k),
            device_id_type=MESH,
        )

    def spread_place(step):
        axis = SPREAD[step]
        return (me, tensor_size) if axis == "tensor" else (place[axis], AXES[axis][1])

    def spread_start(step, value):
        index, size = spread_place(step)
        spread_refs[step][index] = value
        for k in range(1, size):
            spread_copy(step, k, index).start()

    def spread_finish(step):
        index, size = spread_place(step)
        for k in range(1, size):
            spread_copy(step, k, lax.rem(index + size - k, size)).wait_recv()
        value = spread_refs[step][0]
        for other_index in range(1, size):
            value = value + spread_refs[step][other_index]
        return value

    small_acc[...] = jnp.zeros_like(small_acc)

    @pl.when(sec == 0)
    def _():
        for m in range(batches):
            gath[0, m, mine, :] = x_ref[m]

    loads[1].wait()

    @pl.when(sec == 1)
    def _():
        share_start(*wide)

    for m in range(batches):
        @pl.when(sec == 1)
        def _():
            up_copy(m).wait_recv()

        gather_start(0, m)
        if m < batches - 1:
            for k in range(1, tensor_size):
                gather_copy(0, m, k).wait_send()

    loads[0].wait()

    @pl.when(sec == 1)
    def _():
        share_wait(*wide)


    def attention(m):
        entry[m] = gath[0, m, mine, :].astype(F32)
        gather_wait(0, m)
        for third in range(3):
            part = dot(gath[0, m], wqkv_ref[third])
            if third != 1:
                part = part + bqv_ref[0, third // 2 : third // 2 + 1, :]
            qkv[m, :, pl.ds(third * local, local)] = part.astype(BF16)
        across = jnp.broadcast_to(doc_ref[pl.ds(m, 1), :].astype(F32), (slot, slot))
        down = jnp.transpose(across)
        row_id = lax.broadcasted_iota(jnp.int32, (slot, slot), 0)
        col_id = lax.broadcasted_iota(jnp.int32, (slot, slot), 1)
        allowed = ((across == down) & (across >= 0)) | (row_id == col_id)
        low_half = head_mask()
        for pair in range(pairs):
            at = pair * 2 * HEAD_DIM
            queries = qkv[m, :, pl.ds(at, 2 * HEAD_DIM)]
            key_heads = qkv[m, :, pl.ds(local + at, 2 * HEAD_DIM)]
            values = qkv[m, :, pl.ds(2 * local + at, 2 * HEAD_DIM)]
            halves = []
            for half in range(2):
                raw = dot_last(pick(half == 0, queries), key_heads) * scale
                scores = jnp.where(allowed, raw, -1e30)
                peak = jnp.max(scores, axis=-1, keepdims=True)
                exps = jnp.exp(scores - peak)
                soft = exps / jnp.sum(exps, axis=-1, keepdims=True)
                probs[m, pair * 2 + half] = soft
                halves.append(dot(soft.astype(BF16), values))
            ctx[m, :, pl.ds(at, 2 * HEAD_DIM)] = jnp.where(low_half, halves[0], halves[1]).astype(BF16)
        @pl.when(sec == 0)
        def _():
            for cols in chunks(width):
                put_part(0, m, cols, dot(ctx[m], wfull[me, :, cols]))
            scatter_start(0, m)

        @pl.when(sec == 1)
        def _():
            ctx_all[m, me] = ctx[m]
            share_start(*contexts(m))

    each_batch(attention)

    def first_norm(m):
        @pl.when(sec == 0)
        def _():
            hidden = entry[m] + scatter_wait(0, m) + bout_ref[...]
            out, normed, inv_std = norm(hidden, gain1_ref[...], shift1_ref[...])
            y1[m], n1[m], r1[m] = out, normed, inv_std
            gath[1, m, mine, :] = out.astype(BF16)
            gather_start(1, m)

    each_batch(first_norm)

    def whole_norm(m):
        share_wait(*contexts(m))
        for cols in chunks(width):
            part = gath[0, m, :, cols].astype(F32) + bout_ref[:, cols]
            for source in range(tensor_size):
                part = part + dot(ctx_all[m, source], wfull[source, :, cols])
            rs_own[m, :, cols] = part
        for at in range(0, slot, rows):
            lines_at = pl.ds(at, rows)
            out, _, _ = norm(rs_own[m, lines_at, :], gain1_ref[...], shift1_ref[...])
            gath[1, m, lines_at, :] = out.astype(BF16)
        out, normed, inv_std = norm(rs_own[m, mine, :], gain1_ref[...], shift1_ref[...])
        y1[m], n1[m], r1[m] = out, normed, inv_std

    for load in loads[2:]:
        load.wait()

    def feed_forward(m):
        @pl.when(sec == 0)
        def _():
            gather_wait(1, m)

        @pl.when(sec == 1)
        def _():
            whole_norm(m)

        for cols in chunks(units):
            pre = dot(gath[1, m], wup_ref[:, cols]) + bup_ref[:, cols]
            cdf = 0.5 * (1.0 + lax.erf(pre * (1.0 / math.sqrt(2.0))))
            slope[m, :, cols] = cdf + pre * jnp.exp(-0.5 * pre * pre) * (
                1.0 / math.sqrt(2.0 * math.pi)
            )
            act[m, :, cols] = (pre * cdf).astype(BF16)
        for cols in chunks(width):
            put_part(1, m, cols, dot(act[m], wdown_ref[:, cols]))
        scatter_start(1, m)

    each_batch(feed_forward)

    def back_entry(m):
        @pl.when(sec == 1)
        def _():
            back_in[m] = cot_ref[m]

        @pl.when(sec == 0)
        def _():
            back_copy(m).wait_recv()

        grad_out = back_in[m].astype(F32)
        grad = norm_back(grad_out, n2[m], r2[m], gain2_ref[...])
        small_acc[0:1, :] += column_sum(grad)
        small_acc[1:2, :] += column_sum(grad_out * n2[m])
        small_acc[2:3, :] += column_sum(grad_out)
        dh2[m] = grad
        gath[2, m, mine, :] = grad.astype(BF16)
        gather_start(2, m)

    def second_norm(m):
        hidden = y1[m] + scatter_wait(1, m) + bdown_ref[...]
        out, normed, inv_std = norm(hidden, gain2_ref[...], shift2_ref[...])
        n2[m], r2[m] = normed, inv_std
        rounded = out.astype(BF16)
        out_ref[m] = rounded

        @pl.when(sec == 0)
        def _():
            sent_up[m] = rounded
            up_copy(m).start()

        @pl.when(sec == 1)
        def _():
            back_entry(m)

    each_batch(second_norm)

    @pl.when(sec == 0)
    def _():
        for k in range(1, tensor_size):
            target = {"tensor": lax.rem(me + k, tensor_size)}
            pl.semaphore_signal(calm_sem, inc=1, device_id=target, device_id_type=MESH)
        pl.semaphore_wait(calm_sem, tensor_size - 1)
        share_start(*wide)

    @pl.when(sec == 0)
    def _():
        each_batch(back_entry)

    def feed_back(m):
        gather_wait(2, m)
        for cols in chunks(units):
            grad = (dot_last(gath[2, m], wdown_ref[cols, :]) * slope[m, :, cols]).astype(BF16)
            du[m, :, cols] = grad
            small_acc[6:7, cols] += column_sum(grad.astype(F32))
        for cols in chunks(width):
            put_part(2, m, cols, dot_last(du[m], wup_ref[cols, :]))
        scatter_start(2, m)

    each_batch(feed_back)

    def weight_grad(left, right, target, base=0):
        total = batches * slot
        rhs = right[...].reshape(total, right.shape[-1])
        for rows_at in chunks(left.shape[-1]):
            lhs = left[:, :, rows_at].reshape(total, rows_at.size)
            target[pl.ds(base + rows_at.start, rows_at.size), :] = dot_rows(lhs, rhs).astype(BF16)

    weight_grad(act, gath.at[2], pdown)
    advance(0, 0, 1)
    weight_grad(gath.at[1], du, pup)
    advance(0, 2, 3)

    @pl.when(sec == 0)
    def _():
        share_wait(*wide)

    def first_back(m):
        grad_out = dh2[m] + scatter_wait(2, m)
        grad = norm_back(grad_out, n1[m], r1[m], gain1_ref[...])
        small_acc[3:4, :] += column_sum(grad)
        small_acc[4:5, :] += column_sum(grad_out * n1[m])
        small_acc[5:6, :] += column_sum(grad_out)
        dh[m] = grad
        rounded = grad.astype(BF16)
        gath[3, m, mine, :] = rounded
        for target in range(tensor_size):
            dctx_sent[m, target] = dot_last(rounded, wfull[target]).astype(BF16)
        dctx_all[m, mine, :] = dctx_sent[m, me]
        for k in range(1, tensor_size):
            dctx_copy(m, k).start()
        gather_start(3, m)

    each_batch(first_back, lambda m: advance(0, *AFTER_FIRST[m]))

    def attention_back(m):
        dctx_wait(m)
        low_half = head_mask()
        for pair in range(pairs):
            at = pair * 2 * HEAD_DIM
            dctx = dctx_all[m, :, pl.ds(at, 2 * HEAD_DIM)]
            queries = qkv[m, :, pl.ds(at, 2 * HEAD_DIM)]
            key_heads = qkv[m, :, pl.ds(local + at, 2 * HEAD_DIM)]
            values = qkv[m, :, pl.ds(2 * local + at, 2 * HEAD_DIM)]
            dq, dk, dv = [], [], []
            for half in range(2):
                soft = probs[m, pair * 2 + half]
                dv.append(dot_rows(soft.astype(BF16), dctx))
                dprob = dot_last(pick(half == 0, dctx), values)
                dscore = soft * (dprob - jnp.sum(soft * dprob, axis=-1, keepdims=True))
                dscore = dscore.astype(BF16)
                dq.append(dot(dscore, key_heads) * scale)
                dk.append(dot_rows(dscore, queries) * scale)
            for place, (first, second) in enumerate((dq, dk, dv)):
                cols = pl.ds(place * local + at, 2 * HEAD_DIM)
                grad = jnp.where(low_half, first, second).astype(BF16)
                dqkv[m, :, cols] = grad
                if place != 1:
                    to = at if place == 0 else local + at
                    small_acc[7:8, pl.ds(to, 2 * HEAD_DIM)] += column_sum(grad.astype(F32))
        for cols in chunks(width):
            part = dot_last(dqkv[m, :, pl.ds(0, local)], wqkv_ref[0, cols, :])
            for third in range(1, 3):
                part = part + dot_last(
                    dqkv[m, :, pl.ds(third * local, local)], wqkv_ref[third, cols, :]
                )
            put_part(3, m, cols, part)
        scatter_start(3, m)

    each_batch(attention_back, lambda m: advance(0, *AFTER_ATTENTION[m]))

    def joined_grad():
        for third in range(3):
            weight_grad(
                gath.at[0], dqkv.at[:, :, pl.ds(third * local, local)], pqkv, base=third * width
            )

    pl.when(sec == 0)(joined_grad)
    advance(0, 5, 6)
    spread_start(0, small_acc[...])
    for m in range(batches):
        gather_wait(3, m)
    weight_grad(ctx, gath.at[3], pout)
    advance(0, 4, *AFTER_GRADS)

    def last_back(m):
        grad = dh[m] + scatter_wait(3, m)
        dx_ref[m] = grad

        @pl.when(sec == 1)
        def _():
            sent_back[m] = grad.astype(BF16)
            back_copy(m).start()

    each_batch(last_back, lambda m: advance(0, *AFTER_LAST[m]))

    pl.when(sec == 1)(joined_grad)
    advance(1, 0, 1, 2, 3, 4, 5, 6)
    small_row = lax.broadcasted_iota(jnp.int32, small_acc.shape, 0)
    spread_start(1, jnp.where(small_row < 6, spread_finish(0), small_acc[...]))
    small_step = 1
    for part in range(ROUNDS):
        at = len(TAIL) // ROUNDS
        advance(0, *TAIL[part * at : (part + 1) * at if part < ROUNDS - 1 else len(TAIL)])
        advance(1, *TAIL_ONE[part * 14 : part * 14 + 14])
        if small_step < len(SPREAD):
            value = spread_finish(small_step)
            small_step += 1
            if small_step < len(SPREAD):
                spread_start(small_step, value)
            else:
                small_ref[...] = value
    assert not any(events[0]) and not any(events[1])

    for make in sends[0]:
        make().wait_send()
    for step in range(len(SPREAD)):
        index, size = spread_place(step)
        for k in range(1, size):
            spread_copy(step, k, index).wait_send()

    def drain(m):
        for e in range(4):
            for k in range(1, tensor_size):
                if e:
                    scatter_copy(e, m, k).wait_send()
                if e > 1:
                    gather_copy(e, m, k).wait_send()
        for k in range(1, tensor_size):
            dctx_copy(m, k).wait_send()

        @pl.when(sec == 0)
        def _():
            up_copy(m).wait_send()
            for k in range(1, tensor_size):
                scatter_copy(0, m, k).wait_send()
                gather_copy(1, m, k).wait_send()

        @pl.when(sec == 1)
        def _():
            back_copy(m).wait_send()
            share_drain(*contexts(m))

    for k in range(1, tensor_size):
        gather_copy(0, batches - 1, k).wait_send()
    share_drain(*wide)
    each_batch(drain)


def run_layer(x, docs, cot, weights, tensor_size):
    batches, rows, width = x.shape
    slot = rows * tensor_size
    wqkv, bqv, wout, bout, gain1, shift1, wup, bup, wdown, bdown, gain2, shift2 = weights
    local = wout.shape[0]
    units = wup.shape[1]
    heads = local // HEAD_DIM
    vmem = pl.BlockSpec(memory_space=pltpu.VMEM)
    others = tensor_size - 1
    dma = pltpu.SemaphoreType.DMA
    operands = (x, docs, cot) + weights
    small_shape = (8, width)
    shard = (batches, rows, width)
    shapes = (
        pltpu.VMEM(shard, BF16),
        pltpu.VMEM(shard, F32),
        pltpu.VMEM((3 * width, local), BF16),
        pltpu.VMEM(wout.shape, BF16),
        pltpu.VMEM(wup.shape, BF16),
        pltpu.VMEM(wdown.shape, BF16),
        pltpu.VMEM(small_shape, F32),
    )
    plan = sum_plan(width, local, units)
    scratch = [
        pltpu.VMEM(wqkv.shape, BF16),
        pltpu.VMEM((tensor_size,) + wout.shape, BF16),
        pltpu.VMEM(wup.shape, BF16),
        pltpu.VMEM(wdown.shape, BF16),
        pltpu.VMEM((4, batches, slot, width), BF16),
        pltpu.VMEM((4, batches, slot, width), BF16),
        pltpu.VMEM((4, batches, others, rows, width), BF16),
        pltpu.VMEM((batches, slot, width), F32),
        pltpu.VMEM((batches, slot, 3 * local), BF16),
        pltpu.VMEM((batches, heads, slot, slot), F32),
        pltpu.VMEM((batches, slot, local), BF16),
        pltpu.VMEM(shard, F32),
        pltpu.VMEM(shard, F32),
        pltpu.VMEM(shard, F32),
        pltpu.VMEM((batches, rows, 1), F32),
        pltpu.VMEM((batches, slot, units), F32),
        pltpu.VMEM((batches, slot, units), BF16),
        pltpu.VMEM(shard, F32),
        pltpu.VMEM((batches, rows, 1), F32),
        pltpu.VMEM(shard, F32),
        pltpu.VMEM(shard, F32),
        pltpu.VMEM((batches, slot, units), BF16),
        pltpu.VMEM((batches, slot, 3 * local), BF16),
        pltpu.VMEM(shard, BF16),
        pltpu.VMEM(shard, BF16),
        pltpu.VMEM(shard, BF16),
        pltpu.VMEM(small_shape, F32),
        pltpu.VMEM((batches, tensor_size, slot, local), BF16),
        pltpu.VMEM((batches, tensor_size, rows, local), BF16),
        pltpu.VMEM((batches, slot, local), BF16),
        pltpu.VMEM((3 * width, local), BF16),
        pltpu.VMEM(wout.shape, BF16),
        pltpu.VMEM(wup.shape, BF16),
        pltpu.VMEM(wdown.shape, BF16),
        dma((4, batches, others)),
        dma((4, batches, others)),
        dma((4, batches, others)),
        dma((4, batches, others)),
        dma((batches,)),
        dma((batches,)),
        dma((batches,)),
        dma((batches,)),
        dma((others,)),
        dma((others,)),
        dma((batches, others)),
        dma((batches, others)),
        dma((batches, others)),
        dma((batches, others)),
        dma((len(plan), 14)),
        dma((len(plan), 14)),
        dma((len(SPREAD), 3)),
        dma((len(SPREAD), 3)),
        dma((4,)),
        pltpu.SemaphoreType.REGULAR,
    ]
    for axis in SPREAD:
        size = tensor_size if axis == "tensor" else AXES[axis][1]
        scratch.append(pltpu.VMEM((size,) + small_shape, F32))
    for _, _, rows_all, columns, order in plan:
        scratch.extend(pltpu.VMEM(shape, BF16) for shape in sum_buffers(rows_all, columns, order))
    in_specs = [vmem] * len(operands)
    for index in (3, 5, 9, 11):
        in_specs[index] = pl.BlockSpec(memory_space=pl.ANY)
    return pl.pallas_call(
        functools.partial(layer_kernel, tensor_size, plan),
        out_shape=shapes,
        in_specs=in_specs,
        out_specs=[vmem] * len(shapes),
        scratch_shapes=scratch,
        compiler_params=pltpu.CompilerParams(
            collective_id=0, has_side_effects=True, vmem_limit_bytes=VMEM_BYTES
        ),
        name="layer",
    )(*operands)


def unpack_kernel(count, *refs):
    sums, rows_ref, grad_ref, small_ref = refs[:count], *refs[count : count + 3]
    refs = refs[count + 3 :]
    targets, rows_out, grad_out, bqv_out, vectors = (
        refs[:count], refs[count], refs[count + 1], refs[count + 2], refs[count + 3 : count + 10]
    )
    wides, sem = refs[count + 10 : count + 10 + count], refs[-1]
    copies = []
    for source, target, wide in zip(sums, targets, wides):
        for at in range(0, source.shape[0], 2 * STEP):
            rows_at = pl.ds(at, min(2 * STEP, source.shape[0] - at))
            wide[rows_at, :] = source[rows_at, :].astype(F32)
            copy = pltpu.make_async_copy(wide.at[rows_at], target.at[rows_at], sem.at[len(copies)])
            copy.start()
            copies.append(copy)
    rows_out[...] = rows_ref[...]
    grad_out[...] = grad_ref[...]
    for index, vector in enumerate(vectors):
        vector[...] = small_ref[index : index + 1, :]
    half = bqv_out.shape[-1]
    for index in range(2):
        bqv_out[0, index : index + 1, :] = small_ref[7:8, pl.ds(index * half, half)]
    for copy in copies:
        copy.wait()


def unpack(sums, rows, grad, small, local):
    vmem = pl.BlockSpec(memory_space=pltpu.VMEM)
    count = len(sums)
    vector = jax.ShapeDtypeStruct((1, small.shape[1]), F32)
    wide = [jax.ShapeDtypeStruct(part.shape, F32) for part in sums]
    shapes = wide + [
        jax.ShapeDtypeStruct(rows.shape, rows.dtype),
        jax.ShapeDtypeStruct(grad.shape, grad.dtype),
        jax.ShapeDtypeStruct((1, 2, local), F32),
    ] + [vector] * 7
    pieces = sum(-(-part.shape[0] // (2 * STEP)) for part in sums)
    return pl.pallas_call(
        functools.partial(unpack_kernel, count),
        out_shape=shapes,
        in_specs=[vmem] * (count + 3),
        out_specs=[pl.BlockSpec(memory_space=pl.ANY)] * count + [vmem] * 10,
        scratch_shapes=[pltpu.VMEM(part.shape, F32) for part in sums]
        + [pltpu.SemaphoreType.DMA((pieces,))],
        compiler_params=pltpu.CompilerParams(vmem_limit_bytes=UNPACK_BYTES),
        name="unpack",
    )(*sums, rows, grad, small)


def shards(
    inputs, doc_ids, cotangent, w_qkv, b_qv, w_out, b_out, gain1, shift1,
    w_up, b_up, w_down, b_down, gain2, shift2,
):
    tensor_size = lax.axis_size("tensor")
    width = inputs.shape[2]
    local = w_out.shape[1]
    weights = (
        jnp.transpose(w_qkv[0], (1, 0, 2)), b_qv, w_out[0], b_out, gain1, shift1,
        w_up[0], b_up, w_down[0], b_down, gain2, shift2,
    )
    outputs, input_grads, gqkv, gout, gup, gdown, small = run_layer(
        inputs, doc_ids, cotangent, weights, tensor_size
    )
    sums = (gqkv, gout, gup, gdown)
    gqkv, gout, gup, gdown, outputs, input_grads, gbqv, *vectors = unpack(
        sums, outputs, input_grads, small, local
    )
    return (
        outputs[None],
        input_grads[None],
        jnp.transpose(gqkv.reshape(3, width, local), (1, 0, 2))[None],
        gbqv,
        gout[None],
        vectors[3],
        vectors[4],
        vectors[5],
        gup[None],
        vectors[6],
        gdown[None],
        vectors[0],
        vectors[1],
        vectors[2],
    )


def solution(mesh):
    rows = P(None, ("dp", "tensor"), None)
    banked = P("section", None, ("dp", "tensor"), None)
    vector = P("section", None)
    return jax.shard_map(
        shards,
        mesh=mesh,
        in_specs=(
            rows,
            P(None, "dp"),
            rows,
            P("section", None, None, "tensor"),
            P("section", None, "tensor"),
            P("section", "tensor", None),
            vector,
            vector,
            vector,
            P("section", None, "tensor"),
            P("section", "tensor"),
            P("section", "tensor", None),
            vector,
            vector,
            vector,
        ),
        out_specs=(
            banked,
            banked,
            P("section", None, None, "tensor"),
            P("section", None, "tensor"),
            P("section", "tensor", None),
            vector,
            vector,
            vector,
            P("section", None, "tensor"),
            P("section", "tensor"),
            P("section", "tensor", None),
            vector,
            vector,
            vector,
        ),
        check_vma=False,
    )
```

```python
import functools
import math

import jax
import jax.numpy as jnp
from jax import lax
from jax.experimental import pallas as pl
from jax.experimental.pallas import tpu as pltpu
from jax.sharding import PartitionSpec as P

HEAD_DIM = 64
MESH = pl.DeviceIdType.MESH
F32 = jnp.float32
BF16 = jnp.bfloat16
STEP = 256
SPREAD = ("tensor", "core", "y", "x")
VMEM_BYTES = 52 * 1024 * 1024
UNPACK_BYTES = 40 * 1024 * 1024
PIECE = 256
AFTER_FIRST = ((0, 1, 2), ())
AFTER_ATTENTION = ((3,), ())
AFTER_GRADS = (0, 1)
AFTER_LAST = ((5, 2, 3, 6, 4), ())
TAIL = (0, 1, 2, 3, 5, 6, 2, 4, 5, 0, 6, 1, 2, 3, 4, 5, 0, 6, 2, 1, 4, 5, 3, 6, 0, 1, 5, 2, 3, 2, 6, 4, 0, 4, 1, 0, 3, 1, 6, 5, 3, 6, 5)
TAIL_ONE = (0, 1, 2, 3, 4, 5, 6) * 8
ROUNDS = 4
AXES = {"core": (1, 2), "x": (2, 2), "y": (4, 4)}
SIZES = {"core": 2, "x": 2, "y": 4, "ring": 4}
RS_SEM = {"core": 0, "x": 1, "y": 2, "ring": 2}
AG_SEM = {"core": 8, "x": 9, "y": 10, "ring": 10}
X_FIRST = ("core", "x", "ring")
Y_FIRST = ("core", "ring", "x")
X_FIRST_DIRECT = ("core", "x", "y")
Y_FIRST_DIRECT = ("core", "y", "x")


def sum_plan(width, local, units):
    joined = 3 * width
    return (
        ("down", 0, units // 2, width, Y_FIRST),
        ("down", units // 2, units // 2, width, Y_FIRST),
        ("up", 0, width // 2, units, X_FIRST),
        ("up", width // 2, width // 2, units, Y_FIRST),
        ("out", 0, local, width, X_FIRST_DIRECT),
        ("qkv", 0, joined // 2, local, X_FIRST),
        ("qkv", joined // 2, joined // 2, local, Y_FIRST),
    )


def sum_buffers(rows, columns, order):
    shapes = []
    for axis in order:
        rows //= SIZES[axis]
        if axis == "ring":
            shapes.append((8, rows, columns // 2))
        elif axis == "y":
            shapes.append((3, rows, columns))
        else:
            shapes.append((rows, columns))
        shapes.append((rows, columns))
    return shapes


def dot(left, right):
    return lax.dot_general(left, right, (((1,), (0,)), ((), ())), preferred_element_type=F32)


def dot_last(left, right):
    return lax.dot_general(left, right, (((1,), (1,)), ((), ())), preferred_element_type=F32)


def dot_rows(left, right):
    return lax.dot_general(left, right, (((0,), (0,)), ((), ())), preferred_element_type=F32)


def norm(hidden, gain, shift):
    centred = hidden - jnp.mean(hidden, axis=-1, keepdims=True)
    inv_std = lax.rsqrt(jnp.mean(centred * centred, axis=-1, keepdims=True) + 1e-05)
    normed = centred * inv_std
    return normed * gain + shift, normed, inv_std


def norm_back(grad_out, normed, inv_std, gain):
    scaled = grad_out * gain
    return inv_std * (
        scaled
        - jnp.mean(scaled, axis=-1, keepdims=True)
        - normed * jnp.mean(scaled * normed, axis=-1, keepdims=True)
    )


def column_sum(block):
    return jnp.sum(block, axis=0, keepdims=True)


def layer_kernel(tensor_size, plan, *refs):
    (
        x_ref, doc_ref, cot_ref,
        wqkv_hbm, bqv_ref, wout_hbm, bout_ref, gain1_ref, shift1_ref,
        wup_hbm, bup_ref, wdown_hbm, bdown_ref, gain2_ref, shift2_ref,
        out_ref, dx_ref, gqkv_ref, gout_ref, gup_ref, gdown_ref, small_ref,
        wqkv_ref, wfull, wup_ref, wdown_ref,
        gath, rs_send, rs_recv, rs_own,
        qkv, probs, ctx, entry, y1, n1, r1, slope, act, n2, r2, dh2, dh, du, dqkv,
        sent_up, back_in, sent_back, small_acc,
        ctx_all, dctx_sent, dctx_all,
        pqkv, pout, pup, pdown,
        ag_ssem, ag_rsem, rs_ssem, rs_rsem, up_ssem, up_rsem, back_ssem, back_rsem,
        wide_ssem, wide_rsem, ctx_ssem, ctx_rsem, dctx_ssem, dctx_rsem,
        sum_ssem, sum_rsem, small_ssem, small_rsem, load_sem, calm_sem,
        *more,
    ) = refs
    spread_refs, sum_refs = more[: len(SPREAD)], more[len(SPREAD) :]
    grads = {"qkv": pqkv, "out": pout, "up": pup, "down": pdown}
    totals = {"qkv": gqkv_ref, "out": gout_ref, "up": gup_ref, "down": gdown_ref}
    batches, rows, width = x_ref.shape
    slot = rows * tensor_size
    local = wfull.shape[1]
    units = wup_ref.shape[1]
    pairs = local // (2 * HEAD_DIM)
    sec = lax.axis_index("section")
    me = lax.axis_index("tensor")
    dp = lax.axis_index("dp")
    other = 1 - sec
    scale = HEAD_DIM ** (-0.5)
    loads = [
        pltpu.make_async_copy(source, target, load_sem.at[index])
        for index, (source, target) in enumerate(
            (
                (wqkv_hbm, wqkv_ref), (wout_hbm, wfull.at[me]),
                (wup_hbm, wup_ref), (wdown_hbm, wdown_ref),
            )
        )
    ]
    for load in loads:
        load.start()

    barrier = pltpu.get_barrier_semaphore()
    for k in range(1, tensor_size):
        pl.semaphore_signal(
            barrier, inc=1, device_id={"tensor": lax.rem(me + k, tensor_size)}, device_id_type=MESH
        )
    pl.semaphore_signal(barrier, inc=1, device_id={"section": other}, device_id_type=MESH)
    greeted = tensor_size
    for axis, (stride, size) in AXES.items():
        for k in range(1, size):
            index = lax.rem(dp // stride, size)
            near = dp + (lax.rem(index + k, size) - index) * stride
            pl.semaphore_signal(barrier, inc=1, device_id={"dp": near}, device_id_type=MESH)
            greeted += 1
    pl.semaphore_wait(barrier, greeted)

    def band(index):
        return pl.ds(pl.multiple_of(index * rows, rows), rows)

    mine = band(me)

    def gather_copy(e, m, k):
        return pltpu.make_async_remote_copy(
            src_ref=gath.at[e, m, mine],
            dst_ref=gath.at[e, m, mine],
            send_sem=ag_ssem.at[e, m, k - 1],
            recv_sem=ag_rsem.at[e, m, k - 1],
            device_id={"tensor": lax.rem(me + k, tensor_size)},
            device_id_type=MESH,
        )

    def gather_start(e, m):
        for k in (2, 1, 3):
            gather_copy(e, m, k).start()

    def gather_wait(e, m):
        for k in range(1, tensor_size):
            source = band(lax.rem(me + tensor_size - k, tensor_size))
            pltpu.make_async_remote_copy(
                src_ref=gath.at[e, m, source],
                dst_ref=gath.at[e, m, source],
                send_sem=ag_ssem.at[e, m, k - 1],
                recv_sem=ag_rsem.at[e, m, k - 1],
                device_id={"tensor": lax.rem(me + k, tensor_size)},
                device_id_type=MESH,
            ).wait_recv()

    def scatter_copy(e, m, k):
        target = lax.rem(me + k, tensor_size)
        return pltpu.make_async_remote_copy(
            src_ref=rs_send.at[e, m, band(target)],
            dst_ref=rs_recv.at[e, m, k - 1],
            send_sem=rs_ssem.at[e, m, k - 1],
            recv_sem=rs_rsem.at[e, m, k - 1],
            device_id={"tensor": target},
            device_id_type=MESH,
        )

    def scatter_start(e, m):
        for k in (2, 1, 3):
            scatter_copy(e, m, k).start()

    def scatter_wait(e, m):
        total = rs_own[m, mine, :]
        for k in range(1, tensor_size):
            scatter_copy(e, m, k).wait_recv()
        for k in range(1, tensor_size):
            total = total + rs_recv[e, m, k - 1].astype(F32)
        return total

    def share_copy(whole, ssem, rsem, k, source):
        at = whole.at[source]
        return pltpu.make_async_remote_copy(
            src_ref=at,
            dst_ref=at,
            send_sem=ssem.at[k - 1],
            recv_sem=rsem.at[k - 1],
            device_id={"tensor": lax.rem(me + k, tensor_size)},
            device_id_type=MESH,
        )

    def share_start(whole, ssem, rsem):
        for k in (2, 1, 3):
            share_copy(whole, ssem, rsem, k, me).start()

    def share_wait(whole, ssem, rsem):
        for k in range(1, tensor_size):
            source = lax.rem(me + tensor_size - k, tensor_size)
            share_copy(whole, ssem, rsem, k, source).wait_recv()

    def share_drain(whole, ssem, rsem):
        for k in range(1, tensor_size):
            share_copy(whole, ssem, rsem, k, me).wait_send()

    wide = (wfull, wide_ssem, wide_rsem)

    def contexts(m):
        return ctx_all.at[m], ctx_ssem.at[m], ctx_rsem.at[m]

    def dctx_copy(m, k):
        target = lax.rem(me + k, tensor_size)
        return pltpu.make_async_remote_copy(
            src_ref=dctx_sent.at[m, target],
            dst_ref=dctx_all.at[m, mine],
            send_sem=dctx_ssem.at[m, k - 1],
            recv_sem=dctx_rsem.at[m, k - 1],
            device_id={"tensor": target},
            device_id_type=MESH,
        )

    def dctx_wait(m):
        for k in range(1, tensor_size):
            source = lax.rem(me + tensor_size - k, tensor_size)
            pltpu.make_async_remote_copy(
                src_ref=dctx_sent.at[m, source],
                dst_ref=dctx_all.at[m, band(source)],
                send_sem=dctx_ssem.at[m, k - 1],
                recv_sem=dctx_rsem.at[m, k - 1],
                device_id={"tensor": source},
                device_id_type=MESH,
            ).wait_recv()

    def put_part(e, m, columns, part):
        rs_own[m, :, columns] = part
        rs_send[e, m, :, columns] = part.astype(BF16)

    def up_copy(m):
        return pltpu.make_async_remote_copy(
            src_ref=sent_up.at[m],
            dst_ref=gath.at[0, m, mine],
            send_sem=up_ssem.at[m],
            recv_sem=up_rsem.at[m],
            device_id={"section": other},
            device_id_type=MESH,
        )

    def back_copy(m):
        return pltpu.make_async_remote_copy(
            src_ref=sent_back.at[m],
            dst_ref=back_in.at[m],
            send_sem=back_ssem.at[m],
            recv_sem=back_rsem.at[m],
            device_id={"section": other},
            device_id_type=MESH,
        )

    def each_batch(body, between=None):
        def step(m, carry):
            body(m)
            return carry

        if between is None:
            lax.fori_loop(0, batches, step, 0)
        else:
            for m in range(batches):
                body(m)
                between(m)

    def chunks(total):
        return [pl.ds(c, min(STEP, total - c)) for c in range(0, total, STEP)]

    def head_mask():
        return lax.broadcasted_iota(jnp.int32, (slot, 2 * HEAD_DIM), 1) < HEAD_DIM

    def pick(first, block):
        low_half = head_mask()
        keep = low_half if first else jnp.logical_not(low_half)
        return jnp.where(keep, block, jnp.zeros_like(block))


    place = {axis: lax.rem(dp // stride, size) for axis, (stride, size) in AXES.items()}

    def dp_peer(axis, k):
        stride, size = AXES[axis]
        return {"dp": dp + (lax.rem(place[axis] + k, size) - place[axis]) * stride}

    def sum_events(c, send):
        name, first, rows_all, columns, order = plan[c]
        grad, total = grads[name], totals[name]
        buffers = sum_refs[6 * c : 6 * c + 6]
        half = columns // 2
        low, high = pl.ds(0, half), pl.ds(half, half)
        sources, starts, blocks = [(grad, first)], [first], [rows_all]
        for step, axis in enumerate(order):
            blocks.append(blocks[-1] // SIZES[axis])
            index = place["y" if axis == "ring" else axis]
            starts.append(starts[-1] + index * blocks[-1])
            sources.append((buffers[2 * step + 1], 0))

        def lines(start, count):
            return pl.ds(pl.multiple_of(start, count), count)

        def remote(source, target, sem, axis, k):
            return pltpu.make_async_remote_copy(
                src_ref=source,
                dst_ref=target,
                send_sem=sum_ssem.at[c, sem],
                recv_sem=sum_rsem.at[c, sem],
                device_id=dp_peer(axis, k),
                device_id_type=MESH,
            )

        def spot(step):
            return place["y" if order[step] == "ring" else order[step]]

        def block_at(step, index):
            ref, base = sources[step]
            return ref, lines(base + index * blocks[step + 1], blocks[step + 1])

        def add(step, columns_at, parts):
            ref, at = block_at(step, spot(step))
            value = ref[at, columns_at].astype(F32)
            for part in parts:
                value = value + part.astype(F32)
            return value.astype(BF16)

        def finish(step, pieces):
            for columns_at, value in pieces:
                if step == 2:
                    total[lines(starts[3], blocks[3]), columns_at] = value
                else:
                    buffers[2 * step + 1][:, columns_at] = value

        def pair_scatter(step):
            axis = order[step]
            landing = buffers[2 * step]

            def copy():
                ref, at = block_at(step, 1 - place[axis])
                return remote(ref.at[at], landing, RS_SEM[axis], axis, 1)

            def begin():
                send(copy)

            def end():
                copy().wait_recv()
                pieces = []
                for columns_at in (low, high):
                    pieces.append((columns_at, add(step, columns_at, [landing[:, columns_at]])))
                finish(step, pieces)

            return [begin, end]

        def direct_scatter(step):
            landing = buffers[2 * step]

            def copy(k):
                ref, at = block_at(step, lax.rem(place["y"] + k, 4))
                return remote(ref.at[at], landing.at[k - 1], RS_SEM["y"] + k - 1, "y", k)

            def begin():
                for k in range(1, 4):
                    send(functools.partial(copy, k))

            def end():
                for k in range(1, 4):
                    copy(k).wait_recv()
                pieces = []
                for columns_at in (low, high):
                    parts = [landing[k, :, columns_at] for k in range(3)]
                    pieces.append((columns_at, add(step, columns_at, parts)))
                finish(step, pieces)

            return [begin, end]

        def ring_scatter(step):
            landing = buffers[2 * step]
            here = place["y"]

            def at(k, columns_at):
                ref, lines_at = block_at(step, lax.rem(here + k, 4))
                return ref.at[lines_at, columns_at]

            def copy(number):
                source, k = (
                    (lambda: at(2, high), 1),
                    (lambda: at(1, low), 1),
                    (lambda: at(2, low), 3),
                    (lambda: at(3, high), 3),
                    (lambda: landing.at[6], 1),
                    (lambda: landing.at[7], 3),
                )[number]
                return remote(source(), landing.at[number], RS_SEM["y"] + number, "y", k)

            def begin():
                for number in range(4):
                    send(functools.partial(copy, number))

            def relay():
                for number, k, columns_at, out in ((0, 1, high, 4), (2, 3, low, 5)):
                    copy(number).wait_recv()
                    value = at(k, columns_at)[...].astype(F32) + landing[number].astype(F32)
                    landing[out + 2] = value.astype(BF16)
                    send(functools.partial(copy, out))

            def end():
                for number in (1, 3, 4, 5):
                    copy(number).wait_recv()
                finish(
                    step,
                    [
                        (low, add(step, low, [landing[1], landing[5]])),
                        (high, add(step, high, [landing[3], landing[4]])),
                    ],
                )

            return [begin, relay, end]

        def region(step, index, columns_at=None):
            at = lines(starts[step] + index * blocks[step + 1], blocks[step + 1])
            return total.at[at] if columns_at is None else total.at[at, columns_at]

        def pair_gather(step):
            axis = order[step]

            def copy(index):
                return remote(region(step, index), region(step, index), AG_SEM[axis], axis, 1)

            return [
                lambda: send(lambda: copy(place[axis])),
                lambda: copy(1 - place[axis]).wait_recv(),
            ]

        def direct_gather(step):
            def copy(k, back):
                part = region(step, lax.rem(place["y"] + 4 - back, 4))
                return remote(part, part, AG_SEM["y"] + k - 1, "y", k)

            def begin():
                for k in range(1, 4):
                    send(functools.partial(copy, k, 0))

            def end():
                for k in range(1, 4):
                    copy(k, k).wait_recv()

            return [begin, end]

        def ring_gather(step):
            def copy(number, back):
                index = lax.rem(place["y"] + 4 - back, 4)
                columns_at = (None, None, low, high)[number]
                part = region(step, index, columns_at)
                return remote(part, part, AG_SEM["y"] + number, "y", (1, 3, 1, 3)[number])

            def begin():
                send(functools.partial(copy, 0, 0))
                send(functools.partial(copy, 1, 0))

            def relay():
                copy(0, 1).wait_recv()
                send(functools.partial(copy, 2, 1))
                copy(1, 3).wait_recv()
                send(functools.partial(copy, 3, 3))

            def end():
                copy(2, 2).wait_recv()
                copy(3, 2).wait_recv()

            return [begin, relay, end]

        def join(stages):
            events = [stages[0][0]]
            for stage, later in zip(stages, stages[1:] + [None]):
                events.extend(stage[1:-1])
                if later is None:
                    events.append(stage[-1])
                else:
                    events.append(lambda end=stage[-1], begin=later[0]: (end(), begin()))
            return events

        forms = {
            "core": (pair_scatter, pair_gather),
            "x": (pair_scatter, pair_gather),
            "y": (direct_scatter, direct_gather),
            "ring": (ring_scatter, ring_gather),
        }
        scatters = [forms[axis][0](step) for step, axis in enumerate(order)]
        gathers = [forms[axis][1](step) for step, axis in enumerate(order)]
        return join(scatters + gathers[::-1])

    sends, events = ([], []), ([], [])
    for section in range(2):

        def send(make, section=section):
            make().start()
            sends[section].append(make)

        events[section].extend(sum_events(c, send) for c in range(len(plan)))

    def advance(section, *which):
        @pl.when(sec == section)
        def _():
            for c in which:
                if events[section][c]:
                    events[section][c].pop(0)()

    def spread_copy(step, k, source):
        axis = SPREAD[step]
        size = tensor_size if axis == "tensor" else AXES[axis][1]
        at = spread_refs[step].at[source]
        return pltpu.make_async_remote_copy(
            src_ref=at,
            dst_ref=at,
            send_sem=small_ssem.at[step, k - 1],
            recv_sem=small_rsem.at[step, k - 1],
            device_id={"tensor": lax.rem(me + k, size)} if axis == "tensor" else dp_peer(axis, k),
            device_id_type=MESH,
        )

    def spread_place(step):
        axis = SPREAD[step]
        return (me, tensor_size) if axis == "tensor" else (place[axis], AXES[axis][1])

    def spread_start(step, value):
        index, size = spread_place(step)
        spread_refs[step][index] = value
        for k in range(1, size):
            spread_copy(step, k, index).start()

    def spread_finish(step):
        index, size = spread_place(step)
        for k in range(1, size):
            spread_copy(step, k, lax.rem(index + size - k, size)).wait_recv()
        value = spread_refs[step][0]
        for other_index in range(1, size):
            value = value + spread_refs[step][other_index]
        return value

    small_acc[...] = jnp.zeros_like(small_acc)

    @pl.when(sec == 0)
    def _():
        for m in range(batches):
            gath[0, m, mine, :] = x_ref[m]

    loads[1].wait()

    @pl.when(sec == 1)
    def _():
        share_start(*wide)

    for m in range(batches):
        @pl.when(sec == 1)
        def _():
            up_copy(m).wait_recv()

        gather_start(0, m)
        if m < batches - 1:
            for k in range(1, tensor_size):
                gather_copy(0, m, k).wait_send()

    loads[0].wait()

    @pl.when(sec == 1)
    def _():
        share_wait(*wide)


    def attention(m):
        entry[m] = gath[0, m, mine, :].astype(F32)
        gather_wait(0, m)
        for third in range(3):
            part = dot(gath[0, m], wqkv_ref[third])
            if third != 1:
                part = part + bqv_ref[0, third // 2 : third // 2 + 1, :]
            qkv[m, :, pl.ds(third * local, local)] = part.astype(BF16)
        across = jnp.broadcast_to(doc_ref[pl.ds(m, 1), :].astype(F32), (slot, slot))
        down = jnp.transpose(across)
        row_id = lax.broadcasted_iota(jnp.int32, (slot, slot), 0)
        col_id = lax.broadcasted_iota(jnp.int32, (slot, slot), 1)
        allowed = ((across == down) & (across >= 0)) | (row_id == col_id)
        low_half = head_mask()
        def third_of(third, pair):
            return qkv[m, :, pl.ds(third * local + pair * 2 * HEAD_DIM, 2 * HEAD_DIM)]

        heads = range(2 * pairs)
        raws = [
            dot_last(pick(head % 2 == 0, third_of(0, head // 2)), third_of(1, head // 2))
            for head in heads
        ]
        scores = [jnp.where(allowed, raw * scale, -1e30) for raw in raws]
        peaks = [jnp.max(score, axis=-1, keepdims=True) for score in scores]
        exps = [jnp.exp(score - peak) for score, peak in zip(scores, peaks)]
        sums = [jnp.sum(exp, axis=-1, keepdims=True) for exp in exps]
        softs = [exp / row_sum for exp, row_sum in zip(exps, sums)]
        halves = [dot(softs[head].astype(BF16), third_of(2, head // 2)) for head in heads]
        for head in heads:
            probs[m, head] = softs[head]
        for pair in range(pairs):
            both = jnp.where(low_half, halves[2 * pair], halves[2 * pair + 1])
            ctx[m, :, pl.ds(pair * 2 * HEAD_DIM, 2 * HEAD_DIM)] = both.astype(BF16)

        @pl.when(sec == 0)
        def _():
            for cols in chunks(width):
                put_part(0, m, cols, dot(ctx[m], wfull[me, :, cols]))
            scatter_start(0, m)

        @pl.when(sec == 1)
        def _():
            ctx_all[m, me] = ctx[m]
            share_start(*contexts(m))

    each_batch(attention)

    def first_norm(m):
        @pl.when(sec == 0)
        def _():
            hidden = entry[m] + scatter_wait(0, m) + bout_ref[...]
            out, normed, inv_std = norm(hidden, gain1_ref[...], shift1_ref[...])
            y1[m], n1[m], r1[m] = out, normed, inv_std
            gath[1, m, mine, :] = out.astype(BF16)
            gather_start(1, m)

    each_batch(first_norm)

    def whole_norm(m):
        share_wait(*contexts(m))
        for cols in chunks(width):
            part = gath[0, m, :, cols].astype(F32) + bout_ref[:, cols]
            for source in range(tensor_size):
                part = part + dot(ctx_all[m, source], wfull[source, :, cols])
            rs_own[m, :, cols] = part
        for at in range(0, slot, rows):
            lines_at = pl.ds(at, rows)
            out, _, _ = norm(rs_own[m, lines_at, :], gain1_ref[...], shift1_ref[...])
            gath[1, m, lines_at, :] = out.astype(BF16)
        out, normed, inv_std = norm(rs_own[m, mine, :], gain1_ref[...], shift1_ref[...])
        y1[m], n1[m], r1[m] = out, normed, inv_std

    for load in loads[2:]:
        load.wait()

    def feed_forward(m):
        @pl.when(sec == 0)
        def _():
            gather_wait(1, m)

        @pl.when(sec == 1)
        def _():
            whole_norm(m)

        for cols in chunks(units):
            pre = dot(gath[1, m], wup_ref[:, cols]) + bup_ref[:, cols]
            cdf = 0.5 * (1.0 + lax.erf(pre * (1.0 / math.sqrt(2.0))))
            slope[m, :, cols] = cdf + pre * jnp.exp(-0.5 * pre * pre) * (
                1.0 / math.sqrt(2.0 * math.pi)
            )
            act[m, :, cols] = (pre * cdf).astype(BF16)
        for cols in chunks(width):
            put_part(1, m, cols, dot(act[m], wdown_ref[:, cols]))
        scatter_start(1, m)

    each_batch(feed_forward)

    def back_entry(m):
        @pl.when(sec == 1)
        def _():
            back_in[m] = cot_ref[m]

        @pl.when(sec == 0)
        def _():
            back_copy(m).wait_recv()

        grad_out = back_in[m].astype(F32)
        grad = norm_back(grad_out, n2[m], r2[m], gain2_ref[...])
        small_acc[0:1, :] += column_sum(grad)
        small_acc[1:2, :] += column_sum(grad_out * n2[m])
        small_acc[2:3, :] += column_sum(grad_out)
        dh2[m] = grad
        gath[2, m, mine, :] = grad.astype(BF16)
        gather_start(2, m)

    def second_norm(m):
        hidden = y1[m] + scatter_wait(1, m) + bdown_ref[...]
        out, normed, inv_std = norm(hidden, gain2_ref[...], shift2_ref[...])
        n2[m], r2[m] = normed, inv_std
        rounded = out.astype(BF16)
        out_ref[m] = rounded

        @pl.when(sec == 0)
        def _():
            sent_up[m] = rounded
            up_copy(m).start()

        @pl.when(sec == 1)
        def _():
            back_entry(m)

    each_batch(second_norm)

    @pl.when(sec == 0)
    def _():
        for k in range(1, tensor_size):
            target = {"tensor": lax.rem(me + k, tensor_size)}
            pl.semaphore_signal(calm_sem, inc=1, device_id=target, device_id_type=MESH)
        pl.semaphore_wait(calm_sem, tensor_size - 1)
        share_start(*wide)

    @pl.when(sec == 0)
    def _():
        each_batch(back_entry)

    def weight_grad(left, right, target, base=0):
        total = batches * slot
        rhs = right[...].reshape(total, right.shape[-1])
        for rows_at in chunks(left.shape[-1]):
            lhs = left[:, :, rows_at].reshape(total, rows_at.size)
            target[pl.ds(base + rows_at.start, rows_at.size), :] = dot_rows(lhs, rhs).astype(BF16)

    def down_grad():
        weight_grad(act, gath.at[2], pdown)

    def up_grad():
        weight_grad(gath.at[1], du, pup)

    def feed_back(m):
        @pl.when(sec == 1)
        def _():
            gather_wait(2, m)

        for cols in chunks(units):
            grad = (dot_last(gath[2, m], wdown_ref[cols, :]) * slope[m, :, cols]).astype(BF16)
            du[m, :, cols] = grad
            small_acc[6:7, cols] += column_sum(grad.astype(F32))
        for cols in chunks(width):
            put_part(2, m, cols, dot_last(du[m], wup_ref[cols, :]))
        scatter_start(2, m)

    @pl.when(sec == 0)
    def _():
        gather_wait(2, 0)

    feed_back(0)

    @pl.when(sec == 0)
    def _():
        for m in range(1, batches):
            gather_wait(2, m)
        down_grad()

    advance(0, 0, 1)
    for m in range(1, batches):
        feed_back(m)
    pl.when(sec == 0)(up_grad)
    advance(0, 2, 3)

    @pl.when(sec == 0)
    def _():
        share_wait(*wide)

    def first_back(m):
        grad_out = dh2[m] + scatter_wait(2, m)
        grad = norm_back(grad_out, n1[m], r1[m], gain1_ref[...])
        small_acc[3:4, :] += column_sum(grad)
        small_acc[4:5, :] += column_sum(grad_out * n1[m])
        small_acc[5:6, :] += column_sum(grad_out)
        dh[m] = grad
        rounded = grad.astype(BF16)
        gath[3, m, mine, :] = rounded
        for target in range(tensor_size):
            dctx_sent[m, target] = dot_last(rounded, wfull[target]).astype(BF16)
        dctx_all[m, mine, :] = dctx_sent[m, me]
        for k in (2, 1, 3):
            dctx_copy(m, k).start()
        gather_start(3, m)

    each_batch(first_back, lambda m: advance(0, *AFTER_FIRST[m]))

    def attention_back(m):
        dctx_wait(m)
        low_half = head_mask()
        heads = range(2 * pairs)

        def third_of(third, pair):
            return qkv[m, :, pl.ds(third * local + pair * 2 * HEAD_DIM, 2 * HEAD_DIM)]

        dctx = [dctx_all[m, :, pl.ds(pair * 2 * HEAD_DIM, 2 * HEAD_DIM)] for pair in range(pairs)]
        dprobs = [
            dot_last(pick(head % 2 == 0, dctx[head // 2]), third_of(2, head // 2)) for head in heads
        ]
        softs = [probs[m, head] for head in heads]
        means = [
            jnp.sum(soft * dprob, axis=-1, keepdims=True) for soft, dprob in zip(softs, dprobs)
        ]
        dscores = [
            (soft * (dprob - mean)).astype(BF16)
            for soft, dprob, mean in zip(softs, dprobs, means)
        ]
        dq = [dot(dscores[head], third_of(1, head // 2)) * scale for head in heads]
        dk = [dot_rows(dscores[head], third_of(0, head // 2)) * scale for head in heads]
        dv = [dot_rows(softs[head].astype(BF16), dctx[head // 2]) for head in heads]
        for place_of, parts in enumerate((dq, dk, dv)):
            for pair in range(pairs):
                at = pair * 2 * HEAD_DIM
                grad = jnp.where(low_half, parts[2 * pair], parts[2 * pair + 1]).astype(BF16)
                dqkv[m, :, pl.ds(place_of * local + at, 2 * HEAD_DIM)] = grad
                if place_of != 1:
                    to = at if place_of == 0 else local + at
                    small_acc[7:8, pl.ds(to, 2 * HEAD_DIM)] += column_sum(grad.astype(F32))
        for cols in chunks(width):
            part = dot_last(dqkv[m, :, pl.ds(0, local)], wqkv_ref[0, cols, :])
            for third in range(1, 3):
                part = part + dot_last(
                    dqkv[m, :, pl.ds(third * local, local)], wqkv_ref[third, cols, :]
                )
            put_part(3, m, cols, part)
        scatter_start(3, m)

    each_batch(attention_back, lambda m: advance(0, *AFTER_ATTENTION[m]))

    def joined_grad():
        for third in range(3):
            weight_grad(
                gath.at[0], dqkv.at[:, :, pl.ds(third * local, local)], pqkv, base=third * width
            )

    pl.when(sec == 0)(joined_grad)
    advance(0, 5, 6)
    spread_start(0, small_acc[...])
    for m in range(batches):
        gather_wait(3, m)

    def out_grad():
        weight_grad(ctx, gath.at[3], pout)

    pl.when(sec == 0)(out_grad)
    advance(0, 4, *AFTER_GRADS)

    def last_back(m):
        grad = dh[m] + scatter_wait(3, m)
        dx_ref[m] = grad

        @pl.when(sec == 1)
        def _():
            sent_back[m] = grad.astype(BF16)
            back_copy(m).start()

    each_batch(last_back, lambda m: advance(0, *AFTER_LAST[m]))

    @pl.when(sec == 1)
    def _():
        down_grad()
        up_grad()
        out_grad()
        joined_grad()

    advance(1, 0, 1, 2, 3, 4, 5, 6)
    small_row = lax.broadcasted_iota(jnp.int32, small_acc.shape, 0)
    spread_start(1, jnp.where(small_row < 6, spread_finish(0), small_acc[...]))
    small_step = 1
    for part in range(ROUNDS):
        at = len(TAIL) // ROUNDS
        advance(0, *TAIL[part * at : (part + 1) * at if part < ROUNDS - 1 else len(TAIL)])
        advance(1, *TAIL_ONE[part * 14 : part * 14 + 14])
        if small_step < len(SPREAD):
            value = spread_finish(small_step)
            small_step += 1
            if small_step < len(SPREAD):
                spread_start(small_step, value)
            else:
                small_ref[...] = value
    assert not any(events[0]) and not any(events[1])

    for make in sends[0]:
        make().wait_send()
    for step in range(len(SPREAD)):
        index, size = spread_place(step)
        for k in range(1, size):
            spread_copy(step, k, index).wait_send()

    def drain(m):
        for e in range(4):
            for k in range(1, tensor_size):
                if e:
                    scatter_copy(e, m, k).wait_send()
                if e > 1:
                    gather_copy(e, m, k).wait_send()
        for k in range(1, tensor_size):
            dctx_copy(m, k).wait_send()

        @pl.when(sec == 0)
        def _():
            up_copy(m).wait_send()
            for k in range(1, tensor_size):
                scatter_copy(0, m, k).wait_send()
                gather_copy(1, m, k).wait_send()

        @pl.when(sec == 1)
        def _():
            back_copy(m).wait_send()
            share_drain(*contexts(m))

    for k in range(1, tensor_size):
        gather_copy(0, batches - 1, k).wait_send()
    share_drain(*wide)
    each_batch(drain)


def run_layer(x, docs, cot, weights, tensor_size):
    batches, rows, width = x.shape
    slot = rows * tensor_size
    wqkv, bqv, wout, bout, gain1, shift1, wup, bup, wdown, bdown, gain2, shift2 = weights
    local = wout.shape[0]
    units = wup.shape[1]
    heads = local // HEAD_DIM
    vmem = pl.BlockSpec(memory_space=pltpu.VMEM)
    others = tensor_size - 1
    dma = pltpu.SemaphoreType.DMA
    operands = (x, docs, cot) + weights
    small_shape = (8, width)
    shard = (batches, rows, width)
    shapes = (
        pltpu.VMEM(shard, BF16),
        pltpu.VMEM(shard, F32),
        pltpu.VMEM((3 * width, local), BF16),
        pltpu.VMEM(wout.shape, BF16),
        pltpu.VMEM(wup.shape, BF16),
        pltpu.VMEM(wdown.shape, BF16),
        pltpu.VMEM(small_shape, F32),
    )
    plan = sum_plan(width, local, units)
    scratch = [
        pltpu.VMEM(wqkv.shape, BF16),
        pltpu.VMEM((tensor_size,) + wout.shape, BF16),
        pltpu.VMEM(wup.shape, BF16),
        pltpu.VMEM(wdown.shape, BF16),
        pltpu.VMEM((4, batches, slot, width), BF16),
        pltpu.VMEM((4, batches, slot, width), BF16),
        pltpu.VMEM((4, batches, others, rows, width), BF16),
        pltpu.VMEM((batches, slot, width), F32),
        pltpu.VMEM((batches, slot, 3 * local), BF16),
        pltpu.VMEM((batches, heads, slot, slot), F32),
        pltpu.VMEM((batches, slot, local), BF16),
        pltpu.VMEM(shard, F32),
        pltpu.VMEM(shard, F32),
        pltpu.VMEM(shard, F32),
        pltpu.VMEM((batches, rows, 1), F32),
        pltpu.VMEM((batches, slot, units), F32),
        pltpu.VMEM((batches, slot, units), BF16),
        pltpu.VMEM(shard, F32),
        pltpu.VMEM((batches, rows, 1), F32),
        pltpu.VMEM(shard, F32),
        pltpu.VMEM(shard, F32),
        pltpu.VMEM((batches, slot, units), BF16),
        pltpu.VMEM((batches, slot, 3 * local), BF16),
        pltpu.VMEM(shard, BF16),
        pltpu.VMEM(shard, BF16),
        pltpu.VMEM(shard, BF16),
        pltpu.VMEM(small_shape, F32),
        pltpu.VMEM((batches, tensor_size, slot, local), BF16),
        pltpu.VMEM((batches, tensor_size, rows, local), BF16),
        pltpu.VMEM((batches, slot, local), BF16),
        pltpu.VMEM((3 * width, local), BF16),
        pltpu.VMEM(wout.shape, BF16),
        pltpu.VMEM(wup.shape, BF16),
        pltpu.VMEM(wdown.shape, BF16),
        dma((4, batches, others)),
        dma((4, batches, others)),
        dma((4, batches, others)),
        dma((4, batches, others)),
        dma((batches,)),
        dma((batches,)),
        dma((batches,)),
        dma((batches,)),
        dma((others,)),
        dma((others,)),
        dma((batches, others)),
        dma((batches, others)),
        dma((batches, others)),
        dma((batches, others)),
        dma((len(plan), 14)),
        dma((len(plan), 14)),
        dma((len(SPREAD), 3)),
        dma((len(SPREAD), 3)),
        dma((4,)),
        pltpu.SemaphoreType.REGULAR,
    ]
    for axis in SPREAD:
        size = tensor_size if axis == "tensor" else AXES[axis][1]
        scratch.append(pltpu.VMEM((size,) + small_shape, F32))
    for _, _, rows_all, columns, order in plan:
        scratch.extend(pltpu.VMEM(shape, BF16) for shape in sum_buffers(rows_all, columns, order))
    in_specs = [vmem] * len(operands)
    for index in (3, 5, 9, 11):
        in_specs[index] = pl.BlockSpec(memory_space=pl.ANY)
    return pl.pallas_call(
        functools.partial(layer_kernel, tensor_size, plan),
        out_shape=shapes,
        in_specs=in_specs,
        out_specs=[vmem] * len(shapes),
        scratch_shapes=scratch,
        compiler_params=pltpu.CompilerParams(
            collective_id=0, has_side_effects=True, vmem_limit_bytes=VMEM_BYTES
        ),
        name="layer",
    )(*operands)


def unpack_kernel(count, *refs):
    sums, rows_ref, grad_ref, small_ref = refs[:count], *refs[count : count + 3]
    refs = refs[count + 3 :]
    targets, rows_out, grad_out, bqv_out, vectors = (
        refs[:count], refs[count], refs[count + 1], refs[count + 2], refs[count + 3 : count + 10]
    )
    wides, lone, biases, sem = refs[count + 10 : 2 * count + 10], *refs[2 * count + 10 :]
    copies = []

    def write(source, target):
        copy = pltpu.make_async_copy(source, target, sem.at[len(copies)])
        copy.start()
        copies.append(copy)

    for source, target, wide in zip(sums, targets, wides):
        for at in range(0, source.shape[0], PIECE):
            rows_at = pl.ds(at, PIECE)
            wide[rows_at, :] = source[rows_at, :].astype(F32)
            write(wide.at[rows_at], target.at[rows_at])
    write(rows_ref, rows_out)
    write(grad_ref, grad_out)
    half = bqv_out.shape[-1]
    for index in range(2):
        biases[0, index : index + 1, :] = small_ref[7:8, pl.ds(index * half, half)]
    write(biases, bqv_out)
    for index, vector in enumerate(vectors):
        lone[index] = small_ref[index : index + 1, :]
        write(lone.at[index], vector)
    for copy in copies:
        copy.wait()


def unpack(sums, rows, grad, small, local):
    vmem = pl.BlockSpec(memory_space=pltpu.VMEM)
    count = len(sums)
    vector = jax.ShapeDtypeStruct((1, small.shape[1]), F32)
    shapes = [jax.ShapeDtypeStruct(part.shape, F32) for part in sums] + [
        jax.ShapeDtypeStruct(rows.shape, rows.dtype),
        jax.ShapeDtypeStruct(grad.shape, grad.dtype),
        jax.ShapeDtypeStruct((1, 2, local), F32),
    ] + [vector] * 7
    pieces = sum(part.shape[0] // PIECE for part in sums) + 10
    return pl.pallas_call(
        functools.partial(unpack_kernel, count),
        out_shape=shapes,
        in_specs=[vmem] * (count + 3),
        out_specs=[pl.BlockSpec(memory_space=pl.ANY)] * (count + 10),
        scratch_shapes=[pltpu.VMEM(part.shape, F32) for part in sums]
        + [
            pltpu.VMEM((7, 1, small.shape[1]), F32),
            pltpu.VMEM((1, 2, local), F32),
            pltpu.SemaphoreType.DMA((pieces,)),
        ],
        compiler_params=pltpu.CompilerParams(vmem_limit_bytes=UNPACK_BYTES),
        name="unpack",
    )(*sums, rows, grad, small)


def shards(
    inputs, doc_ids, cotangent, w_qkv, b_qv, w_out, b_out, gain1, shift1,
    w_up, b_up, w_down, b_down, gain2, shift2,
):
    tensor_size = lax.axis_size("tensor")
    width = inputs.shape[2]
    local = w_out.shape[1]
    weights = (
        jnp.transpose(w_qkv[0], (1, 0, 2)), b_qv, w_out[0], b_out, gain1, shift1,
        w_up[0], b_up, w_down[0], b_down, gain2, shift2,
    )
    outputs, input_grads, gqkv, gout, gup, gdown, small = run_layer(
        inputs, doc_ids, cotangent, weights, tensor_size
    )
    sums = (gqkv, gout, gup, gdown)
    gqkv, gout, gup, gdown, outputs, input_grads, gbqv, *vectors = unpack(
        sums, outputs, input_grads, small, local
    )
    return (
        outputs[None],
        input_grads[None],
        jnp.transpose(gqkv.reshape(3, width, local), (1, 0, 2))[None],
        gbqv,
        gout[None],
        vectors[3],
        vectors[4],
        vectors[5],
        gup[None],
        vectors[6],
        gdown[None],
        vectors[0],
        vectors[1],
        vectors[2],
    )


def solution(mesh):
    rows = P(None, ("dp", "tensor"), None)
    banked = P("section", None, ("dp", "tensor"), None)
    vector = P("section", None)
    return jax.shard_map(
        shards,
        mesh=mesh,
        in_specs=(
            rows,
            P(None, "dp"),
            rows,
            P("section", None, None, "tensor"),
            P("section", None, "tensor"),
            P("section", "tensor", None),
            vector,
            vector,
            vector,
            P("section", None, "tensor"),
            P("section", "tensor"),
            P("section", "tensor", None),
            vector,
            vector,
            vector,
        ),
        out_specs=(
            banked,
            banked,
            P("section", None, None, "tensor"),
            P("section", None, "tensor"),
            P("section", "tensor", None),
            vector,
            vector,
            vector,
            P("section", None, "tensor"),
            P("section", "tensor"),
            P("section", "tensor", None),
            vector,
            vector,
            vector,
        ),
        check_vma=False,
    )
```

```python
import functools
import math

import jax
import jax.numpy as jnp
from jax import lax
from jax.experimental import pallas as pl
from jax.experimental.pallas import tpu as pltpu
from jax.sharding import PartitionSpec as P

HEAD_DIM = 64
MESH = pl.DeviceIdType.MESH
F32 = jnp.float32
BF16 = jnp.bfloat16
STEP = 256
SPREAD = ("tensor", "core", "y", "x")
VMEM_BYTES = 52 * 1024 * 1024
UNPACK_BYTES = 40 * 1024 * 1024
PIECE = 256
AFTER_FIRST = ((0, 1, 2), ())
AFTER_ATTENTION = ((3,), ())
AFTER_GRADS = (0, 1)
AFTER_LAST = ((5, 2, 3, 6, 4), ())
TAIL = (0, 1, 2, 3, 5, 6, 2, 4, 5, 0, 6, 1, 2, 3, 4, 5, 0, 6, 2, 1, 4, 5, 3, 6, 0, 1, 5, 2, 3, 2, 6, 4, 0, 4, 1, 0, 3, 1, 6, 5, 3, 6, 5)
TAIL_ONE = (0, 1, 2, 3, 4, 5, 6) * 8
ROUNDS = 4
AXES = {"core": (1, 2), "x": (2, 2), "y": (4, 4)}
SIZES = {"core": 2, "x": 2, "y": 4, "ring": 4}
RS_SEM = {"core": 0, "x": 1, "y": 2, "ring": 2}
AG_SEM = {"core": 8, "x": 9, "y": 10, "ring": 10}
X_FIRST = ("core", "x", "ring")
Y_FIRST = ("core", "ring", "x")
X_FIRST_DIRECT = ("core", "x", "y")
Y_FIRST_DIRECT = ("core", "y", "x")


def sum_plan(width, local, units):
    joined = 3 * width
    return (
        ("down", 0, units // 2, width, Y_FIRST),
        ("down", units // 2, units // 2, width, Y_FIRST),
        ("up", 0, width // 2, units, X_FIRST),
        ("up", width // 2, width // 2, units, Y_FIRST),
        ("out", 0, local, width, X_FIRST_DIRECT),
        ("qkv", 0, joined // 2, local, X_FIRST),
        ("qkv", joined // 2, joined // 2, local, Y_FIRST),
    )


def sum_buffers(rows, columns, order):
    shapes = []
    for axis in order:
        rows //= SIZES[axis]
        if axis == "ring":
            shapes.append((8, rows, columns // 2))
        elif axis == "y":
            shapes.append((3, rows, columns))
        else:
            shapes.append((rows, columns))
        shapes.append((rows, columns))
    return shapes


def dot(left, right):
    return lax.dot_general(left, right, (((1,), (0,)), ((), ())), preferred_element_type=F32)


def dot_last(left, right):
    return lax.dot_general(left, right, (((1,), (1,)), ((), ())), preferred_element_type=F32)


def dot_rows(left, right):
    return lax.dot_general(left, right, (((0,), (0,)), ((), ())), preferred_element_type=F32)


def norm(hidden, gain, shift):
    centred = hidden - jnp.mean(hidden, axis=-1, keepdims=True)
    inv_std = lax.rsqrt(jnp.mean(centred * centred, axis=-1, keepdims=True) + 1e-05)
    normed = centred * inv_std
    return normed * gain + shift, normed, inv_std


def norm_back(grad_out, normed, inv_std, gain):
    scaled = grad_out * gain
    return inv_std * (
        scaled
        - jnp.mean(scaled, axis=-1, keepdims=True)
        - normed * jnp.mean(scaled * normed, axis=-1, keepdims=True)
    )


def column_sum(block):
    return jnp.sum(block, axis=0, keepdims=True)


def layer_kernel(tensor_size, plan, *refs):
    (
        x_ref, doc_ref, cot_ref,
        wqkv_hbm, bqv_ref, wout_hbm, bout_ref, gain1_ref, shift1_ref,
        wup_hbm, bup_ref, wdown_hbm, bdown_ref, gain2_ref, shift2_ref,
        out_ref, dx_ref, gqkv_ref, gout_ref, gup_ref, gdown_ref, small_ref,
        wqkv_ref, wfull, wup_ref, wdown_ref,
        gath, rs_send, rs_recv, rs_own,
        qkv, probs, ctx, entry, y1, n1, r1, slope, act, n2, r2, dh2, dh, du, dqkv,
        sent_up, back_in, sent_back, small_acc,
        ctx_all, dctx_sent, dctx_all,
        pqkv, pout, pup, pdown,
        ag_ssem, ag_rsem, rs_ssem, rs_rsem, up_ssem, up_rsem, back_ssem, back_rsem,
        wide_ssem, wide_rsem, ctx_ssem, ctx_rsem, dctx_ssem, dctx_rsem,
        sum_ssem, sum_rsem, small_ssem, small_rsem, load_sem, calm_sem,
        *more,
    ) = refs
    spread_refs, sum_refs = more[: len(SPREAD)], more[len(SPREAD) :]
    grads = {"qkv": pqkv, "out": pout, "up": pup, "down": pdown}
    totals = {"qkv": gqkv_ref, "out": gout_ref, "up": gup_ref, "down": gdown_ref}
    batches, rows, width = x_ref.shape
    slot = rows * tensor_size
    local = wfull.shape[1]
    units = wup_ref.shape[1]
    pairs = local // (2 * HEAD_DIM)
    sec = lax.axis_index("section")
    me = lax.axis_index("tensor")
    dp = lax.axis_index("dp")
    other = 1 - sec
    scale = HEAD_DIM ** (-0.5)
    loads = [
        pltpu.make_async_copy(source, target, load_sem.at[index])
        for index, (source, target) in enumerate(
            (
                (wqkv_hbm, wqkv_ref), (wout_hbm, wfull.at[me]),
                (wup_hbm, wup_ref), (wdown_hbm, wdown_ref),
            )
        )
    ]
    for load in loads:
        load.start()

    barrier = pltpu.get_barrier_semaphore()
    for k in range(1, tensor_size):
        pl.semaphore_signal(
            barrier, inc=1, device_id={"tensor": lax.rem(me + k, tensor_size)}, device_id_type=MESH
        )
    pl.semaphore_signal(barrier, inc=1, device_id={"section": other}, device_id_type=MESH)
    greeted = tensor_size
    for axis, (stride, size) in AXES.items():
        for k in range(1, size):
            index = lax.rem(dp // stride, size)
            near = dp + (lax.rem(index + k, size) - index) * stride
            pl.semaphore_signal(barrier, inc=1, device_id={"dp": near}, device_id_type=MESH)
            greeted += 1
    pl.semaphore_wait(barrier, greeted)

    def band(index):
        return pl.ds(pl.multiple_of(index * rows, rows), rows)

    mine = band(me)

    def gather_copy(e, m, k):
        return pltpu.make_async_remote_copy(
            src_ref=gath.at[e, m, mine],
            dst_ref=gath.at[e, m, mine],
            send_sem=ag_ssem.at[e, m, k - 1],
            recv_sem=ag_rsem.at[e, m, k - 1],
            device_id={"tensor": lax.rem(me + k, tensor_size)},
            device_id_type=MESH,
        )

    def gather_start(e, m):
        for k in (2, 1, 3):
            gather_copy(e, m, k).start()

    def gather_wait(e, m):
        for k in range(1, tensor_size):
            source = band(lax.rem(me + tensor_size - k, tensor_size))
            pltpu.make_async_remote_copy(
                src_ref=gath.at[e, m, source],
                dst_ref=gath.at[e, m, source],
                send_sem=ag_ssem.at[e, m, k - 1],
                recv_sem=ag_rsem.at[e, m, k - 1],
                device_id={"tensor": lax.rem(me + k, tensor_size)},
                device_id_type=MESH,
            ).wait_recv()

    def scatter_copy(e, m, k):
        target = lax.rem(me + k, tensor_size)
        return pltpu.make_async_remote_copy(
            src_ref=rs_send.at[e, m, band(target)],
            dst_ref=rs_recv.at[e, m, k - 1],
            send_sem=rs_ssem.at[e, m, k - 1],
            recv_sem=rs_rsem.at[e, m, k - 1],
            device_id={"tensor": target},
            device_id_type=MESH,
        )

    def scatter_start(e, m):
        for k in (2, 1, 3):
            scatter_copy(e, m, k).start()

    def scatter_wait(e, m):
        total = rs_own[m, mine, :]
        for k in range(1, tensor_size):
            scatter_copy(e, m, k).wait_recv()
        for k in range(1, tensor_size):
            total = total + rs_recv[e, m, k - 1].astype(F32)
        return total

    def share_copy(whole, ssem, rsem, k, source):
        at = whole.at[source]
        return pltpu.make_async_remote_copy(
            src_ref=at,
            dst_ref=at,
            send_sem=ssem.at[k - 1],
            recv_sem=rsem.at[k - 1],
            device_id={"tensor": lax.rem(me + k, tensor_size)},
            device_id_type=MESH,
        )

    def share_start(whole, ssem, rsem):
        for k in (2, 1, 3):
            share_copy(whole, ssem, rsem, k, me).start()

    def share_wait(whole, ssem, rsem):
        for k in range(1, tensor_size):
            source = lax.rem(me + tensor_size - k, tensor_size)
            share_copy(whole, ssem, rsem, k, source).wait_recv()

    def share_drain(whole, ssem, rsem):
        for k in range(1, tensor_size):
            share_copy(whole, ssem, rsem, k, me).wait_send()

    wide = (wfull, wide_ssem, wide_rsem)

    def contexts(m):
        return ctx_all.at[m], ctx_ssem.at[m], ctx_rsem.at[m]

    def dctx_copy(m, k):
        target = lax.rem(me + k, tensor_size)
        return pltpu.make_async_remote_copy(
            src_ref=dctx_sent.at[m, target],
            dst_ref=dctx_all.at[m, mine],
            send_sem=dctx_ssem.at[m, k - 1],
            recv_sem=dctx_rsem.at[m, k - 1],
            device_id={"tensor": target},
            device_id_type=MESH,
        )

    def dctx_wait(m):
        for k in range(1, tensor_size):
            source = lax.rem(me + tensor_size - k, tensor_size)
            pltpu.make_async_remote_copy(
                src_ref=dctx_sent.at[m, source],
                dst_ref=dctx_all.at[m, band(source)],
                send_sem=dctx_ssem.at[m, k - 1],
                recv_sem=dctx_rsem.at[m, k - 1],
                device_id={"tensor": source},
                device_id_type=MESH,
            ).wait_recv()

    def put_part(e, m, columns, part):
        rs_own[m, :, columns] = part
        rs_send[e, m, :, columns] = part.astype(BF16)

    def up_copy(m):
        return pltpu.make_async_remote_copy(
            src_ref=sent_up.at[m],
            dst_ref=gath.at[0, m, mine],
            send_sem=up_ssem.at[m],
            recv_sem=up_rsem.at[m],
            device_id={"section": other},
            device_id_type=MESH,
        )

    def back_copy(m):
        return pltpu.make_async_remote_copy(
            src_ref=sent_back.at[m],
            dst_ref=back_in.at[m],
            send_sem=back_ssem.at[m],
            recv_sem=back_rsem.at[m],
            device_id={"section": other},
            device_id_type=MESH,
        )

    def each_batch(body, between=None):
        def step(m, carry):
            body(m)
            return carry

        if between is None:
            lax.fori_loop(0, batches, step, 0)
        else:
            for m in range(batches):
                body(m)
                between(m)

    def chunks(total):
        return [pl.ds(c, min(STEP, total - c)) for c in range(0, total, STEP)]

    def head_mask():
        return lax.broadcasted_iota(jnp.int32, (slot, 2 * HEAD_DIM), 1) < HEAD_DIM

    def pick(first, block):
        low_half = head_mask()
        keep = low_half if first else jnp.logical_not(low_half)
        return jnp.where(keep, block, jnp.zeros_like(block))


    place = {axis: lax.rem(dp // stride, size) for axis, (stride, size) in AXES.items()}

    def dp_peer(axis, k):
        stride, size = AXES[axis]
        return {"dp": dp + (lax.rem(place[axis] + k, size) - place[axis]) * stride}

    def sum_events(c, send):
        name, first, rows_all, columns, order = plan[c]
        grad, total = grads[name], totals[name]
        buffers = sum_refs[6 * c : 6 * c + 6]
        half = columns // 2
        low, high = pl.ds(0, half), pl.ds(half, half)
        sources, starts, blocks = [(grad, first)], [first], [rows_all]
        for step, axis in enumerate(order):
            blocks.append(blocks[-1] // SIZES[axis])
            index = place["y" if axis == "ring" else axis]
            starts.append(starts[-1] + index * blocks[-1])
            sources.append((buffers[2 * step + 1], 0))

        def lines(start, count):
            return pl.ds(pl.multiple_of(start, count), count)

        def remote(source, target, sem, axis, k):
            return pltpu.make_async_remote_copy(
                src_ref=source,
                dst_ref=target,
                send_sem=sum_ssem.at[c, sem % 8],
                recv_sem=sum_rsem.at[c, sem],
                device_id=dp_peer(axis, k),
                device_id_type=MESH,
            )

        def spot(step):
            return place["y" if order[step] == "ring" else order[step]]

        def block_at(step, index):
            ref, base = sources[step]
            return ref, lines(base + index * blocks[step + 1], blocks[step + 1])

        def add(step, columns_at, parts):
            ref, at = block_at(step, spot(step))
            value = ref[at, columns_at].astype(F32)
            for part in parts:
                value = value + part.astype(F32)
            return value.astype(BF16)

        def finish(step, pieces):
            for columns_at, value in pieces:
                if step == 2:
                    total[lines(starts[3], blocks[3]), columns_at] = value
                else:
                    buffers[2 * step + 1][:, columns_at] = value

        def pair_scatter(step):
            axis = order[step]
            landing = buffers[2 * step]

            def copy():
                ref, at = block_at(step, 1 - place[axis])
                return remote(ref.at[at], landing, RS_SEM[axis], axis, 1)

            def begin():
                send((c, RS_SEM[axis]), copy)

            def end():
                copy().wait_recv()
                pieces = []
                for columns_at in (low, high):
                    pieces.append((columns_at, add(step, columns_at, [landing[:, columns_at]])))
                finish(step, pieces)

            return [begin, end]

        def direct_scatter(step):
            landing = buffers[2 * step]

            def copy(k):
                ref, at = block_at(step, lax.rem(place["y"] + k, 4))
                return remote(ref.at[at], landing.at[k - 1], RS_SEM["y"] + k - 1, "y", k)

            def begin():
                for k in (2, 1, 3):
                    send((c, RS_SEM["y"] + k - 1), functools.partial(copy, k))

            def end():
                for k in range(1, 4):
                    copy(k).wait_recv()
                pieces = []
                for columns_at in (low, high):
                    parts = [landing[k, :, columns_at] for k in range(3)]
                    pieces.append((columns_at, add(step, columns_at, parts)))
                finish(step, pieces)

            return [begin, end]

        def ring_scatter(step):
            landing = buffers[2 * step]
            here = place["y"]

            def at(k, columns_at):
                ref, lines_at = block_at(step, lax.rem(here + k, 4))
                return ref.at[lines_at, columns_at]

            def copy(number):
                source, k = (
                    (lambda: at(2, high), 1),
                    (lambda: at(1, low), 1),
                    (lambda: at(2, low), 3),
                    (lambda: at(3, high), 3),
                    (lambda: landing.at[6], 1),
                    (lambda: landing.at[7], 3),
                )[number]
                return remote(source(), landing.at[number], RS_SEM["y"] + number, "y", k)

            def begin():
                for number in range(4):
                    send((c, RS_SEM["y"] + number), functools.partial(copy, number))

            def relay():
                for number, k, columns_at, out in ((0, 1, high, 4), (2, 3, low, 5)):
                    copy(number).wait_recv()
                    value = at(k, columns_at)[...].astype(F32) + landing[number].astype(F32)
                    landing[out + 2] = value.astype(BF16)
                    send((c, RS_SEM["y"] + out), functools.partial(copy, out))

            def end():
                for number in (1, 3, 4, 5):
                    copy(number).wait_recv()
                finish(
                    step,
                    [
                        (low, add(step, low, [landing[1], landing[5]])),
                        (high, add(step, high, [landing[3], landing[4]])),
                    ],
                )

            return [begin, relay, end]

        def region(step, index, columns_at=None):
            at = lines(starts[step] + index * blocks[step + 1], blocks[step + 1])
            return total.at[at] if columns_at is None else total.at[at, columns_at]

        def pair_gather(step):
            axis = order[step]

            def copy(index):
                return remote(region(step, index), region(step, index), AG_SEM[axis], axis, 1)

            return [
                lambda: send((c, AG_SEM[axis] % 8), lambda: copy(place[axis])),
                lambda: copy(1 - place[axis]).wait_recv(),
            ]

        def direct_gather(step):
            def copy(k, back):
                part = region(step, lax.rem(place["y"] + 4 - back, 4))
                return remote(part, part, AG_SEM["y"] + k - 1, "y", k)

            def begin():
                for k in (2, 1, 3):
                    send((c, (AG_SEM["y"] + k - 1) % 8), functools.partial(copy, k, 0))

            def end():
                for k in range(1, 4):
                    copy(k, k).wait_recv()

            return [begin, end]

        def ring_gather(step):
            def copy(number, back):
                index = lax.rem(place["y"] + 4 - back, 4)
                columns_at = (None, None, low, high)[number]
                part = region(step, index, columns_at)
                return remote(part, part, AG_SEM["y"] + number, "y", (1, 3, 1, 3)[number])

            def begin():
                send((c, (AG_SEM["y"] + 0) % 8), functools.partial(copy, 0, 0))
                send((c, (AG_SEM["y"] + 1) % 8), functools.partial(copy, 1, 0))

            def relay():
                copy(0, 1).wait_recv()
                send((c, (AG_SEM["y"] + 2) % 8), functools.partial(copy, 2, 1))
                copy(1, 3).wait_recv()
                send((c, (AG_SEM["y"] + 3) % 8), functools.partial(copy, 3, 3))

            def end():
                copy(2, 2).wait_recv()
                copy(3, 2).wait_recv()

            return [begin, relay, end]

        def join(stages):
            events = [stages[0][0]]
            for stage, later in zip(stages, stages[1:] + [None]):
                events.extend(stage[1:-1])
                if later is None:
                    events.append(stage[-1])
                else:
                    events.append(lambda end=stage[-1], begin=later[0]: (end(), begin()))
            return events

        forms = {
            "core": (pair_scatter, pair_gather),
            "x": (pair_scatter, pair_gather),
            "y": (direct_scatter, direct_gather),
            "ring": (ring_scatter, ring_gather),
        }
        scatters = [forms[axis][0](step) for step, axis in enumerate(order)]
        gathers = [forms[axis][1](step) for step, axis in enumerate(order)]
        return join(scatters + gathers[::-1])

    sends, events = ({}, {}), ([], [])
    for section in range(2):

        def send(slot_of, make, section=section):
            earlier = sends[section].pop(slot_of, None)
            if earlier is not None:
                earlier().wait_send()
            make().start()
            sends[section][slot_of] = make

        events[section].extend(sum_events(c, send) for c in range(len(plan)))

    def advance(section, *which):
        @pl.when(sec == section)
        def _():
            for c in which:
                if events[section][c]:
                    events[section][c].pop(0)()

    def spread_copy(step, k, source):
        axis = SPREAD[step]
        size = tensor_size if axis == "tensor" else AXES[axis][1]
        at = spread_refs[step].at[source]
        return pltpu.make_async_remote_copy(
            src_ref=at,
            dst_ref=at,
            send_sem=small_ssem.at[step, k - 1],
            recv_sem=small_rsem.at[step, k - 1],
            device_id={"tensor": lax.rem(me + k, size)} if axis == "tensor" else dp_peer(axis, k),
            device_id_type=MESH,
        )

    def spread_place(step):
        axis = SPREAD[step]
        return (me, tensor_size) if axis == "tensor" else (place[axis], AXES[axis][1])

    def spread_start(step, value):
        index, size = spread_place(step)
        spread_refs[step][index] = value
        for k in range(1, size):
            spread_copy(step, k, index).start()

    def spread_finish(step):
        index, size = spread_place(step)
        for k in range(1, size):
            spread_copy(step, k, lax.rem(index + size - k, size)).wait_recv()
        value = spread_refs[step][0]
        for other_index in range(1, size):
            value = value + spread_refs[step][other_index]
        return value

    small_acc[...] = jnp.zeros_like(small_acc)

    @pl.when(sec == 0)
    def _():
        for m in range(batches):
            gath[0, m, mine, :] = x_ref[m]

    loads[1].wait()

    @pl.when(sec == 1)
    def _():
        share_start(*wide)

    for m in range(batches):
        @pl.when(sec == 1)
        def _():
            up_copy(m).wait_recv()

        gather_start(0, m)
        if m < batches - 1:
            for k in range(1, tensor_size):
                gather_copy(0, m, k).wait_send()

    loads[0].wait()

    @pl.when(sec == 1)
    def _():
        share_wait(*wide)


    def attention(m):
        entry[m] = gath[0, m, mine, :].astype(F32)
        gather_wait(0, m)
        for third in range(3):
            part = dot(gath[0, m], wqkv_ref[third])
            if third != 1:
                part = part + bqv_ref[0, third // 2 : third // 2 + 1, :]
            qkv[m, :, pl.ds(third * local, local)] = part.astype(BF16)
        across = jnp.broadcast_to(doc_ref[pl.ds(m, 1), :].astype(F32), (slot, slot))
        down = jnp.transpose(across)
        row_id = lax.broadcasted_iota(jnp.int32, (slot, slot), 0)
        col_id = lax.broadcasted_iota(jnp.int32, (slot, slot), 1)
        allowed = ((across == down) & (across >= 0)) | (row_id == col_id)
        low_half = head_mask()
        def third_of(third, pair):
            return qkv[m, :, pl.ds(third * local + pair * 2 * HEAD_DIM, 2 * HEAD_DIM)]

        heads = range(2 * pairs)
        raws = [
            dot_last(pick(head % 2 == 0, third_of(0, head // 2)), third_of(1, head // 2))
            for head in heads
        ]
        scores = [jnp.where(allowed, raw * scale, -1e30) for raw in raws]
        peaks = [jnp.max(score, axis=-1, keepdims=True) for score in scores]
        exps = [jnp.exp(score - peak) for score, peak in zip(scores, peaks)]
        sums = [jnp.sum(exp, axis=-1, keepdims=True) for exp in exps]
        softs = [exp / row_sum for exp, row_sum in zip(exps, sums)]
        halves = [dot(softs[head].astype(BF16), third_of(2, head // 2)) for head in heads]
        for head in heads:
            probs[m, head] = softs[head]
        for pair in range(pairs):
            both = jnp.where(low_half, halves[2 * pair], halves[2 * pair + 1])
            ctx[m, :, pl.ds(pair * 2 * HEAD_DIM, 2 * HEAD_DIM)] = both.astype(BF16)

        @pl.when(sec == 0)
        def _():
            for cols in chunks(width):
                put_part(0, m, cols, dot(ctx[m], wfull[me, :, cols]))
            scatter_start(0, m)

        @pl.when(sec == 1)
        def _():
            ctx_all[m, me] = ctx[m]
            share_start(*contexts(m))

    each_batch(attention)

    def first_norm(m):
        @pl.when(sec == 0)
        def _():
            hidden = entry[m] + scatter_wait(0, m) + bout_ref[...]
            out, normed, inv_std = norm(hidden, gain1_ref[...], shift1_ref[...])
            y1[m], n1[m], r1[m] = out, normed, inv_std
            gath[1, m, mine, :] = out.astype(BF16)
            gather_start(1, m)

    each_batch(first_norm)

    def whole_norm(m):
        share_wait(*contexts(m))
        for cols in chunks(width):
            part = gath[0, m, :, cols].astype(F32) + bout_ref[:, cols]
            for source in range(tensor_size):
                part = part + dot(ctx_all[m, source], wfull[source, :, cols])
            rs_own[m, :, cols] = part
        for at in range(0, slot, rows):
            lines_at = pl.ds(at, rows)
            out, _, _ = norm(rs_own[m, lines_at, :], gain1_ref[...], shift1_ref[...])
            gath[1, m, lines_at, :] = out.astype(BF16)
        out, normed, inv_std = norm(rs_own[m, mine, :], gain1_ref[...], shift1_ref[...])
        y1[m], n1[m], r1[m] = out, normed, inv_std

    for load in loads[2:]:
        load.wait()

    def feed_forward(m):
        @pl.when(sec == 0)
        def _():
            gather_wait(1, m)

        @pl.when(sec == 1)
        def _():
            whole_norm(m)

        for cols in chunks(units):
            pre = dot(gath[1, m], wup_ref[:, cols]) + bup_ref[:, cols]
            cdf = 0.5 * (1.0 + lax.erf(pre * (1.0 / math.sqrt(2.0))))
            slope[m, :, cols] = cdf + pre * jnp.exp(-0.5 * pre * pre) * (
                1.0 / math.sqrt(2.0 * math.pi)
            )
            act[m, :, cols] = (pre * cdf).astype(BF16)
        for cols in chunks(width):
            put_part(1, m, cols, dot(act[m], wdown_ref[:, cols]))
        scatter_start(1, m)

    each_batch(feed_forward)

    def back_entry(m):
        @pl.when(sec == 1)
        def _():
            back_in[m] = cot_ref[m]

        @pl.when(sec == 0)
        def _():
            back_copy(m).wait_recv()

        grad_out = back_in[m].astype(F32)
        grad = norm_back(grad_out, n2[m], r2[m], gain2_ref[...])
        small_acc[0:1, :] += column_sum(grad)
        small_acc[1:2, :] += column_sum(grad_out * n2[m])
        small_acc[2:3, :] += column_sum(grad_out)
        dh2[m] = grad
        gath[2, m, mine, :] = grad.astype(BF16)
        gather_start(2, m)

    def second_norm(m):
        hidden = y1[m] + scatter_wait(1, m) + bdown_ref[...]
        out, normed, inv_std = norm(hidden, gain2_ref[...], shift2_ref[...])
        n2[m], r2[m] = normed, inv_std
        rounded = out.astype(BF16)
        out_ref[m] = rounded

        @pl.when(sec == 0)
        def _():
            sent_up[m] = rounded
            up_copy(m).start()

        @pl.when(sec == 1)
        def _():
            back_entry(m)

    each_batch(second_norm)

    @pl.when(sec == 0)
    def _():
        for k in range(1, tensor_size):
            target = {"tensor": lax.rem(me + k, tensor_size)}
            pl.semaphore_signal(calm_sem, inc=1, device_id=target, device_id_type=MESH)
        pl.semaphore_wait(calm_sem, tensor_size - 1)
        share_start(*wide)

    @pl.when(sec == 0)
    def _():
        each_batch(back_entry)

    def weight_grad(left, right, target, base=0):
        total = batches * slot
        rhs = right[...].reshape(total, right.shape[-1])
        for rows_at in chunks(left.shape[-1]):
            lhs = left[:, :, rows_at].reshape(total, rows_at.size)
            target[pl.ds(base + rows_at.start, rows_at.size), :] = dot_rows(lhs, rhs).astype(BF16)

    def down_grad():
        weight_grad(act, gath.at[2], pdown)

    def up_grad():
        weight_grad(gath.at[1], du, pup)

    def feed_back(m):
        @pl.when(sec == 1)
        def _():
            gather_wait(2, m)

        for cols in chunks(units):
            grad = (dot_last(gath[2, m], wdown_ref[cols, :]) * slope[m, :, cols]).astype(BF16)
            du[m, :, cols] = grad
            small_acc[6:7, cols] += column_sum(grad.astype(F32))
        for cols in chunks(width):
            put_part(2, m, cols, dot_last(du[m], wup_ref[cols, :]))
        scatter_start(2, m)

    @pl.when(sec == 0)
    def _():
        gather_wait(2, 0)

    feed_back(0)

    @pl.when(sec == 0)
    def _():
        for m in range(1, batches):
            gather_wait(2, m)

    for m in range(1, batches):
        feed_back(m)
    pl.when(sec == 0)(down_grad)
    advance(0, 0, 1)
    pl.when(sec == 0)(up_grad)
    advance(0, 2, 3)

    @pl.when(sec == 0)
    def _():
        share_wait(*wide)

    def first_back(m):
        grad_out = dh2[m] + scatter_wait(2, m)
        grad = norm_back(grad_out, n1[m], r1[m], gain1_ref[...])
        small_acc[3:4, :] += column_sum(grad)
        small_acc[4:5, :] += column_sum(grad_out * n1[m])
        small_acc[5:6, :] += column_sum(grad_out)
        dh[m] = grad
        rounded = grad.astype(BF16)
        gath[3, m, mine, :] = rounded
        for target in range(tensor_size):
            dctx_sent[m, target] = dot_last(rounded, wfull[target]).astype(BF16)
        dctx_all[m, mine, :] = dctx_sent[m, me]
        for k in (2, 1, 3):
            dctx_copy(m, k).start()
        gather_start(3, m)

    each_batch(first_back, lambda m: advance(0, *AFTER_FIRST[m]))

    def attention_back(m):
        dctx_wait(m)
        low_half = head_mask()
        heads = range(2 * pairs)

        def third_of(third, pair):
            return qkv[m, :, pl.ds(third * local + pair * 2 * HEAD_DIM, 2 * HEAD_DIM)]

        dctx = [dctx_all[m, :, pl.ds(pair * 2 * HEAD_DIM, 2 * HEAD_DIM)] for pair in range(pairs)]
        dprobs = [
            dot_last(pick(head % 2 == 0, dctx[head // 2]), third_of(2, head // 2)) for head in heads
        ]
        softs = [probs[m, head] for head in heads]
        means = [
            jnp.sum(soft * dprob, axis=-1, keepdims=True) for soft, dprob in zip(softs, dprobs)
        ]
        dscores = [
            (soft * (dprob - mean)).astype(BF16)
            for soft, dprob, mean in zip(softs, dprobs, means)
        ]
        dq = [dot(dscores[head], third_of(1, head // 2)) * scale for head in heads]
        dk = [dot_rows(dscores[head], third_of(0, head // 2)) * scale for head in heads]
        dv = [dot_rows(softs[head].astype(BF16), dctx[head // 2]) for head in heads]
        for place_of, parts in enumerate((dq, dk, dv)):
            for pair in range(pairs):
                at = pair * 2 * HEAD_DIM
                grad = jnp.where(low_half, parts[2 * pair], parts[2 * pair + 1]).astype(BF16)
                dqkv[m, :, pl.ds(place_of * local + at, 2 * HEAD_DIM)] = grad
                if place_of != 1:
                    to = at if place_of == 0 else local + at
                    small_acc[7:8, pl.ds(to, 2 * HEAD_DIM)] += column_sum(grad.astype(F32))
        for cols in chunks(width):
            part = dot_last(dqkv[m, :, pl.ds(0, local)], wqkv_ref[0, cols, :])
            for third in range(1, 3):
                part = part + dot_last(
                    dqkv[m, :, pl.ds(third * local, local)], wqkv_ref[third, cols, :]
                )
            put_part(3, m, cols, part)
        scatter_start(3, m)

    each_batch(attention_back, lambda m: advance(0, *AFTER_ATTENTION[m]))

    def joined_grad():
        for third in range(3):
            weight_grad(
                gath.at[0], dqkv.at[:, :, pl.ds(third * local, local)], pqkv, base=third * width
            )

    pl.when(sec == 0)(joined_grad)
    advance(0, 5, 6)
    spread_start(0, small_acc[...])
    for m in range(batches):
        gather_wait(3, m)

    def out_grad():
        weight_grad(ctx, gath.at[3], pout)

    pl.when(sec == 0)(out_grad)
    advance(0, 4, *AFTER_GRADS)

    def last_back(m):
        grad = dh[m] + scatter_wait(3, m)
        dx_ref[m] = grad

        @pl.when(sec == 1)
        def _():
            sent_back[m] = grad.astype(BF16)
            back_copy(m).start()

    each_batch(last_back, lambda m: advance(0, *AFTER_LAST[m]))

    @pl.when(sec == 1)
    def _():
        down_grad()
        up_grad()
        out_grad()
        joined_grad()

    advance(1, 0, 1, 2, 3, 4, 5, 6)
    small_row = lax.broadcasted_iota(jnp.int32, small_acc.shape, 0)
    spread_start(1, jnp.where(small_row < 6, spread_finish(0), small_acc[...]))
    small_step = 1
    for part in range(ROUNDS):
        at = len(TAIL) // ROUNDS
        advance(0, *TAIL[part * at : (part + 1) * at if part < ROUNDS - 1 else len(TAIL)])
        advance(1, *TAIL_ONE[part * 14 : part * 14 + 14])
        if small_step < len(SPREAD):
            value = spread_finish(small_step)
            small_step += 1
            if small_step < len(SPREAD):
                spread_start(small_step, value)
            else:
                small_ref[...] = value
    assert not any(events[0]) and not any(events[1])

    for make in sends[0].values():
        make().wait_send()
    for step in range(len(SPREAD)):
        index, size = spread_place(step)
        for k in range(1, size):
            spread_copy(step, k, index).wait_send()

    def drain(m):
        for e in range(4):
            for k in range(1, tensor_size):
                if e:
                    scatter_copy(e, m, k).wait_send()
                if e > 1:
                    gather_copy(e, m, k).wait_send()
        for k in range(1, tensor_size):
            dctx_copy(m, k).wait_send()

        @pl.when(sec == 0)
        def _():
            up_copy(m).wait_send()
            for k in range(1, tensor_size):
                scatter_copy(0, m, k).wait_send()
                gather_copy(1, m, k).wait_send()

        @pl.when(sec == 1)
        def _():
            back_copy(m).wait_send()
            share_drain(*contexts(m))

    for k in range(1, tensor_size):
        gather_copy(0, batches - 1, k).wait_send()
    share_drain(*wide)
    each_batch(drain)


def run_layer(x, docs, cot, weights, tensor_size):
    batches, rows, width = x.shape
    slot = rows * tensor_size
    wqkv, bqv, wout, bout, gain1, shift1, wup, bup, wdown, bdown, gain2, shift2 = weights
    local = wout.shape[0]
    units = wup.shape[1]
    heads = local // HEAD_DIM
    vmem = pl.BlockSpec(memory_space=pltpu.VMEM)
    others = tensor_size - 1
    dma = pltpu.SemaphoreType.DMA
    operands = (x, docs, cot) + weights
    small_shape = (8, width)
    shard = (batches, rows, width)
    shapes = (
        pltpu.VMEM(shard, BF16),
        pltpu.VMEM(shard, F32),
        pltpu.VMEM((3 * width, local), BF16),
        pltpu.VMEM(wout.shape, BF16),
        pltpu.VMEM(wup.shape, BF16),
        pltpu.VMEM(wdown.shape, BF16),
        pltpu.VMEM(small_shape, F32),
    )
    plan = sum_plan(width, local, units)
    scratch = [
        pltpu.VMEM(wqkv.shape, BF16),
        pltpu.VMEM((tensor_size,) + wout.shape, BF16),
        pltpu.VMEM(wup.shape, BF16),
        pltpu.VMEM(wdown.shape, BF16),
        pltpu.VMEM((4, batches, slot, width), BF16),
        pltpu.VMEM((4, batches, slot, width), BF16),
        pltpu.VMEM((4, batches, others, rows, width), BF16),
        pltpu.VMEM((batches, slot, width), F32),
        pltpu.VMEM((batches, slot, 3 * local), BF16),
        pltpu.VMEM((batches, heads, slot, slot), F32),
        pltpu.VMEM((batches, slot, local), BF16),
        pltpu.VMEM(shard, F32),
        pltpu.VMEM(shard, F32),
        pltpu.VMEM(shard, F32),
        pltpu.VMEM((batches, rows, 1), F32),
        pltpu.VMEM((batches, slot, units), F32),
        pltpu.VMEM((batches, slot, units), BF16),
        pltpu.VMEM(shard, F32),
        pltpu.VMEM((batches, rows, 1), F32),
        pltpu.VMEM(shard, F32),
        pltpu.VMEM(shard, F32),
        pltpu.VMEM((batches, slot, units), BF16),
        pltpu.VMEM((batches, slot, 3 * local), BF16),
        pltpu.VMEM(shard, BF16),
        pltpu.VMEM(shard, BF16),
        pltpu.VMEM(shard, BF16),
        pltpu.VMEM(small_shape, F32),
        pltpu.VMEM((batches, tensor_size, slot, local), BF16),
        pltpu.VMEM((batches, tensor_size, rows, local), BF16),
        pltpu.VMEM((batches, slot, local), BF16),
        pltpu.VMEM((3 * width, local), BF16),
        pltpu.VMEM(wout.shape, BF16),
        pltpu.VMEM(wup.shape, BF16),
        pltpu.VMEM(wdown.shape, BF16),
        dma((4, batches, others)),
        dma((4, batches, others)),
        dma((4, batches, others)),
        dma((4, batches, others)),
        dma((batches,)),
        dma((batches,)),
        dma((batches,)),
        dma((batches,)),
        dma((others,)),
        dma((others,)),
        dma((batches, others)),
        dma((batches, others)),
        dma((batches, others)),
        dma((batches, others)),
        dma((len(plan), 8)),
        dma((len(plan), 14)),
        dma((len(SPREAD), 3)),
        dma((len(SPREAD), 3)),
        dma((4,)),
        pltpu.SemaphoreType.REGULAR,
    ]
    for axis in SPREAD:
        size = tensor_size if axis == "tensor" else AXES[axis][1]
        scratch.append(pltpu.VMEM((size,) + small_shape, F32))
    for _, _, rows_all, columns, order in plan:
        scratch.extend(pltpu.VMEM(shape, BF16) for shape in sum_buffers(rows_all, columns, order))
    in_specs = [vmem] * len(operands)
    for index in (3, 5, 9, 11):
        in_specs[index] = pl.BlockSpec(memory_space=pl.ANY)
    return pl.pallas_call(
        functools.partial(layer_kernel, tensor_size, plan),
        out_shape=shapes,
        in_specs=in_specs,
        out_specs=[vmem] * len(shapes),
        scratch_shapes=scratch,
        compiler_params=pltpu.CompilerParams(
            collective_id=0, has_side_effects=True, vmem_limit_bytes=VMEM_BYTES
        ),
        name="layer",
    )(*operands)


def unpack_kernel(count, *refs):
    sums, rows_ref, grad_ref, small_ref = refs[:count], *refs[count : count + 3]
    refs = refs[count + 3 :]
    targets, rows_out, grad_out, bqv_out, vectors = (
        refs[:count], refs[count], refs[count + 1], refs[count + 2], refs[count + 3 : count + 10]
    )
    wides, lone, biases, sem = refs[count + 10 : 2 * count + 10], *refs[2 * count + 10 :]
    copies = []

    def write(source, target):
        copy = pltpu.make_async_copy(source, target, sem.at[len(copies)])
        copy.start()
        copies.append(copy)

    for source, target, wide in zip(sums, targets, wides):
        for at in range(0, source.shape[0], PIECE):
            rows_at = pl.ds(at, PIECE)
            wide[rows_at, :] = source[rows_at, :].astype(F32)
            write(wide.at[rows_at], target.at[rows_at])
    write(rows_ref, rows_out)
    write(grad_ref, grad_out)
    half = bqv_out.shape[-1]
    for index in range(2):
        biases[0, index : index + 1, :] = small_ref[7:8, pl.ds(index * half, half)]
    write(biases, bqv_out)
    for index, vector in enumerate(vectors):
        lone[index] = small_ref[index : index + 1, :]
        write(lone.at[index], vector)
    for copy in copies:
        copy.wait()


def unpack(sums, rows, grad, small, local):
    vmem = pl.BlockSpec(memory_space=pltpu.VMEM)
    count = len(sums)
    vector = jax.ShapeDtypeStruct((1, small.shape[1]), F32)
    shapes = [jax.ShapeDtypeStruct(part.shape, F32) for part in sums] + [
        jax.ShapeDtypeStruct(rows.shape, rows.dtype),
        jax.ShapeDtypeStruct(grad.shape, grad.dtype),
        jax.ShapeDtypeStruct((1, 2, local), F32),
    ] + [vector] * 7
    pieces = sum(part.shape[0] // PIECE for part in sums) + 10
    return pl.pallas_call(
        functools.partial(unpack_kernel, count),
        out_shape=shapes,
        in_specs=[vmem] * (count + 3),
        out_specs=[pl.BlockSpec(memory_space=pl.ANY)] * (count + 10),
        scratch_shapes=[pltpu.VMEM(part.shape, F32) for part in sums]
        + [
            pltpu.VMEM((7, 1, small.shape[1]), F32),
            pltpu.VMEM((1, 2, local), F32),
            pltpu.SemaphoreType.DMA((pieces,)),
        ],
        compiler_params=pltpu.CompilerParams(vmem_limit_bytes=UNPACK_BYTES),
        name="unpack",
    )(*sums, rows, grad, small)


def shards(
    inputs, doc_ids, cotangent, w_qkv, b_qv, w_out, b_out, gain1, shift1,
    w_up, b_up, w_down, b_down, gain2, shift2,
):
    tensor_size = lax.axis_size("tensor")
    width = inputs.shape[2]
    local = w_out.shape[1]
    weights = (
        jnp.transpose(w_qkv[0], (1, 0, 2)), b_qv, w_out[0], b_out, gain1, shift1,
        w_up[0], b_up, w_down[0], b_down, gain2, shift2,
    )
    outputs, input_grads, gqkv, gout, gup, gdown, small = run_layer(
        inputs, doc_ids, cotangent, weights, tensor_size
    )
    sums = (gqkv, gout, gup, gdown)
    gqkv, gout, gup, gdown, outputs, input_grads, gbqv, *vectors = unpack(
        sums, outputs, input_grads, small, local
    )
    return (
        outputs[None],
        input_grads[None],
        jnp.transpose(gqkv.reshape(3, width, local), (1, 0, 2))[None],
        gbqv,
        gout[None],
        vectors[3],
        vectors[4],
        vectors[5],
        gup[None],
        vectors[6],
        gdown[None],
        vectors[0],
        vectors[1],
        vectors[2],
    )


def solution(mesh):
    rows = P(None, ("dp", "tensor"), None)
    banked = P("section", None, ("dp", "tensor"), None)
    vector = P("section", None)
    return jax.shard_map(
        shards,
        mesh=mesh,
        in_specs=(
            rows,
            P(None, "dp"),
            rows,
            P("section", None, None, "tensor"),
            P("section", None, "tensor"),
            P("section", "tensor", None),
            vector,
            vector,
            vector,
            P("section", None, "tensor"),
            P("section", "tensor"),
            P("section", "tensor", None),
            vector,
            vector,
            vector,
        ),
        out_specs=(
            banked,
            banked,
            P("section", None, None, "tensor"),
            P("section", None, "tensor"),
            P("section", "tensor", None),
            vector,
            vector,
            vector,
            P("section", None, "tensor"),
            P("section", "tensor"),
            P("section", "tensor", None),
            vector,
            vector,
            vector,
        ),
        check_vma=False,
    )
```
